32 devices in a mesh: slab: 8 (over z, x), ctrl: 4 (over y, core).
Axes of the slice: x: 2, y: 2, z: 4, core: 2. Of those that a mesh axis runs over, the one named last changes fastest.
Arguments:
- face_pressure: float32 [131072], P(('slab', 'ctrl')), may hold values from 0 to 18
- face_area: float32 [3, 131072], P(None, ('slab', 'ctrl')), may hold values from -0.015625 to 0.015625
- face_center: float32 [3, 131072], P(None, ('slab', 'ctrl')), may hold values from -6 to 6
- motion: float32 [6], replicated, may hold values from -1 to 1
- inverse_mass: float32 [6], replicated, may hold values from 0.5 to 2
- control_points: float32 [3, 8192], P(None, ('slab', 'ctrl')), may hold values from -4 to 4
- control_modes: float32 [18, 8192], P(None, ('slab', 'ctrl')), may hold values from -0.25 to 0.25
- node_points: float32 [3, 64, 32, 128], P(None, 'slab', 'ctrl'), may hold values from -5 to 5
- tile_list: int32 [64, 32, 16], P('slab', 'ctrl'), may hold values from 0 to 63, as said below
- tile_count: int32 [64, 32], P('slab', 'ctrl'), may hold values from 0 to 16, as said below
Outputs:
- node_shift: float32 [3, 64, 32, 128], P(None, 'slab', 'ctrl')
- cell_volume: float32 [64, 32, 128], P('slab', 'ctrl')
- volume_change: float32 [64, 32, 128], P('slab', 'ctrl')
- new_state: float32 [6], replicated
The draws below stay inside these ranges and needn't reach their ends.
Inputs may be any that keep to these rules, and one draw needn't show every extreme that they name: `tile_list`: the entries of one line are distinct tile numbers; only the first tile_count entries of a line are live, the others are to be ignored. `tile_count`: every line in the planes x with 192 <= 8 x < 320 has 16 live entries; every other line has at most 4.
All inputs are finite; a program needn't handle non-finite values.
Results may differ from the reference program's by a relative error of at most 0.0003.
Values sent between devices are 32-bit elements; how exact they have to be, the bound alone decides.
No kernel may reach another device: no remote copies, remote signals or barrier semaphores. Data moves between devices by JAX's collectives and lax.ppermute only.
A program may use at most 64 MiB of HBM per device.

```python
import math
import jax
import jax.numpy as jnp
from jax import lax

NZ = 128
NCTRL = 8192
TILE = 128
KMAX = 16
NTILE = 64
FACES = 131072
NX = 64
NY = 32


def draw_face_pressure(key, part):
    position = jnp.arange(FACES, dtype=jnp.float32)
    ramp_up = 1.0 + 2.0 * position / FACES
    base_level = jnp.clip(1.0 + 0.25 * jax.random.normal(key, (FACES,), jnp.float32), 0.25, 1.75)
    return ramp_up * base_level


def tile_draws(key):
    score_key = jax.random.fold_in(key, 101)
    light_key = jax.random.fold_in(key, 202)
    scores = jax.random.randint(score_key, (NX, NY, NTILE), 0, 1 << 20, dtype=jnp.int32) * NTILE
    scores = scores + jnp.arange(NTILE, dtype=jnp.int32)
    ranking = jnp.argsort(scores, axis=-1, stable=True)
    tile_ids = ranking[:, :, :KMAX].astype(jnp.int32)
    planes = jnp.arange(NX, dtype=jnp.int32)
    heavy_rows = (8 * planes >= 3 * NX) & (8 * planes < 5 * NX)
    light_count = jax.random.randint(light_key, (NX, NY), 0, KMAX // 4 + 1, dtype=jnp.int32)
    counts = jnp.where(heavy_rows[:, None], KMAX, light_count).astype(jnp.int32)
    return (tile_ids, counts)


def draw_tile_list(key, part):
    return tile_draws(key)[0]


def draw_tile_count(key, part):
    return tile_draws(key)[1]


def steps_of(rng, dims, cuts, low, high):
    def one(dim, parts):
        heights = jax.random.uniform(jax.random.fold_in(jax.random.fold_in(rng, 6), dim), (parts,), jnp.float32, low / len(cuts), high / len(cuts))
        return jnp.repeat(jnp.exp(heights), dims[dim] // parts).reshape((-1,) + (1,) * (len(dims) - dim - 1))

    level = one(*cuts[0])
    for cut in cuts[1:]:
        level = level * one(*cut)
    return level


def centred(key, extent, spread, limit, cuts=(), kind=jnp.bfloat16):
    values = spread * jax.random.normal(key, extent, jnp.float32)
    if cuts:
        values = values * steps_of(key, extent, cuts, -0.22, 0.18)
    return jnp.clip(values, -limit, limit).astype(kind)


def setup_inputs(seed: int = 0) -> dict:
    streams_of = jax.random.split(jax.random.key(seed), 11)
    face_pressure = draw_face_pressure(jax.random.fold_in(streams_of[10], 71), 0)
    face_area = centred(streams_of[1], (3, FACES), FACES ** -0.5, 0.015625, ((1, 32),), jnp.float32)
    face_center = centred(streams_of[2], (3, FACES), 1.0, 6.0, ((1, 32),), jnp.float32)
    motion = jnp.clip(jax.random.uniform(streams_of[3], (6,), jnp.float32, -1.0, 1.0), -1.0, 1.0)
    inverse_mass = jnp.clip(jnp.exp(jax.random.uniform(streams_of[4], (6,), jnp.float32, math.log(0.5), math.log(2.0))), 0.5, 2.0)
    control_points = centred(streams_of[5], (3, NCTRL), 0.7, 4.0, ((1, 32),), jnp.float32)
    control_modes = centred(streams_of[6], (18, NCTRL), (4 * TILE) ** -0.5, 0.25, ((1, 32),), jnp.float32)
    node_points = centred(streams_of[7], (3, NX, NY, NZ), 1.0, 5.0, ((1, 8), (2, 4)), jnp.float32)
    tile_list = draw_tile_list(jax.random.fold_in(streams_of[10], 71), 0)
    tile_count = draw_tile_count(jax.random.fold_in(streams_of[10], 71), 0)
    return dict(face_pressure=face_pressure, face_area=face_area, face_center=face_center, motion=motion, inverse_mass=inverse_mass, control_points=control_points, control_modes=control_modes, node_points=node_points, tile_list=tile_list, tile_count=tile_count)


TIME_STEP = 0.5
RADIUS = 4.0
GRAVITY = (0.0, 0.0, -0.5, 0.0, 0.0, 0.0)

def surface_loads(pressure, area, center):
    pushed = pressure[None, :] * area
    forces = lax.optimization_barrier(jnp.sum(pushed, axis=1))
    moment_x = jnp.sum(center[1] * pushed[2] - center[2] * pushed[1])
    moment_y = jnp.sum(center[2] * pushed[0] - center[0] * pushed[2])
    moment_z = jnp.sum(center[0] * pushed[1] - center[1] * pushed[0])
    return jnp.concatenate([forces, jnp.stack([moment_x, moment_y, moment_z])])

def advance(total_loads, motion, inverse_mass):
    acceleration = inverse_mass * total_loads + jnp.array(GRAVITY, dtype=jnp.float32)
    new_state = motion + TIME_STEP * acceleration
    rigid_step = TIME_STEP * motion + 0.5 * TIME_STEP * TIME_STEP * acceleration
    return (new_state, rigid_step)

def mode_mix(rigid_step, modes):
    shaped = modes.reshape(6, 3, modes.shape[1])
    return jnp.einsum('k,kcj->cj', rigid_step, shaped, precision=lax.Precision.HIGHEST)

def kernel_sum(points, tile_ids, counts, center_tiles, coeff_tiles):
    longest = jnp.max(counts)

    def accumulate(entry_id, running):
        picked = jnp.take(tile_ids, entry_id, axis=1)
        centers = jnp.take(center_tiles, picked, axis=1)
        coeffs = jnp.take(coeff_tiles, picked, axis=1)
        square = jnp.zeros((points.shape[1], points.shape[2], centers.shape[2]), jnp.float32)
        for axis_id in range(3):
            offset = points[axis_id][:, :, None] - centers[axis_id][:, None, :]
            square = square + offset * offset
        radial = jnp.sqrt(square) / RADIUS
        falloff = jnp.maximum(1.0 - radial, 0.0)
        fourth = falloff * falloff
        fourth = fourth * fourth
        kernel = fourth * (4.0 * radial + 1.0)
        alive_mask = (entry_id < counts)[:, None, None]
        kernel = jnp.where(alive_mask, kernel, 0.0)
        return running + jnp.einsum('lnj,clj->cln', kernel, coeffs, precision=lax.Precision.HIGHEST)
    start = jnp.zeros((3, points.shape[1], points.shape[2]), jnp.float32)
    return lax.fori_loop(0, longest, accumulate, start)

def cell_volumes(lattice):
    span_x = lattice.shape[-3] - 1
    span_y = lattice.shape[-2] - 1

    def corner(shift_x, shift_y, shift_z):
        sliced = lattice[..., shift_x:shift_x + span_x, shift_y:shift_y + span_y, :]
        if shift_z == 1:
            sliced = jnp.concatenate([sliced[..., 1:], jnp.zeros_like(sliced[..., :1])], axis=-1)
        return sliced
    corners = {}
    for shift_x in range(2):
        for shift_y in range(2):
            for shift_z in range(2):
                corners[shift_x, shift_y, shift_z] = corner(shift_x, shift_y, shift_z)
    edge_x = 0.0
    edge_y = 0.0
    edge_z = 0.0
    for first in range(2):
        for second in range(2):
            edge_x = edge_x + corners[1, first, second] - corners[0, first, second]
            edge_y = edge_y + corners[first, 1, second] - corners[first, 0, second]
            edge_z = edge_z + corners[first, second, 1] - corners[first, second, 0]
    edge_x = 0.25 * edge_x
    edge_y = 0.25 * edge_y
    edge_z = 0.25 * edge_z
    ex0, ex1, ex2 = (edge_x[..., 0, :, :, :], edge_x[..., 1, :, :, :], edge_x[..., 2, :, :, :])
    ey0, ey1, ey2 = (edge_y[..., 0, :, :, :], edge_y[..., 1, :, :, :], edge_y[..., 2, :, :, :])
    ez0, ez1, ez2 = (edge_z[..., 0, :, :, :], edge_z[..., 1, :, :, :], edge_z[..., 2, :, :, :])
    return ex0 * (ey1 * ez2 - ey2 * ez1) + ex1 * (ey2 * ez0 - ey0 * ez2) + ex2 * (ey0 * ez1 - ey1 * ez0)

def reference(face_pressure, face_area, face_center, motion, inverse_mass, control_points, control_modes, node_points, tile_list, tile_count):
    total_loads = surface_loads(face_pressure, face_area, face_center)
    new_state, rigid_step = advance(total_loads, motion, inverse_mass)
    coefficients = mode_mix(rigid_step, control_modes)
    center_tiles = control_points.reshape(3, NTILE, TILE)
    coeff_tiles = coefficients.reshape(3, NTILE, TILE)

    def one_plane(pieces):
        plane_points, plane_ids, plane_counts = pieces
        return kernel_sum(plane_points, plane_ids, plane_counts, center_tiles, coeff_tiles)
    shifted = lax.map(one_plane, (jnp.moveaxis(node_points, 1, 0), tile_list, tile_count))
    node_shift = jnp.moveaxis(shifted, 0, 1)
    displaced = node_points + node_shift
    stacked = jnp.stack([node_points, displaced])
    padded = jnp.pad(stacked, ((0, 0), (0, 0), (0, 1), (0, 1), (0, 0)))
    volumes = cell_volumes(padded)
    inside = (jnp.arange(NX, dtype=jnp.int32) < NX - 1)[:, None, None]
    inside = inside & (jnp.arange(NY, dtype=jnp.int32) < NY - 1)[None, :, None]
    inside = inside & (jnp.arange(NZ, dtype=jnp.int32) < NZ - 1)[None, None, :]
    volumes = jnp.where(inside[None], volumes, 0.0)
    return (node_shift, volumes[1], volumes[1] - volumes[0], new_state)
```

```python
import functools
import jax
import jax.numpy as jnp
from jax import lax
from jax.experimental import pallas as pl
from jax.experimental.pallas import tpu as pltpu
from jax.sharding import PartitionSpec as P

TILE = 128
TIME_STEP = 0.5
RADIUS = 4.0
GRAVITY = (0.0, 0.0, -0.5, 0.0, 0.0, 0.0)
ROWS = 24
FEATS = 32
UNROLL = 4
TINY = 1e-30
F32 = jnp.float32
BF16 = jnp.bfloat16


def vmem():
    return pl.BlockSpec(memory_space=pltpu.VMEM)


def smem():
    return pl.BlockSpec(memory_space=pltpu.SMEM)


def swapped(value, slab_bit, ctrl_bit):
    slabs, ctrls = lax.axis_size("slab"), lax.axis_size("ctrl")
    pairs = [
        (s * ctrls + c, (s ^ slab_bit) * ctrls + (c ^ ctrl_bit))
        for s in range(slabs)
        for c in range(ctrls)
    ]
    return lax.ppermute(value, ("slab", "ctrl"), pairs)


def shifted_back(value, axis):
    return lax.ppermute(value, axis, [(i, i - 1) for i in range(1, lax.axis_size(axis))])


def load_rows(pressure, area, center):
    pushed = pressure * area

    def turned(value, by):
        return jnp.concatenate([value[by:3], value[0:by]], axis=0)

    moment = turned(center, 1) * turned(pushed, 2) - turned(center, 2) * turned(pushed, 1)
    sums = [jnp.sum(pushed, axis=1, keepdims=True), jnp.sum(moment, axis=1, keepdims=True)]
    lane = lax.broadcasted_iota(jnp.int32, (1, 128), 1)
    row = jnp.zeros((1, 128), F32)
    for k in range(6):
        row = jnp.where(lane == k, sums[k // 3][k % 3 : k % 3 + 1, :], row)
    return row


def pack_kernel(pressure, area, center, points, modes, out):
    row = load_rows(pressure[...], area[...], center[...])
    for t in range(out.shape[0] // ROWS):
        span = slice(t * TILE, (t + 1) * TILE)
        base = t * ROWS
        for c in range(3):
            out[base + 8 * c : base + 8 * c + 1, :] = points[c : c + 1, span]
            for k in range(6):
                at = base + 8 * c + 1 + k
                out[at : at + 1, :] = modes[3 * k + c : 3 * k + c + 1, span]
            at = base + 8 * c + 7
            out[at : at + 1, :] = row if (t == 0 and c == 0) else jnp.zeros((1, 128), F32)


def loads_kernel(pressure, area, center, out):
    out[...] = load_rows(pressure[...], area[...], center[...])


def list_kernel(lines, slots, dummy, codes, counts, items, total):
    lead = 2 * UNROLL
    for e in range(lead):
        items[e] = dummy

    def one(line, at):
        for e in range(slots):
            items[at + e] = codes[line * slots + e]
        return at + counts[line]

    end = lax.fori_loop(0, lines, one, jnp.int32(lead))
    for e in range(4 * UNROLL):
        items[end + e] = dummy
    total[0] = end - lead


def split3(value):
    first = value.astype(BF16).astype(F32)
    rest = value - first
    second = rest.astype(BF16).astype(F32)
    return first, second, rest - second


def shift_kernel(
    own, lent, bits, items, total, table, points, extra, motion, inverse, gravity,
    out_own, out_extra, out_state, out_row, out_plane,
    tile_raw, line_raw, coef_raw, tile_feat, line_feat, coefs, acc, *stages,
):
    squares, phis = stages[:UNROLL], stages[UNROLL:]
    tiles = table.shape[0] // ROWS
    lines = own + lent

    loads = jnp.sum(table[pl.ds(7, tiles, stride=ROWS), :], axis=0, keepdims=True)
    acceleration = inverse[...] * loads + gravity[...]
    out_state[...] = motion[...] + TIME_STEP * acceleration
    step = TIME_STEP * motion[...] + 0.5 * TIME_STEP * TIME_STEP * acceleration

    one = jnp.ones((tiles, 128), F32)
    zero = jnp.zeros((tiles, 128), F32)
    norm = zero
    for c in range(3):
        place = table[pl.ds(8 * c, tiles, stride=ROWS), :] * (1.0 / RADIUS)
        norm = norm + place * place
        b1, b2, b3 = split3(-2.0 * place)
        for f, value in enumerate((b1, b1, b2, b2, b1, b3, b2, b3)):
            tile_raw[pl.ds(8 * c + f, tiles, stride=FEATS), :] = value
        coef = zero
        for k in range(6):
            coef = coef + step[:, k : k + 1] * table[pl.ds(8 * c + 1 + k, tiles, stride=ROWS), :]
        for f, value in enumerate(split3(4.0 * coef)):
            coef_raw[pl.ds(3 * f + c, tiles, stride=16), :] = value
    for f in range(9, 16):
        coef_raw[pl.ds(f, tiles, stride=16), :] = zero
    for f, value in enumerate(split3(norm) + (one, one, one, zero, zero)):
        tile_raw[pl.ds(24 + f, tiles, stride=FEATS), :] = value

    packed = coef_raw[...].astype(BF16)
    coefs[:, 0:128] = packed
    coefs[:, 128:256] = packed

    def turn(t, carry):
        block = tile_raw[pl.ds(pl.multiple_of(t * FEATS, FEATS), FEATS), :]
        tile_feat[pl.ds(pl.multiple_of(t * TILE, TILE), TILE), :] = block.T.astype(BF16)
        return carry

    lax.fori_loop(0, tiles, turn, 0, unroll=4)

    def features(ref, count, first):
        norm = jnp.zeros((count, 128), F32)
        for c in range(3):
            place = ref[c * count : (c + 1) * count, :] * (1.0 / RADIUS)
            norm = norm + place * place
            a1, a2, a3 = split3(place)
            for f, value in enumerate((a1, a2, a1, a2, a3, a1, a3, a2)):
                line_raw[pl.ds(first * FEATS + 8 * c + f, count, stride=FEATS), :] = value
        one = jnp.ones((count, 128), F32)
        zero = jnp.zeros((count, 128), F32)
        for f, value in enumerate((one, one, one) + split3(norm) + (zero, zero)):
            line_raw[pl.ds(first * FEATS + 24 + f, count, stride=FEATS), :] = value

    features(points, own, 0)
    if lent:
        features(extra, lent, own)
    line_raw[lines * FEATS :, :] = jnp.zeros((FEATS, 128), F32)
    line_feat[...] = line_raw[...].astype(BF16)
    acc[...] = jnp.zeros(acc.shape, F32)

    mask = (1 << bits) - 1

    def body(j, carry):
        base = j * UNROLL
        for u in range(UNROLL):
            code = items[base + u]
            line, tile = lax.shift_right_logical(code, bits), code & mask
            got = jnp.dot(
                coefs[pl.ds(pl.multiple_of(tile * 16, 16), 16), :],
                phis[u][...],
                preferred_element_type=F32,
            )
            at = pl.ds(pl.multiple_of(line * 16, 16), 16)
            acc[at, :] = acc[at, :] + got
        for u in range(UNROLL):
            square = jnp.maximum(squares[u][...], TINY)
            near = jnp.maximum(1.0 - square * lax.rsqrt(square), 0.0)
            fourth = near * near
            fourth = fourth * fourth
            phi = fourth * (1.25 - near)
            high = phi.astype(BF16)
            phis[u][0:128, :] = high
            phis[u][128:256, :] = (phi - high.astype(F32)).astype(BF16)
        for u in range(UNROLL):
            code = items[base + 2 * UNROLL + u]
            line, tile = lax.shift_right_logical(code, bits), code & mask
            squares[u][...] = jnp.dot(
                tile_feat[pl.ds(pl.multiple_of(tile * TILE, TILE), TILE), :],
                line_feat[pl.ds(pl.multiple_of(line * FEATS, FEATS), FEATS), :],
                preferred_element_type=F32,
            )
        return carry

    groups = lax.div(total[0] + (UNROLL - 1), jnp.int32(UNROLL))
    lax.fori_loop(0, groups + 2, body, 0)

    rows = out_row.shape[1] // 3
    wide = out_plane.shape[1] // 3
    for c in range(3):
        def sums(first, count):
            value = acc[pl.ds(first * 16 + c, count, stride=16), :]
            for f in (1, 2):
                value = value + acc[pl.ds(first * 16 + 3 * f + c, count, stride=16), :]
            return value

        value = sums(0, own)
        out_own[c * own : (c + 1) * own, :] = value
        if lent:
            out_extra[c * lent : (c + 1) * lent, :] = sums(own, lent)
        out_plane[0, c * wide : (c + 1) * wide, :] = points[c * own : c * own + wide, :]
        out_plane[1, c * wide : (c + 1) * wide, :] = (
            points[c * own : c * own + wide, :] + value[0:wide, :]
        )
        old_row = points[pl.ds(c * own, rows, stride=wide), :]
        out_row[0, c * rows : (c + 1) * rows, :] = old_row
        out_row[1, c * rows : (c + 1) * rows, :] = (
            old_row + out_own[pl.ds(c * own, rows, stride=wide), :]
        )


def volume_kernel(
    keep, has_lent, points, shift, back, row_halo, plane_halo,
    out_shift, out_volume, out_change,
):
    planes, rows, depth = points.shape[1:]
    slab, ctrl = lax.axis_index("slab"), lax.axis_index("ctrl")
    slabs, ctrls = lax.axis_size("slab"), lax.axis_size("ctrl")
    row_id = lax.broadcasted_iota(jnp.int32, (rows, depth), 0)
    lane = lax.broadcasted_iota(jnp.int32, (rows, depth), 1)
    inside = (lane < depth - 1) & (row_id + ctrl * rows < ctrls * rows - 1)
    if has_lent:
        from_helper = (row_id >= 1) & is_heavy(slab, slabs)
    last_row = row_id == rows - 1

    def next_row(value, edge):
        return jnp.where(last_row, edge, pltpu.roll(value, rows - 1, 0))

    def next_depth(value):
        return pltpu.roll(value, depth - 1, 1)

    def level(x):
        found = []
        for field in range(2):
            parts = []
            for c in range(3):
                if x == planes:
                    here = plane_halo[field, c, 0:rows, :]
                    edge = plane_halo[field, c, rows : rows + 1, :]
                else:
                    here = points[c, x]
                    if field == 1:
                        moved = shift[c, x]
                        if has_lent and x >= keep:
                            moved = jnp.where(from_helper, back[c, x - keep], moved)
                        out_shift[c, x] = moved
                        here = here + moved
                    edge = row_halo[field, c, x : x + 1, :]
                there = next_row(here, edge)
                parts.append((here + there, there - here))
            found.append(parts)
        return found

    before = level(0)
    for x in range(planes):
        after = level(x + 1)
        volumes = []
        for field in range(2):
            edges = []
            for c in range(3):
                both0, step0 = before[field][c]
                both1, step1 = after[field][c]
                along, across, total = both1 - both0, step0 + step1, both0 + both1
                edges.append(
                    (
                        0.25 * (along + next_depth(along)),
                        0.25 * (across + next_depth(across)),
                        0.25 * (next_depth(total) - total),
                    )
                )
            ex, ey, ez = zip(*edges)
            volumes.append(
                ex[0] * (ey[1] * ez[2] - ey[2] * ez[1])
                + ex[1] * (ey[2] * ez[0] - ey[0] * ez[2])
                + ex[2] * (ey[0] * ez[1] - ey[1] * ez[0])
            )
        live = inside & (slab * planes + x < slabs * planes - 1)
        out_volume[x] = jnp.where(live, volumes[1], 0.0)
        out_change[x] = jnp.where(live, volumes[1] - volumes[0], 0.0)
        before = after


def is_heavy(slab, slabs):
    return (8 * slab >= 3 * slabs) & (8 * slab < 5 * slabs)


def local(
    face_pressure,
    face_area,
    face_center,
    motion,
    inverse_mass,
    control_points,
    control_modes,
    node_points,
    tile_list,
    tile_count,
):
    slabs, ctrls = lax.axis_size("slab"), lax.axis_size("ctrl")
    slab, ctrl = lax.axis_index("slab"), lax.axis_index("ctrl")
    _, planes, rows, depth = node_points.shape
    slots = tile_list.shape[2]
    own = planes * rows
    columns = control_points.shape[1]
    tiles = columns * slabs * ctrls // TILE
    bits = max(1, (tiles - 1).bit_length())
    pressure = face_pressure.reshape(1, -1)

    lend = slabs % 8 == 0 and slabs & (slabs - 1) == 0 and planes % 2 == 0
    unit = slabs // 8
    keep = planes // 2
    lent = (planes - keep) * rows if lend else 0
    heavy = [s for s in range(slabs) if is_heavy(s, slabs)]

    if lend:
        listed = jnp.concatenate(
            [tile_list[keep:], tile_count[keep:, :, None]], axis=2
        ).astype(F32)
        listed = jnp.pad(listed, ((0, 0), (0, 0), (0, TILE - slots - 1)))
        sent = jnp.concatenate(
            [node_points[:, keep:].reshape(-1, depth), listed.reshape(-1, TILE)], axis=0
        )

    direct = columns % TILE == 0 and slabs & (slabs - 1) == 0 and ctrls & (ctrls - 1) == 0
    own_tiles = columns // TILE
    device = slab * ctrls + ctrl
    got = None
    if direct:
        table = pl.pallas_call(
            pack_kernel,
            out_shape=jax.ShapeDtypeStruct((own_tiles * ROWS, TILE), F32),
            in_specs=[vmem()] * 5,
            out_specs=vmem(),
        )(pressure, face_area, face_center, control_points, control_modes)
        place = jnp.zeros(tile_list.shape, jnp.int32)
        bit = slabs // 2
        order = []
        while bit:
            order.append((bit, 0))
            bit //= 2
        bit = ctrls // 2
        while bit:
            order.append((0, bit))
            bit //= 2
        for slab_bit, ctrl_bit in order:
            size = table.shape[0]
            if lend and slab_bit == unit:
                reply = swapped(jnp.concatenate([table, sent], axis=0), slab_bit, ctrl_bit)
                got = reply[size:]
                reply = reply[:size]
            else:
                reply = swapped(table, slab_bit, ctrl_bit)
            table = jnp.concatenate([table, reply], axis=0)

        def placed(number):
            apart = (number // own_tiles) ^ device
            at = jnp.zeros(number.shape, jnp.int32)
            for turn, (slab_bit, ctrl_bit) in enumerate(order):
                flag = slab_bit * ctrls + ctrl_bit
                at = at + jnp.where((apart & flag) != 0, 1 << turn, 0)
            return at * own_tiles + number % own_tiles
    else:
        loads = pl.pallas_call(
            loads_kernel,
            out_shape=jax.ShapeDtypeStruct((1, TILE), F32),
            in_specs=[vmem()] * 3,
            out_specs=vmem(),
        )(pressure, face_area, face_center)
        loads = lax.psum(loads, ("slab", "ctrl"))
        whole = jnp.concatenate([control_points, control_modes], axis=0)
        whole = lax.all_gather(whole, ("slab", "ctrl"), axis=1, tiled=True)
        whole = whole.reshape(7, 3, tiles, TILE).transpose(2, 1, 0, 3)
        spare = jnp.zeros((tiles, 3, 1, TILE), F32).at[0, 0, 0, :].set(loads[0])
        table = jnp.concatenate([whole, spare], axis=2).reshape(tiles * ROWS, TILE)

        def placed(number):
            return number

    if lend and got is None:
        got = swapped(sent, unit, 0)

    numbers = tile_list.reshape(own, slots)
    counts = tile_count
    extra = None
    if lend:
        mine_heavy = is_heavy(slab, slabs)
        helper = is_heavy(slab ^ unit, slabs) & jnp.logical_not(mine_heavy)
        plane_id = lax.broadcasted_iota(jnp.int32, (planes, rows), 0)
        row_id = lax.broadcasted_iota(jnp.int32, (planes, rows), 1)
        counts = jnp.where(mine_heavy & (plane_id >= keep) & (row_id >= 1), 0, counts)
        extra = got[: 3 * lent]
        listed = got[3 * lent :, : slots + 1].astype(jnp.int32)
        numbers = jnp.concatenate([numbers, listed[:, :slots]], axis=0)
        lent_row = lax.broadcasted_iota(jnp.int32, (planes - keep, rows), 1).reshape(-1)
        lent_counts = jnp.where(helper & (lent_row >= 1), listed[:, slots], 0)
        counts = jnp.concatenate([counts.reshape(-1), lent_counts])
    else:
        counts = counts.reshape(-1)
    lines = own + lent
    codes = (jnp.arange(lines, dtype=jnp.int32)[:, None] << bits) + placed(numbers)
    length = lines * slots + 6 * UNROLL + slots
    items, total = pl.pallas_call(
        functools.partial(list_kernel, lines, slots, lines << bits),
        out_shape=(
            jax.ShapeDtypeStruct((length,), jnp.int32),
            jax.ShapeDtypeStruct((1,), jnp.int32),
        ),
        in_specs=[smem()] * 2,
        out_specs=(smem(), smem()),
        cost_estimate=pl.CostEstimate(flops=0, bytes_accessed=4_000_000, transcendentals=0),
    )(codes.reshape(-1), counts)

    def wide(value):
        return jnp.pad(value, (0, TILE - value.shape[0])).reshape(1, TILE)

    outs = pl.pallas_call(
        functools.partial(shift_kernel, own, lent, bits),
        out_shape=(
            jax.ShapeDtypeStruct((3 * own, depth), F32),
            jax.ShapeDtypeStruct((3 * max(lent, 8), depth), F32),
            jax.ShapeDtypeStruct((1, TILE), F32),
            jax.ShapeDtypeStruct((2, 3 * planes, depth), F32),
            jax.ShapeDtypeStruct((2, 3 * rows, depth), F32),
        ),
        in_specs=[smem()] * 2 + [vmem()] * 6,
        out_specs=(vmem(),) * 5,
        scratch_shapes=[
            pltpu.VMEM((tiles * FEATS, TILE), F32),
            pltpu.VMEM(((lines + 1) * FEATS, depth), F32),
            pltpu.VMEM((tiles * 16, TILE), F32),
            pltpu.VMEM((tiles * TILE, FEATS), BF16),
            pltpu.VMEM(((lines + 1) * FEATS, depth), BF16),
            pltpu.VMEM((tiles * 16, 2 * TILE), BF16),
            pltpu.VMEM(((lines + 1) * 16, depth), F32),
        ]
        + [pltpu.VMEM((TILE, depth), F32)] * UNROLL
        + [pltpu.VMEM((2 * TILE, depth), BF16)] * UNROLL,
        compiler_params=pltpu.CompilerParams(vmem_limit_bytes=32 << 20),
    )(
        items, total, table, node_points.reshape(3 * own, depth),
        extra if lend else jnp.zeros((24, depth), F32),
        wide(motion), wide(inverse_mass), wide(jnp.array(GRAVITY, F32)),
    )
    shift, lent_shift, state, row_sent, plane_sent = outs

    if lend:
        back = lax.ppermute(lent_shift, "slab", [(h ^ unit, h) for h in heavy])
        back = back.reshape(3, planes - keep, rows, depth)
    else:
        back = jnp.zeros((3, 1, rows, depth), F32)
    row_halo = shifted_back(row_sent, "ctrl").reshape(2, 3, planes, depth)
    plane_sent = plane_sent.reshape(2, 3, rows, depth)
    plane_halo = shifted_back(
        jnp.concatenate([plane_sent, row_halo[:, :, :1]], axis=2), "slab"
    )
    node_shift, volume, change = pl.pallas_call(
        functools.partial(volume_kernel, keep, lend),
        out_shape=(
            jax.ShapeDtypeStruct(node_points.shape, F32),
            jax.ShapeDtypeStruct(node_points.shape[1:], F32),
            jax.ShapeDtypeStruct(node_points.shape[1:], F32),
        ),
        in_specs=[vmem()] * 5,
        out_specs=(vmem(),) * 3,
    )(node_points, shift.reshape(3, planes, rows, depth), back, row_halo, plane_halo)
    return node_shift, volume, change, state[0, : motion.shape[0]]


def solution(mesh):
    placed = (
        P(("slab", "ctrl")),
        P(None, ("slab", "ctrl")),
        P(None, ("slab", "ctrl")),
        P(),
        P(),
        P(None, ("slab", "ctrl")),
        P(None, ("slab", "ctrl")),
        P(None, "slab", "ctrl", None),
        P("slab", "ctrl", None),
        P("slab", "ctrl"),
    )
    return jax.shard_map(
        local,
        mesh=mesh,
        in_specs=placed,
        out_specs=(
            P(None, "slab", "ctrl", None),
            P("slab", "ctrl", None),
            P("slab", "ctrl", None),
            P(),
        ),
        check_vma=False,
    )
```

```python
import functools
import jax
import jax.numpy as jnp
from jax import lax
from jax.experimental import pallas as pl
from jax.experimental.pallas import tpu as pltpu
from jax.sharding import PartitionSpec as P

TILE = 128
TIME_STEP = 0.5
RADIUS = 4.0
GRAVITY = (0.0, 0.0, -0.5, 0.0, 0.0, 0.0)
ROWS = 24
FEATS = 32
UNROLL = 16
MIX = 48
TINY = 1e-30
F32 = jnp.float32
BF16 = jnp.bfloat16


def vmem():
    return pl.BlockSpec(memory_space=pltpu.VMEM)


def smem():
    return pl.BlockSpec(memory_space=pltpu.SMEM)


def swapped(value, slab_bit, ctrl_bit):
    slabs, ctrls = lax.axis_size("slab"), lax.axis_size("ctrl")
    pairs = [
        (s * ctrls + c, (s ^ slab_bit) * ctrls + (c ^ ctrl_bit))
        for s in range(slabs)
        for c in range(ctrls)
    ]
    return lax.ppermute(value, ("slab", "ctrl"), pairs)


def shifted_back(value, axis):
    return lax.ppermute(value, axis, [(i, i - 1) for i in range(1, lax.axis_size(axis))])


def load_rows(pressure, area, center):
    pushed = pressure * area

    def turned(value, by):
        return jnp.concatenate([value[by:3], value[0:by]], axis=0)

    moment = turned(center, 1) * turned(pushed, 2) - turned(center, 2) * turned(pushed, 1)
    sums = [jnp.sum(pushed, axis=1, keepdims=True), jnp.sum(moment, axis=1, keepdims=True)]
    lane = lax.broadcasted_iota(jnp.int32, (1, 128), 1)
    row = jnp.zeros((1, 128), F32)
    for k in range(6):
        row = jnp.where(lane == k, sums[k // 3][k % 3 : k % 3 + 1, :], row)
    return row


def pack_kernel(pressure, area, center, points, modes, out):
    row = load_rows(pressure[...], area[...], center[...])
    for t in range(out.shape[0] // ROWS):
        span = slice(t * TILE, (t + 1) * TILE)
        base = t * ROWS
        for c in range(3):
            out[base + 8 * c : base + 8 * c + 1, :] = points[c : c + 1, span]
            for k in range(6):
                at = base + 8 * c + 1 + k
                out[at : at + 1, :] = modes[3 * k + c : 3 * k + c + 1, span]
            at = base + 8 * c + 7
            out[at : at + 1, :] = row if (t == 0 and c == 0) else jnp.zeros((1, 128), F32)


def loads_kernel(pressure, area, center, out):
    out[...] = load_rows(pressure[...], area[...], center[...])


def split3(value):
    first = value.astype(BF16).astype(F32)
    rest = value - first
    second = rest.astype(BF16).astype(F32)
    return first, second, rest - second


def spread(ref, at):
    return jnp.broadcast_to(ref[pl.ds(at, 1), :], (8, ref.shape[1]))


def products(rows, scale, order, ends):
    row = lax.broadcasted_iota(jnp.int32, rows[0].shape, 0)
    norm = jnp.zeros(rows[0].shape, F32)
    blocks = []
    for value in rows:
        place = value * (1.0 / RADIUS)
        norm = norm + place * place
        first, second, third = split3(place * scale)
        low = jnp.where((row & 1) == 1, order[1](first, second, third, row), order[0](first, second, third, row))
        blocks.append(low)
    first, second, third = split3(norm)
    blocks.append(ends(first, second, third, row))
    return jnp.concatenate(blocks, axis=0)


def tile_block(rows):
    return products(
        rows,
        -2.0,
        (
            lambda a, b, c, row: jnp.where((row == 2) | (row == 6), b, a),
            lambda a, b, c, row: jnp.where(row == 1, a, jnp.where(row == 3, b, c)),
        ),
        lambda a, b, c, row: jnp.where(
            row == 0, a, jnp.where(row == 1, b, jnp.where(row == 2, c, jnp.where(row < 6, 1.0, 0.0)))
        ),
    )


def line_block(rows):
    return products(
        rows,
        1.0,
        (
            lambda a, b, c, row: jnp.where(row < 4, a, c),
            lambda a, b, c, row: jnp.where(row == 5, a, b),
        ),
        lambda a, b, c, row: jnp.where(
            row < 3, 1.0, jnp.where(row == 3, a, jnp.where(row == 4, b, jnp.where(row == 5, c, 0.0)))
        ),
    )


def lend_kernel(keep, points, numbers, counts, out):
    _, planes, rows, _ = points.shape
    slots = numbers.shape[2]
    lent = (planes - keep) * rows
    row = lax.broadcasted_iota(jnp.int32, (rows, rows), 0)
    lane = lax.broadcasted_iota(jnp.int32, (rows, rows), 1)
    wide = lax.broadcasted_iota(jnp.int32, (rows, out.shape[1]), 1)
    for x in range(keep, planes):
        at = (x - keep) * rows
        for c in range(3):
            out[c * lent + at : c * lent + at + rows, :] = points[c, x]
        many = jnp.broadcast_to(counts[x : x + 1, :].astype(F32), (rows, rows))
        column = jnp.sum(jnp.where(row == lane, many, 0.0), axis=1, keepdims=True)
        at = at + 3 * lent
        out[at : at + rows, :] = jnp.where(wide == slots, column, 0.0)
        out[at : at + rows, 0:slots] = numbers[x].astype(F32)


def prepare_kernel(
    first, slots, bits, placed, counted, numbers, counts, points,
    items_a, items_b, totals, line_feat, codes, listed, sem,
):
    lines = numbers.shape[0]
    number = numbers[:, 0:slots].astype(jnp.int32)
    count = counted(counts[...].astype(jnp.int32))
    row = lax.broadcasted_iota(jnp.int32, (lines, slots), 0)
    slot = lax.broadcasted_iota(jnp.int32, (lines, slots), 1)
    code = lax.shift_left(row + first, jnp.full_like(row, bits)) + placed(number)
    codes[:, 0:slots] = jnp.where(slot < count, code, -1)
    codes[:, slots : slots + 1] = count
    copy = pltpu.make_async_copy(codes, listed, sem)
    copy.start()

    def block(l, carry):
        rows = [spread(points, c * lines + l) for c in range(3)]
        at = pl.ds(pl.multiple_of(l * FEATS, FEATS), FEATS)
        line_feat[at, :] = line_block(rows).astype(BF16)
        return carry

    lax.fori_loop(0, lines, block, 0, unroll=4)
    copy.wait()
    step = 4

    def one(line, ends):
        def some(g, ends):
            end_a, end_b = ends
            for e in range(step):
                code = listed[line, g * step + e]
                live = 1 + lax.shift_right_arithmetic(code, 31)
                late = live & lax.shift_right_logical(code, bits - 1)
                items_a[end_a] = code
                items_b[end_b] = code
                end_a, end_b = end_a + (live - late), end_b + late
            return end_a, end_b

        groups = lax.shift_right_logical(listed[line, slots] + (step - 1), 2)
        return lax.fori_loop(0, groups, some, ends)

    end_a, end_b = lax.fori_loop(0, lines, one, (jnp.int32(0), jnp.int32(0)))
    dummy = (first + lines) << bits
    for e in range(2 * UNROLL):
        items_a[end_a + e] = dummy
        items_b[end_b + e] = dummy
    totals[0] = end_a
    totals[1] = end_b


def prepared(first, slots, bits, placed, counted, numbers, counts, points):
    lines, depth = numbers.shape[0], points.shape[1]
    length = lines * slots + 2 * UNROLL
    return pl.pallas_call(
        functools.partial(prepare_kernel, first, slots, bits, placed, counted),
        out_shape=(
            jax.ShapeDtypeStruct((length,), jnp.int32),
            jax.ShapeDtypeStruct((length,), jnp.int32),
            jax.ShapeDtypeStruct((2,), jnp.int32),
            jax.ShapeDtypeStruct((lines * FEATS, depth), BF16),
        ),
        in_specs=[vmem()] * 3,
        out_specs=(smem(), smem(), smem(), vmem()),
        scratch_shapes=[
            pltpu.VMEM((lines, TILE), jnp.int32),
            pltpu.SMEM((lines, TILE), jnp.int32),
            pltpu.SemaphoreType.DMA,
        ],
        cost_estimate=pl.CostEstimate(flops=0, bytes_accessed=8_000_000, transcendentals=0),
    )(numbers, counts, points)


def add_items(bits, half, lists, table, feats, line_feat, tile_feat, modes, acc, squares):
    tiles = table.shape[0] // ROWS
    at = 0
    for feat in feats:
        line_feat[at : at + feat.shape[0], :] = feat[...]
        at += feat.shape[0]
    line_feat[at:, :] = jnp.zeros((line_feat.shape[0] - at, line_feat.shape[1]), BF16)
    first = lists[0][1][half]
    count = sum(total[half] for _, total in lists)

    def build(t, carry):
        base = pl.multiple_of(t * ROWS, 8)
        rows = [spread(table, base + 8 * c) for c in range(3)]
        block = tile_block(rows)
        tile_feat[pl.ds(pl.multiple_of(t * TILE, TILE), TILE), :] = block.T.astype(BF16)
        value = 4.0 * table[pl.ds(base, ROWS), :]
        high = value.astype(BF16)
        low = (value - high.astype(F32)).astype(BF16)
        at = pl.ds(pl.multiple_of(t * MIX, 16), MIX)
        modes[at, :] = jnp.concatenate([high, low], axis=0)
        return carry

    lax.fori_loop(0, tiles, build, 0, unroll=4)
    mask = tiles - 1

    def unpack(at):
        code = lists[0][0][jnp.minimum(at, first)]
        if len(lists) > 1:
            code = jnp.where(at < first, code, lists[1][0][jnp.maximum(at - first, 0)])
        return lax.shift_right_logical(code, bits), code & mask

    def distances(u, at):
        line, tile = unpack(at)
        squares[u][...] = jnp.dot(
            tile_feat[pl.ds(pl.multiple_of(tile * TILE, TILE), TILE), :],
            line_feat[pl.ds(pl.multiple_of(line * FEATS, FEATS), FEATS), :],
            preferred_element_type=F32,
        )

    def gather(u, at):
        line, tile = unpack(at)
        square = jnp.maximum(squares[u][...], TINY)
        near = jnp.maximum(1.0 - square * lax.rsqrt(square), 0.0)
        fourth = near * near
        fourth = fourth * fourth
        phi = fourth * (1.25 - near)
        high = phi.astype(BF16)
        low = (phi - high.astype(F32)).astype(BF16)
        mode = modes[pl.ds(pl.multiple_of(tile * MIX, 16), MIX), :]
        got = jnp.dot(
            jnp.concatenate([mode, mode], axis=1),
            jnp.concatenate([high, low], axis=0),
            preferred_element_type=F32,
        )
        where = pl.ds(pl.multiple_of(line * ROWS, 8), ROWS)
        acc[where, :] = acc[where, :] + (got[0:ROWS] + got[ROWS:MIX])

    def body(j, carry):
        base = j * UNROLL
        for u in range(UNROLL):
            gather(u, base + u)
            distances(u, base + UNROLL + u)
        return carry

    for u in range(UNROLL):
        distances(u, u)
    lax.fori_loop(0, lax.div(count + (UNROLL - 1), jnp.int32(UNROLL)), body, 0)


def load_sum(table):
    tiles = table.shape[0] // ROWS
    return jnp.sum(table[pl.ds(7, tiles, stride=ROWS), :], axis=0, keepdims=True)


def early_kernel(parts, bits, *refs):
    lists = [(refs[i], refs[i + 1]) for i in range(0, 2 * parts, 2)]
    feats = refs[2 * parts : 3 * parts]
    table, acc, loads, line_feat, tile_feat, modes, *squares = refs[3 * parts :]
    acc[...] = jnp.zeros(acc.shape, F32)
    loads[...] = load_sum(table)
    add_items(bits, 0, lists, table, feats, line_feat, tile_feat, modes, acc, squares)


def late_kernel(own, lent, parts, bits, *refs):
    lists = [(refs[i], refs[i + 1]) for i in range(0, 2 * parts, 2)]
    feats = refs[2 * parts : 3 * parts]
    table, early, loads, points, motion, inverse, gravity, *rest = refs[3 * parts :]
    out_own, out_extra, out_state, out_row, out_plane, *rest = rest
    line_feat, tile_feat, modes, acc, *squares = rest
    total = loads[...] + load_sum(table)
    acceleration = inverse[...] * total + gravity[...]
    out_state[...] = motion[...] + TIME_STEP * acceleration
    step = TIME_STEP * motion[...] + 0.5 * TIME_STEP * TIME_STEP * acceleration
    row = lax.broadcasted_iota(jnp.int32, (8, 128), 0)
    lane = lax.broadcasted_iota(jnp.int32, (8, 128), 1)
    chosen = jnp.where((lane == row - 1) & (lane < 6), jnp.broadcast_to(step, (8, 128)), 0.0)
    weight = jnp.broadcast_to(jnp.sum(chosen, axis=1, keepdims=True), (8, 128))

    acc[...] = early[...]
    add_items(bits, 1, lists, table, feats, line_feat, tile_feat, modes, acc, squares)

    def finish(count, first, out):
        def one(l, carry):
            base = pl.multiple_of((first + l) * ROWS, 8)
            for c in range(3):
                value = jnp.sum(weight * acc[pl.ds(base + 8 * c, 8), :], axis=0, keepdims=True)
                out[pl.ds(c * count + l, 1), :] = value
            return carry

        lax.fori_loop(0, count, one, 0, unroll=4)

    finish(own, 0, out_own)
    if lent:
        finish(lent, own, out_extra)
    rows = out_row.shape[1] // 3
    wide = out_plane.shape[1] // 3
    for c in range(3):
        old = points[c * own : c * own + wide, :]
        out_plane[0, c * wide : (c + 1) * wide, :] = old
        out_plane[1, c * wide : (c + 1) * wide, :] = old + out_own[c * own : c * own + wide, :]
        old = points[pl.ds(c * own, rows, stride=wide), :]
        out_row[0, c * rows : (c + 1) * rows, :] = old
        out_row[1, c * rows : (c + 1) * rows, :] = (
            old + out_own[pl.ds(c * own, rows, stride=wide), :]
        )


def volume_kernel(
    keep, has_lent, points, shift, back, row_halo, plane_halo,
    out_shift, out_volume, out_change,
):
    planes, rows, depth = points.shape[1:]
    slab, ctrl = lax.axis_index("slab"), lax.axis_index("ctrl")
    slabs, ctrls = lax.axis_size("slab"), lax.axis_size("ctrl")
    row_id = lax.broadcasted_iota(jnp.int32, (rows, depth), 0)
    lane = lax.broadcasted_iota(jnp.int32, (rows, depth), 1)
    inside = (lane < depth - 1) & (row_id + ctrl * rows < ctrls * rows - 1)
    if has_lent:
        from_helper = (row_id >= 1) & is_heavy(slab, slabs)
    last_row = row_id == rows - 1

    def next_row(value, edge):
        return jnp.where(last_row, edge, pltpu.roll(value, rows - 1, 0))

    def next_depth(value):
        return pltpu.roll(value, depth - 1, 1)

    def level(x):
        found = []
        for field in range(2):
            parts = []
            for c in range(3):
                if x == planes:
                    here = plane_halo[field, c, 0:rows, :]
                    edge = plane_halo[field, c, rows : rows + 1, :]
                else:
                    here = points[c, x]
                    if field == 1:
                        moved = shift[c, x]
                        if has_lent and x >= keep:
                            moved = jnp.where(from_helper, back[c, x - keep], moved)
                        out_shift[c, x] = moved
                        here = here + moved
                    edge = row_halo[field, c, x : x + 1, :]
                there = next_row(here, edge)
                parts.append((here + there, there - here))
            found.append(parts)
        return found

    before = level(0)
    for x in range(planes):
        after = level(x + 1)
        volumes = []
        for field in range(2):
            edges = []
            for c in range(3):
                both0, step0 = before[field][c]
                both1, step1 = after[field][c]
                along, across, total = both1 - both0, step0 + step1, both0 + both1
                edges.append(
                    (
                        0.25 * (along + next_depth(along)),
                        0.25 * (across + next_depth(across)),
                        0.25 * (next_depth(total) - total),
                    )
                )
            ex, ey, ez = zip(*edges)
            volumes.append(
                ex[0] * (ey[1] * ez[2] - ey[2] * ez[1])
                + ex[1] * (ey[2] * ez[0] - ey[0] * ez[2])
                + ex[2] * (ey[0] * ez[1] - ey[1] * ez[0])
            )
        live = inside & (slab * planes + x < slabs * planes - 1)
        out_volume[x] = jnp.where(live, volumes[1], 0.0)
        out_change[x] = jnp.where(live, volumes[1] - volumes[0], 0.0)
        before = after


def is_heavy(slab, slabs):
    return (8 * slab >= 3 * slabs) & (8 * slab < 5 * slabs)


def local(
    face_pressure,
    face_area,
    face_center,
    motion,
    inverse_mass,
    control_points,
    control_modes,
    node_points,
    tile_list,
    tile_count,
):
    slabs, ctrls = lax.axis_size("slab"), lax.axis_size("ctrl")
    slab, ctrl = lax.axis_index("slab"), lax.axis_index("ctrl")
    _, planes, rows, depth = node_points.shape
    slots = tile_list.shape[2]
    own = planes * rows
    columns = control_points.shape[1]
    tiles = columns * slabs * ctrls // TILE
    bits = max(1, (tiles - 1).bit_length())
    pressure = face_pressure.reshape(1, -1)

    lend = slabs % 8 == 0 and slabs & (slabs - 1) == 0 and planes % 2 == 0
    unit = slabs // 8 * 2
    keep = planes // 2
    lent = (planes - keep) * rows if lend else 0
    heavy = [s for s in range(slabs) if is_heavy(s, slabs)]

    if lend:
        sent = pl.pallas_call(
            functools.partial(lend_kernel, keep),
            out_shape=jax.ShapeDtypeStruct((4 * lent, TILE), F32),
            in_specs=[vmem()] * 3,
            out_specs=vmem(),
            cost_estimate=pl.CostEstimate(flops=0, bytes_accessed=2_000_000, transcendentals=0),
        )(node_points, tile_list, tile_count)

    direct = columns % TILE == 0 and slabs & (slabs - 1) == 0 and ctrls & (ctrls - 1) == 0
    direct = direct and ctrls > 1 and (columns // TILE) & (columns // TILE - 1) == 0
    own_tiles = columns // TILE
    got = None
    order = []
    bit = slabs // 2
    while bit:
        order.append((bit, 0))
        bit //= 2
    bit = 1
    while bit < ctrls:
        order.append((0, bit))
        bit *= 2

    def placed(number):
        if not direct:
            return number
        device = lax.axis_index("slab") * ctrls + lax.axis_index("ctrl")
        apart = (number >> (own_tiles.bit_length() - 1)) ^ device
        at = jnp.zeros(number.shape, jnp.int32)
        for turn, (slab_bit, ctrl_bit) in enumerate(order):
            flag = slab_bit * ctrls + ctrl_bit
            at = at + jnp.where((apart & flag) != 0, own_tiles << turn, 0)
        return at + (number & (own_tiles - 1))

    plane_id = lax.broadcasted_iota(jnp.int32, (planes, rows), 0)
    row_id = lax.broadcasted_iota(jnp.int32, (planes, rows), 1)
    counts = tile_count
    if lend:
        lends = is_heavy(slab, slabs) & (plane_id >= keep) & (row_id >= 1)
        counts = jnp.where(lends, 0, counts)
    flat_points = node_points.reshape(3 * own, depth)
    own_lists = prepared(
        0, slots, bits, placed, lambda count: count,
        tile_list.reshape(own, slots), counts.reshape(own, 1), flat_points,
    )

    def borrowed(got):
        def counted(count):
            at = lax.axis_index("slab")
            helper = is_heavy(at ^ unit, slabs) & jnp.logical_not(is_heavy(at, slabs))
            line = lax.broadcasted_iota(jnp.int32, count.shape, 0)
            return jnp.where(helper & (line % rows >= 1), count, 0)

        listed = got[3 * lent :]
        return prepared(
            own, slots, bits, placed, counted, listed, listed[:, slots : slots + 1], got[: 3 * lent]
        )

    if direct:
        early = pl.pallas_call(
            pack_kernel,
            out_shape=jax.ShapeDtypeStruct((own_tiles * ROWS, TILE), F32),
            in_specs=[vmem()] * 5,
            out_specs=vmem(),
        )(pressure, face_area, face_center, control_points, control_modes)
        own_ready, lent_ready = False, False
        for slab_bit, ctrl_bit in order[:-1]:
            size = early.shape[0]
            if got is not None and not own_ready:
                early, own_lists = lax.optimization_barrier((early, own_lists))
                own_ready = True
            elif own_ready and not lent_ready:
                early, lent_lists = lax.optimization_barrier((early, lent_lists))
                lent_ready = True
            if lend and slab_bit == unit:
                reply = swapped(jnp.concatenate([early, sent], axis=0), slab_bit, ctrl_bit)
                got = reply[size:]
                reply = reply[:size]
                lent_lists = borrowed(got)
            else:
                reply = swapped(early, slab_bit, ctrl_bit)
            early = jnp.concatenate([early, reply], axis=0)
        late = swapped(early, *order[-1])
    else:
        loads = pl.pallas_call(
            loads_kernel,
            out_shape=jax.ShapeDtypeStruct((1, TILE), F32),
            in_specs=[vmem()] * 3,
            out_specs=vmem(),
        )(pressure, face_area, face_center)
        loads = lax.psum(loads, ("slab", "ctrl"))
        whole = jnp.concatenate([control_points, control_modes], axis=0)
        whole = lax.all_gather(whole, ("slab", "ctrl"), axis=1, tiled=True)
        whole = whole.reshape(7, 3, tiles, TILE).transpose(2, 1, 0, 3)
        spare = jnp.zeros((tiles, 3, 1, TILE), F32).at[0, 0, 0, :].set(loads[0])
        table = jnp.concatenate([whole, spare], axis=2).reshape(tiles * ROWS, TILE)
        early, late = table[: tiles // 2 * ROWS], table[tiles // 2 * ROWS :]

    if lend and got is None:
        lent_lists = borrowed(swapped(sent, unit, 0))
    groups = [own_lists] + ([lent_lists] if lend else [])
    lines = own + lent

    def wide(value):
        return jnp.pad(value, (0, TILE - value.shape[0])).reshape(1, TILE)

    half = tiles // 2
    parts = len(groups)
    early_items = [ref for group in groups for ref in (group[0], group[2])]
    late_items = [ref for group in groups for ref in (group[1], group[2])]
    feats = [group[3] for group in groups]
    list_specs = [smem()] * (2 * parts) + [vmem()] * parts
    scratch = [
        pltpu.VMEM(((lines + 1) * FEATS, depth), BF16),
        pltpu.VMEM((half * TILE, FEATS), BF16),
        pltpu.VMEM((half * MIX, TILE), BF16),
    ]
    squares = [pltpu.VMEM((TILE, depth), F32)] * UNROLL
    partial, part_loads = pl.pallas_call(
        functools.partial(early_kernel, parts, bits),
        out_shape=(
            jax.ShapeDtypeStruct(((lines + 1) * ROWS, depth), F32),
            jax.ShapeDtypeStruct((1, TILE), F32),
        ),
        in_specs=list_specs + [vmem()],
        out_specs=(vmem(), vmem()),
        scratch_shapes=scratch + squares,
        compiler_params=pltpu.CompilerParams(vmem_limit_bytes=32 << 20),
        cost_estimate=pl.CostEstimate(flops=0, bytes_accessed=30_000_000, transcendentals=0),
    )(*early_items, *feats, early)
    outs = pl.pallas_call(
        functools.partial(late_kernel, own, lent, parts, bits),
        out_shape=(
            jax.ShapeDtypeStruct((3 * own, depth), F32),
            jax.ShapeDtypeStruct((3 * max(lent, 8), depth), F32),
            jax.ShapeDtypeStruct((1, TILE), F32),
            jax.ShapeDtypeStruct((2, 3 * planes, depth), F32),
            jax.ShapeDtypeStruct((2, 3 * rows, depth), F32),
        ),
        in_specs=list_specs + [vmem()] * 7,
        out_specs=(vmem(),) * 5,
        scratch_shapes=scratch + [pltpu.VMEM(((lines + 1) * ROWS, depth), F32)] + squares,
        compiler_params=pltpu.CompilerParams(vmem_limit_bytes=32 << 20),
    )(
        *late_items, *feats, late, partial, part_loads, flat_points,
        wide(motion), wide(inverse_mass), wide(jnp.array(GRAVITY, F32)),
    )
    shift, lent_shift, state, row_sent, plane_sent = outs

    if lend:
        back = lax.ppermute(lent_shift, "slab", [(h ^ unit, h) for h in heavy])
        back = back.reshape(3, planes - keep, rows, depth)
    else:
        back = jnp.zeros((3, 1, rows, depth), F32)
    row_halo = shifted_back(row_sent, "ctrl").reshape(2, 3, planes, depth)
    plane_sent = plane_sent.reshape(2, 3, rows, depth)
    plane_halo = shifted_back(
        jnp.concatenate([plane_sent, row_halo[:, :, :1]], axis=2), "slab"
    )
    node_shift, volume, change = pl.pallas_call(
        functools.partial(volume_kernel, keep, lend),
        out_shape=(
            jax.ShapeDtypeStruct(node_points.shape, F32),
            jax.ShapeDtypeStruct(node_points.shape[1:], F32),
            jax.ShapeDtypeStruct(node_points.shape[1:], F32),
        ),
        in_specs=[vmem()] * 5,
        out_specs=(vmem(),) * 3,
    )(node_points, shift.reshape(3, planes, rows, depth), back, row_halo, plane_halo)
    return node_shift, volume, change, state[0, : motion.shape[0]]


def solution(mesh):
    placed = (
        P(("slab", "ctrl")),
        P(None, ("slab", "ctrl")),
        P(None, ("slab", "ctrl")),
        P(),
        P(),
        P(None, ("slab", "ctrl")),
        P(None, ("slab", "ctrl")),
        P(None, "slab", "ctrl", None),
        P("slab", "ctrl", None),
        P("slab", "ctrl"),
    )
    return jax.shard_map(
        local,
        mesh=mesh,
        in_specs=placed,
        out_specs=(
            P(None, "slab", "ctrl", None),
            P("slab", "ctrl", None),
            P("slab", "ctrl", None),
            P(),
        ),
        check_vma=False,
    )
```

```python
import functools
import jax
import jax.numpy as jnp
from jax import lax
from jax.experimental import pallas as pl
from jax.experimental.pallas import tpu as pltpu
from jax.sharding import PartitionSpec as P

TILE = 128
TIME_STEP = 0.5
RADIUS = 4.0
GRAVITY = (0.0, 0.0, -0.5, 0.0, 0.0, 0.0)
ROWS = 24
FEATS = 32
UNROLL = 16
MIX = 48
TINY = 1e-30
F32 = jnp.float32
BF16 = jnp.bfloat16


def limited(mib):
    return pltpu.CompilerParams(vmem_limit_bytes=mib << 20)


def vmem():
    return pl.BlockSpec(memory_space=pltpu.VMEM)


def smem():
    return pl.BlockSpec(memory_space=pltpu.SMEM)


def swapped(value, slab_bit, ctrl_bit):
    slabs, ctrls = lax.axis_size("slab"), lax.axis_size("ctrl")
    pairs = [
        (s * ctrls + c, (s ^ slab_bit) * ctrls + (c ^ ctrl_bit))
        for s in range(slabs)
        for c in range(ctrls)
    ]
    return lax.ppermute(value, ("slab", "ctrl"), pairs)


def shifted_back(value, axis):
    return lax.ppermute(value, axis, [(i, i - 1) for i in range(1, lax.axis_size(axis))])


def load_rows(pressure, area, center):
    pushed = pressure * area

    def turned(value, by):
        return jnp.concatenate([value[by:3], value[0:by]], axis=0)

    moment = turned(center, 1) * turned(pushed, 2) - turned(center, 2) * turned(pushed, 1)
    sums = [jnp.sum(pushed, axis=1, keepdims=True), jnp.sum(moment, axis=1, keepdims=True)]
    lane = lax.broadcasted_iota(jnp.int32, (1, 128), 1)
    row = jnp.zeros((1, 128), F32)
    for k in range(6):
        row = jnp.where(lane == k, sums[k // 3][k % 3 : k % 3 + 1, :], row)
    return row


def pack_table(row, points, modes, out):
    for t in range(points.shape[1] // TILE):
        span = slice(t * TILE, (t + 1) * TILE)
        base = t * ROWS
        for c in range(3):
            out[base + 8 * c : base + 8 * c + 1, :] = points[c : c + 1, span]
            for k in range(6):
                at = base + 8 * c + 1 + k
                out[at : at + 1, :] = modes[3 * k + c : 3 * k + c + 1, span]
            at = base + 8 * c + 7
            out[at : at + 1, :] = row if (t == 0 and c == 0) else jnp.zeros((1, 128), F32)


def count_column(counts, x):
    rows = counts.shape[1]
    row = lax.broadcasted_iota(jnp.int32, (rows, rows), 0)
    lane = lax.broadcasted_iota(jnp.int32, (rows, rows), 1)
    many = jnp.broadcast_to(counts[x : x + 1, :].astype(F32), (rows, rows))
    return jnp.sum(jnp.where(row == lane, many, 0.0), axis=1, keepdims=True)


def pack_lent(planes, base, nodes, numbers, counts, out):
    rows, slots = numbers.shape[1:]
    lent = len(planes) * rows
    wide = lax.broadcasted_iota(jnp.int32, (rows, out.shape[1]), 1)
    for i, x in enumerate(planes):
        at = base + i * rows
        for c in range(3):
            out[at + c * lent : at + c * lent + rows, :] = nodes[c, x]
        at = at + 3 * lent
        out[at : at + rows, :] = jnp.where(wide == slots, count_column(counts, x), 0.0)
        out[at : at + rows, 0:slots] = numbers[x].astype(F32)


def pack_kernel(spans, pressure, area, center, points, modes, nodes, numbers, counts, out, *lents):
    row = load_rows(pressure[...], area[...], center[...])
    pack_table(row, points, modes, out)
    if spans:
        pack_lent(spans[0], points.shape[1] // TILE * ROWS, nodes, numbers, counts, out)
    for span, lent in zip(spans[1:], lents):
        pack_lent(span, 0, nodes, numbers, counts, lent)


def lend_kernel(spans, nodes, numbers, counts, *outs):
    for span, out in zip(spans, outs):
        pack_lent(span, 0, nodes, numbers, counts, out)


def loads_kernel(pressure, area, center, out):
    out[...] = load_rows(pressure[...], area[...], center[...])


def split3(value):
    first = value.astype(BF16).astype(F32)
    rest = value - first
    second = rest.astype(BF16).astype(F32)
    return first, second, rest - second


def spread(ref, at):
    return jnp.broadcast_to(ref[pl.ds(at, 1), :], (8, ref.shape[1]))


def products(rows, scale, order, ends):
    row = lax.broadcasted_iota(jnp.int32, rows[0].shape, 0)
    norm = jnp.zeros(rows[0].shape, F32)
    blocks = []
    for value in rows:
        place = value * (1.0 / RADIUS)
        norm = norm + place * place
        first, second, third = split3(place * scale)
        low = jnp.where((row & 1) == 1, order[1](first, second, third, row), order[0](first, second, third, row))
        blocks.append(low)
    first, second, third = split3(norm)
    blocks.append(ends(first, second, third, row))
    return jnp.concatenate(blocks, axis=0)


def tile_block(rows):
    return products(
        rows,
        -2.0,
        (
            lambda a, b, c, row: jnp.where((row == 2) | (row == 6), b, a),
            lambda a, b, c, row: jnp.where(row == 1, a, jnp.where(row == 3, b, c)),
        ),
        lambda a, b, c, row: jnp.where(
            row == 0, a, jnp.where(row == 1, b, jnp.where(row == 2, c, jnp.where(row < 6, 1.0, 0.0)))
        ),
    )


def line_block(rows):
    return products(
        rows,
        1.0,
        (
            lambda a, b, c, row: jnp.where(row < 4, a, c),
            lambda a, b, c, row: jnp.where(row == 5, a, b),
        ),
        lambda a, b, c, row: jnp.where(
            row < 3, 1.0, jnp.where(row == 3, a, jnp.where(row == 4, b, jnp.where(row == 5, c, 0.0)))
        ),
    )


def build_lists(lines, slots, bits, first, listed, items_a, items_b, totals):
    step = 4

    def one(line, ends):
        def some(g, ends):
            end_a, end_b = ends
            found = [listed[line, g * step + e] for e in range(step)]
            live = [1 + lax.shift_right_arithmetic(code, 31) for code in found]
            late = [n & lax.shift_right_logical(code, bits - 1) for n, code in zip(live, found)]
            for code, n, m in zip(found, live, late):
                items_a[end_a] = code
                items_b[end_b] = code
                end_a, end_b = end_a + (n - m), end_b + m
            return end_a, end_b

        groups = lax.shift_right_logical(listed[line, slots] + (step - 1), 2)
        return lax.fori_loop(0, groups, some, ends)

    end_a, end_b = lax.fori_loop(0, lines, one, (jnp.int32(0), jnp.int32(0)))
    dummy = (first + lines) << bits
    for e in range(2 * UNROLL):
        items_a[end_a + e] = dummy
        items_b[end_b + e] = dummy
    totals[0] = end_a
    totals[1] = end_b


def line_features(lines, points, line_feat):
    def block(l, carry):
        rows = [spread(points, c * lines + l) for c in range(3)]
        at = pl.ds(pl.multiple_of(l * FEATS, FEATS), FEATS)
        line_feat[at, :] = line_block(rows).astype(BF16)
        return carry

    lax.fori_loop(0, lines, block, 0, unroll=4)


def coded(first, bits, placed, number, count):
    row = lax.broadcasted_iota(jnp.int32, number.shape, 0)
    slot = lax.broadcasted_iota(jnp.int32, number.shape, 1)
    code = lax.shift_left(row + first, jnp.full_like(row, bits)) + placed(number)
    return jnp.where(slot < count, code, -1)


def own_kernel(
    keep, bits, placed, points, numbers, counts,
    items_a, items_b, totals, line_feat, codes, listed, sem,
):
    planes, rows, slots = numbers.shape
    slabs = lax.axis_size("slab")
    lends = is_heavy(lax.axis_index("slab"), slabs)
    for x in range(planes):
        count = count_column(counts, x).astype(jnp.int32)
        if x >= keep:
            row = lax.broadcasted_iota(jnp.int32, count.shape, 0)
            count = jnp.where(lends & (row >= 1), 0, count)
        span = slice(x * rows, (x + 1) * rows)
        codes[span, 0:slots] = coded(x * rows, bits, placed, numbers[x], count)
        codes[span, slots : slots + 1] = count
    copy = pltpu.make_async_copy(codes, listed, sem)
    copy.start()
    line_features(planes * rows, points, line_feat)
    copy.wait()
    build_lists(planes * rows, slots, bits, 0, listed, items_a, items_b, totals)


def lent_kernel(
    first, rows, slots, lent, bits, placed, units, bases, *refs
):
    gots, refs = refs[: len(units)], refs[len(units) :]
    items_a, items_b, totals, line_feat, codes, listed, got, sem = refs
    slab, slabs = lax.axis_index("slab"), lax.axis_size("slab")
    value = gots[-1][pl.ds(bases[-1], 4 * lent), :]
    for unit, base, ref in list(zip(units, bases, gots))[:-1]:
        value = jnp.where(is_heavy(slab ^ unit, slabs), ref[pl.ds(base, 4 * lent), :], value)
    got[...] = value
    helps = jnp.logical_not(is_heavy(slab, slabs))
    number = got[3 * lent :, 0:slots].astype(jnp.int32)
    count = got[3 * lent :, slots : slots + 1].astype(jnp.int32)
    line = lax.broadcasted_iota(jnp.int32, count.shape, 0)
    count = jnp.where(helps & (lax.rem(line, rows) >= 1), count, 0)
    codes[:, 0:slots] = coded(first, bits, placed, number, count)
    codes[:, slots : slots + 1] = count
    copy = pltpu.make_async_copy(codes, listed, sem)
    copy.start()
    line_features(lent, got, line_feat)
    copy.wait()
    build_lists(lent, slots, bits, first, listed, items_a, items_b, totals)


def prepared(kernel, lines, slots, depth, scratch, *operands):
    length = lines * slots + 2 * UNROLL
    return pl.pallas_call(
        kernel,
        out_shape=(
            jax.ShapeDtypeStruct((length,), jnp.int32),
            jax.ShapeDtypeStruct((length,), jnp.int32),
            jax.ShapeDtypeStruct((2,), jnp.int32),
            jax.ShapeDtypeStruct((lines * FEATS, depth), BF16),
        ),
        in_specs=[vmem()] * len(operands),
        out_specs=(smem(), smem(), smem(), vmem()),
        scratch_shapes=[
            pltpu.VMEM((lines, TILE), jnp.int32),
            pltpu.SMEM((lines, TILE), jnp.int32),
        ]
        + scratch
        + [pltpu.SemaphoreType.DMA],
        compiler_params=limited(4),
        cost_estimate=pl.CostEstimate(flops=0, bytes_accessed=8_000_000, transcendentals=0),
    )(*operands)


def add_items(bits, half, lists, table, feats, line_feat, tile_feat, modes, acc, squares):
    tiles = table.shape[0] // ROWS
    at = 0
    for feat in feats:
        line_feat[at : at + feat.shape[0], :] = feat[...]
        at += feat.shape[0]
    line_feat[at:, :] = jnp.zeros((line_feat.shape[0] - at, line_feat.shape[1]), BF16)
    first = lists[0][1][half]
    count = sum(total[half] for _, total in lists)

    def build(t, carry):
        base = pl.multiple_of(t * ROWS, 8)
        rows = [spread(table, base + 8 * c) for c in range(3)]
        block = tile_block(rows)
        tile_feat[pl.ds(pl.multiple_of(t * TILE, TILE), TILE), :] = block.T.astype(BF16)
        value = 4.0 * table[pl.ds(base, ROWS), :]
        high = value.astype(BF16)
        low = (value - high.astype(F32)).astype(BF16)
        at = pl.ds(pl.multiple_of(t * MIX, 16), MIX)
        modes[at, :] = jnp.concatenate([high, low], axis=0)
        return carry

    lax.fori_loop(0, tiles, build, 0, unroll=4)
    mask = tiles - 1

    def unpack(at):
        code = lists[0][0][jnp.minimum(at, first)]
        if len(lists) > 1:
            code = jnp.where(at < first, code, lists[1][0][jnp.maximum(at - first, 0)])
        return lax.shift_right_logical(code, bits), code & mask

    def distances(u, at):
        line, tile = unpack(at)
        squares[u][...] = jnp.dot(
            tile_feat[pl.ds(pl.multiple_of(tile * TILE, TILE), TILE), :],
            line_feat[pl.ds(pl.multiple_of(line * FEATS, FEATS), FEATS), :],
            preferred_element_type=F32,
        )

    def gather(u, at):
        line, tile = unpack(at)
        square = jnp.maximum(squares[u][...], TINY)
        near = jnp.maximum(1.0 - square * lax.rsqrt(square), 0.0)
        fourth = near * near
        fourth = fourth * fourth
        phi = fourth * (1.25 - near)
        high = phi.astype(BF16)
        low = (phi - high.astype(F32)).astype(BF16)
        mode = modes[pl.ds(pl.multiple_of(tile * MIX, 16), MIX), :]
        got = jnp.dot(
            jnp.concatenate([mode, mode], axis=1),
            jnp.concatenate([high, low], axis=0),
            preferred_element_type=F32,
        )
        where = pl.ds(pl.multiple_of(line * ROWS, 8), ROWS)
        acc[where, :] = acc[where, :] + (got[0:ROWS] + got[ROWS:MIX])

    def body(j, carry):
        base = j * UNROLL
        for u in range(UNROLL):
            gather(u, base + u)
            distances(u, base + UNROLL + u)
        return carry

    for u in range(UNROLL):
        distances(u, u)
    lax.fori_loop(0, lax.div(count + (UNROLL - 1), jnp.int32(UNROLL)), body, 0)


def load_sum(table):
    tiles = table.shape[0] // ROWS
    return jnp.sum(table[pl.ds(7, tiles, stride=ROWS), :], axis=0, keepdims=True)


def early_kernel(parts, bits, *refs):
    lists = [(refs[i], refs[i + 1]) for i in range(0, 2 * parts, 2)]
    feats = refs[2 * parts : 3 * parts]
    table, acc, loads, line_feat, tile_feat, modes, *squares = refs[3 * parts :]
    acc[...] = jnp.zeros(acc.shape, F32)
    loads[...] = load_sum(table)
    add_items(bits, 0, lists, table, feats, line_feat, tile_feat, modes, acc, squares)


def late_kernel(own, lent, parts, bits, *refs):
    lists = [(refs[i], refs[i + 1]) for i in range(0, 2 * parts, 2)]
    feats = refs[2 * parts : 3 * parts]
    table, early, loads, points, motion, inverse, gravity, *rest = refs[3 * parts :]
    out_own, out_extra, out_state, out_row, out_plane, *rest = rest
    line_feat, tile_feat, modes, acc, *squares = rest
    total = loads[...] + load_sum(table)
    acceleration = inverse[...] * total + gravity[...]
    out_state[...] = motion[...] + TIME_STEP * acceleration
    step = TIME_STEP * motion[...] + 0.5 * TIME_STEP * TIME_STEP * acceleration
    row = lax.broadcasted_iota(jnp.int32, (8, 128), 0)
    lane = lax.broadcasted_iota(jnp.int32, (8, 128), 1)
    chosen = jnp.where((lane == row - 1) & (lane < 6), jnp.broadcast_to(step, (8, 128)), 0.0)
    weight = jnp.broadcast_to(jnp.sum(chosen, axis=1, keepdims=True), (8, 128))

    acc[...] = early[...]
    add_items(bits, 1, lists, table, feats, line_feat, tile_feat, modes, acc, squares)

    def finish(count, first, out):
        def one(l, carry):
            base = pl.multiple_of((first + l) * ROWS, 8)
            for c in range(3):
                value = jnp.sum(weight * acc[pl.ds(base + 8 * c, 8), :], axis=0, keepdims=True)
                out[pl.ds(c * count + l, 1), :] = value
            return carry

        lax.fori_loop(0, count, one, 0, unroll=4)

    finish(own, 0, out_own)
    if lent:
        finish(lent, own, out_extra)
    rows = out_row.shape[1] // 3
    wide = out_plane.shape[1] // 3
    for c in range(3):
        old = points[c * own : c * own + wide, :]
        out_plane[0, c * wide : (c + 1) * wide, :] = old
        out_plane[1, c * wide : (c + 1) * wide, :] = old + out_own[c * own : c * own + wide, :]
        old = points[pl.ds(c * own, rows, stride=wide), :]
        out_row[0, c * rows : (c + 1) * rows, :] = old
        out_row[1, c * rows : (c + 1) * rows, :] = (
            old + out_own[pl.ds(c * own, rows, stride=wide), :]
        )


def volume_kernel(
    keep, share, points, shift, row_halo, plane_halo, *refs
):
    *backs, out_shift, out_volume, out_change = refs
    planes, rows, depth = points.shape[1:]
    slab, ctrl = lax.axis_index("slab"), lax.axis_index("ctrl")
    slabs, ctrls = lax.axis_size("slab"), lax.axis_size("ctrl")
    row_id = lax.broadcasted_iota(jnp.int32, (rows, depth), 0)
    lane = lax.broadcasted_iota(jnp.int32, (rows, depth), 1)
    inside = (lane < depth - 1) & (row_id + ctrl * rows < ctrls * rows - 1)
    if backs:
        from_helper = (row_id >= 1) & is_heavy(slab, slabs)
    last_row = row_id == rows - 1

    def next_row(value, edge):
        return jnp.where(last_row, edge, pltpu.roll(value, rows - 1, 0))

    def next_depth(value):
        return pltpu.roll(value, depth - 1, 1)

    def level(x):
        found = []
        for field in range(2):
            parts = []
            for c in range(3):
                if x == planes:
                    here = plane_halo[field, c, 0:rows, :]
                    edge = plane_halo[field, c, rows : rows + 1, :]
                else:
                    here = points[c, x]
                    if field == 1:
                        moved = shift[c, x]
                        if backs and x >= keep:
                            back = backs[(x - keep) // share]
                            moved = jnp.where(from_helper, back[c, (x - keep) % share], moved)
                        out_shift[c, x] = moved
                        here = here + moved
                    edge = row_halo[field, c, x : x + 1, :]
                there = next_row(here, edge)
                parts.append((here + there, there - here))
            found.append(parts)
        return found

    before = level(0)
    for x in range(planes):
        after = level(x + 1)
        volumes = []
        for field in range(2):
            edges = []
            for c in range(3):
                both0, step0 = before[field][c]
                both1, step1 = after[field][c]
                along, across, total = both1 - both0, step0 + step1, both0 + both1
                edges.append(
                    (
                        0.25 * (along + next_depth(along)),
                        0.25 * (across + next_depth(across)),
                        0.25 * (next_depth(total) - total),
                    )
                )
            ex, ey, ez = zip(*edges)
            volumes.append(
                ex[0] * (ey[1] * ez[2] - ey[2] * ez[1])
                + ex[1] * (ey[2] * ez[0] - ey[0] * ez[2])
                + ex[2] * (ey[0] * ez[1] - ey[1] * ez[0])
            )
        live = inside & (slab * planes + x < slabs * planes - 1)
        out_volume[x] = jnp.where(live, volumes[1], 0.0)
        out_change[x] = jnp.where(live, volumes[1] - volumes[0], 0.0)
        before = after


def is_heavy(slab, slabs):
    return (8 * slab >= 3 * slabs) & (8 * slab < 5 * slabs)


def local(
    face_pressure,
    face_area,
    face_center,
    motion,
    inverse_mass,
    control_points,
    control_modes,
    node_points,
    tile_list,
    tile_count,
):
    slabs, ctrls = lax.axis_size("slab"), lax.axis_size("ctrl")
    slab, ctrl = lax.axis_index("slab"), lax.axis_index("ctrl")
    _, planes, rows, depth = node_points.shape
    slots = tile_list.shape[2]
    own = planes * rows
    columns = control_points.shape[1]
    tiles = columns * slabs * ctrls // TILE
    bits = max(1, (tiles - 1).bit_length())
    pressure = face_pressure.reshape(1, -1)

    unit = slabs // 8
    share = (planes - 1) // 3
    keep = planes - 3 * share
    lend = slabs % 8 == 0 and slabs & (slabs - 1) == 0 and share > 0
    units = (4 * unit, 2 * unit, unit) if lend else ()
    spans = [tuple(range(keep + g * share, keep + (g + 1) * share)) for g in range(len(units))]
    lent = share * rows if lend else 0
    heavy = [s for s in range(slabs) if is_heavy(s, slabs)]

    direct = columns % TILE == 0 and slabs & (slabs - 1) == 0 and ctrls & (ctrls - 1) == 0
    direct = direct and ctrls > 1 and (columns // TILE) & (columns // TILE - 1) == 0
    own_tiles = columns // TILE
    order = []
    bit = slabs // 2
    while bit:
        order.append((bit, 0))
        bit //= 2
    bit = 1
    while bit < ctrls:
        order.append((0, bit))
        bit *= 2

    def placed(number):
        if not direct:
            return number
        device = lax.axis_index("slab") * ctrls + lax.axis_index("ctrl")
        apart = (number >> (own_tiles.bit_length() - 1)) ^ device
        at = jnp.zeros(number.shape, jnp.int32)
        for turn, (slab_bit, ctrl_bit) in enumerate(order):
            flag = slab_bit * ctrls + ctrl_bit
            at = at + jnp.where((apart & flag) != 0, own_tiles << turn, 0)
        return at + (number & (own_tiles - 1))

    flat_points = node_points.reshape(3 * own, depth)
    own_lists = prepared(
        functools.partial(own_kernel, keep if lend else planes, bits, placed),
        own, slots, depth, [], flat_points, tile_list, tile_count,
    )

    def borrowed(gots, bases):
        kernel = functools.partial(
            lent_kernel, own, rows, slots, lent, bits, placed, units, tuple(bases)
        )
        return prepared(kernel, lent, slots, depth, [pltpu.VMEM((4 * lent, TILE), F32)], *gots)

    gots, bases = [], []
    if direct:
        size = own_tiles * ROWS
        first, *sents = pl.pallas_call(
            functools.partial(pack_kernel, spans),
            out_shape=[
                jax.ShapeDtypeStruct((rows_of, TILE), F32)
                for rows_of in [size + 4 * lent] + [4 * lent] * (len(units) - 1)
            ],
            in_specs=[vmem()] * 8,
            out_specs=[vmem()] * max(1, len(units)),
            compiler_params=limited(56),
        )(
            pressure, face_area, face_center, control_points, control_modes,
            node_points, tile_list, tile_count,
        )
        early = first[:size]
        for turn, (slab_bit, ctrl_bit) in enumerate(order[:-1]):
            size = early.shape[0]
            if turn == 2:
                early, own_lists = lax.optimization_barrier((early, own_lists))
            if turn == 3 and lend:
                early, lent_lists = lax.optimization_barrier((early, lent_lists))
            if lend and slab_bit in units:
                payload = jnp.concatenate([early, sents[len(gots) - 1]], axis=0) if gots else first
                reply = swapped(payload, slab_bit, ctrl_bit)
                gots.append(reply)
                bases.append(size)
                reply = reply[:size]
                if len(gots) == len(units):
                    lent_lists = borrowed(gots, bases)
            else:
                reply = swapped(early, slab_bit, ctrl_bit)
            early = jnp.concatenate([early, reply], axis=0)
        late = swapped(early, *order[-1])
    else:
        loads = pl.pallas_call(
            loads_kernel,
            out_shape=jax.ShapeDtypeStruct((1, TILE), F32),
            in_specs=[vmem()] * 3,
            out_specs=vmem(),
        )(pressure, face_area, face_center)
        loads = lax.psum(loads, ("slab", "ctrl"))
        whole = jnp.concatenate([control_points, control_modes], axis=0)
        whole = lax.all_gather(whole, ("slab", "ctrl"), axis=1, tiled=True)
        whole = whole.reshape(7, 3, tiles, TILE).transpose(2, 1, 0, 3)
        spare = jnp.zeros((tiles, 3, 1, TILE), F32).at[0, 0, 0, :].set(loads[0])
        table = jnp.concatenate([whole, spare], axis=2).reshape(tiles * ROWS, TILE)
        early, late = table[: tiles // 2 * ROWS], table[tiles // 2 * ROWS :]
        if lend:
            sents = pl.pallas_call(
                functools.partial(lend_kernel, spans),
                out_shape=[jax.ShapeDtypeStruct((4 * lent, TILE), F32)] * len(units),
                in_specs=[vmem()] * 3,
                out_specs=[vmem()] * len(units),
            )(node_points, tile_list, tile_count)
            gots = [swapped(sent, bit, 0) for sent, bit in zip(sents, units)]
            lent_lists = borrowed(gots, [0] * len(units))
    groups = [own_lists] + ([lent_lists] if lend else [])
    lines = own + lent

    def wide(value):
        return jnp.pad(value, (0, TILE - value.shape[0])).reshape(1, TILE)

    half = tiles // 2
    parts = len(groups)
    early_items = [ref for group in groups for ref in (group[0], group[2])]
    late_items = [ref for group in groups for ref in (group[1], group[2])]
    feats = [group[3] for group in groups]
    list_specs = [smem()] * (2 * parts) + [vmem()] * parts
    scratch = [
        pltpu.VMEM(((lines + 1) * FEATS, depth), BF16),
        pltpu.VMEM((half * TILE, FEATS), BF16),
        pltpu.VMEM((half * MIX, TILE), BF16),
    ]
    squares = [pltpu.VMEM((TILE, depth), F32)] * UNROLL
    partial, part_loads = pl.pallas_call(
        functools.partial(early_kernel, parts, bits),
        out_shape=(
            jax.ShapeDtypeStruct(((lines + 1) * ROWS, depth), F32),
            jax.ShapeDtypeStruct((1, TILE), F32),
        ),
        in_specs=list_specs + [vmem()],
        out_specs=(vmem(), vmem()),
        scratch_shapes=scratch + squares,
        compiler_params=limited(16),
        cost_estimate=pl.CostEstimate(flops=0, bytes_accessed=30_000_000, transcendentals=0),
    )(*early_items, *feats, early)
    outs = pl.pallas_call(
        functools.partial(late_kernel, own, lent, parts, bits),
        out_shape=(
            jax.ShapeDtypeStruct((3 * own, depth), F32),
            jax.ShapeDtypeStruct((3 * max(lent, 8), depth), F32),
            jax.ShapeDtypeStruct((1, TILE), F32),
            jax.ShapeDtypeStruct((2, 3 * planes, depth), F32),
            jax.ShapeDtypeStruct((2, 3 * rows, depth), F32),
        ),
        in_specs=list_specs + [vmem()] * 7,
        out_specs=(vmem(),) * 5,
        scratch_shapes=scratch + [pltpu.VMEM(((lines + 1) * ROWS, depth), F32)] + squares,
        compiler_params=limited(16),
    )(
        *late_items, *feats, late, partial, part_loads, flat_points,
        wide(motion), wide(inverse_mass), wide(jnp.array(GRAVITY, F32)),
    )
    shift, lent_shift, state, row_sent, plane_sent = outs

    backs = [
        lax.ppermute(lent_shift, "slab", [(h ^ bit, h) for h in heavy]).reshape(
            3, share, rows, depth
        )
        for bit in units
    ]
    row_halo = shifted_back(row_sent, "ctrl").reshape(2, 3, planes, depth)
    plane_sent = plane_sent.reshape(2, 3, rows, depth)
    plane_halo = shifted_back(
        jnp.concatenate([plane_sent, row_halo[:, :, :1]], axis=2), "slab"
    )
    node_shift, volume, change = pl.pallas_call(
        functools.partial(volume_kernel, keep, share),
        out_shape=(
            jax.ShapeDtypeStruct(node_points.shape, F32),
            jax.ShapeDtypeStruct(node_points.shape[1:], F32),
            jax.ShapeDtypeStruct(node_points.shape[1:], F32),
        ),
        in_specs=[vmem()] * (4 + len(backs)),
        out_specs=(vmem(),) * 3,
        compiler_params=limited(8),
    )(node_points, shift.reshape(3, planes, rows, depth), row_halo, plane_halo, *backs)
    return node_shift, volume, change, state[0, : motion.shape[0]]


def solution(mesh):
    placed = (
        P(("slab", "ctrl")),
        P(None, ("slab", "ctrl")),
        P(None, ("slab", "ctrl")),
        P(),
        P(),
        P(None, ("slab", "ctrl")),
        P(None, ("slab", "ctrl")),
        P(None, "slab", "ctrl", None),
        P("slab", "ctrl", None),
        P("slab", "ctrl"),
    )
    return jax.shard_map(
        local,
        mesh=mesh,
        in_specs=placed,
        out_specs=(
            P(None, "slab", "ctrl", None),
            P("slab", "ctrl", None),
            P("slab", "ctrl", None),
            P(),
        ),
        check_vma=False,
    )
```

```python
import functools
import jax
import jax.numpy as jnp
from jax import lax
from jax.experimental import pallas as pl
from jax.experimental.pallas import tpu as pltpu
from jax.sharding import PartitionSpec as P

TILE = 128
TIME_STEP = 0.5
RADIUS = 4.0
GRAVITY = (0.0, 0.0, -0.5, 0.0, 0.0, 0.0)
ROWS = 24
FEATS = 32
UNROLL = 16
MIX = 48
TINY = 1e-30
F32 = jnp.float32
BF16 = jnp.bfloat16


def limited(mib):
    return pltpu.CompilerParams(vmem_limit_bytes=mib << 20)


def vmem():
    return pl.BlockSpec(memory_space=pltpu.VMEM)


def smem():
    return pl.BlockSpec(memory_space=pltpu.SMEM)


def swapped(value, slab_bit, ctrl_bit):
    slabs, ctrls = lax.axis_size("slab"), lax.axis_size("ctrl")
    pairs = [
        (s * ctrls + c, (s ^ slab_bit) * ctrls + (c ^ ctrl_bit))
        for s in range(slabs)
        for c in range(ctrls)
    ]
    return lax.ppermute(value, ("slab", "ctrl"), pairs)


def shifted_back(value, axis):
    return lax.ppermute(value, axis, [(i, i - 1) for i in range(1, lax.axis_size(axis))])


def load_rows(pressure, area, center):
    pushed = pressure * area

    def turned(value, by):
        return jnp.concatenate([value[by:3], value[0:by]], axis=0)

    moment = turned(center, 1) * turned(pushed, 2) - turned(center, 2) * turned(pushed, 1)
    sums = [jnp.sum(pushed, axis=1, keepdims=True), jnp.sum(moment, axis=1, keepdims=True)]
    lane = lax.broadcasted_iota(jnp.int32, (1, 128), 1)
    row = jnp.zeros((1, 128), F32)
    for k in range(6):
        row = jnp.where(lane == k, sums[k // 3][k % 3 : k % 3 + 1, :], row)
    return row


def pack_table(row, points, modes, out):
    for t in range(points.shape[1] // TILE):
        span = slice(t * TILE, (t + 1) * TILE)
        base = t * ROWS
        for c in range(3):
            out[base + 8 * c : base + 8 * c + 1, :] = points[c : c + 1, span]
            for k in range(6):
                at = base + 8 * c + 1 + k
                out[at : at + 1, :] = modes[3 * k + c : 3 * k + c + 1, span]
            at = base + 8 * c + 7
            out[at : at + 1, :] = row if (t == 0 and c == 0) else jnp.zeros((1, 128), F32)


def count_column(counts, x):
    rows = counts.shape[1]
    row = lax.broadcasted_iota(jnp.int32, (rows, rows), 0)
    lane = lax.broadcasted_iota(jnp.int32, (rows, rows), 1)
    many = jnp.broadcast_to(counts[x : x + 1, :].astype(F32), (rows, rows))
    return jnp.sum(jnp.where(row == lane, many, 0.0), axis=1, keepdims=True)


def pack_lent(planes, base, nodes, numbers, counts, out):
    rows, slots = numbers.shape[1:]
    lent = len(planes) * rows
    wide = lax.broadcasted_iota(jnp.int32, (rows, out.shape[1]), 1)
    for i, x in enumerate(planes):
        at = base + i * rows
        for c in range(3):
            first = (c * counts.shape[0] + x) * rows
            out[at + c * lent : at + c * lent + rows, :] = nodes[first : first + rows, :]
        at = at + 3 * lent
        out[at : at + rows, :] = jnp.where(wide == slots, count_column(counts, x), 0.0)
        out[at : at + rows, 0:slots] = numbers[x].astype(F32)


def pack_corner(nodes, numbers, counts, out):
    slots = numbers.shape[2]
    lane = lax.broadcasted_iota(jnp.int32, (1, out.shape[1]), 1)
    out[...] = jnp.zeros(out.shape, F32)
    for c in range(3):
        first = c * counts.shape[0] * counts.shape[1]
        out[c : c + 1, :] = nodes[first : first + 1, :]
    out[3:4, :] = jnp.where(lane == slots, count_column(counts, 0)[0:1], 0.0)
    out[3:4, 0:slots] = numbers[0, 0:1, :].astype(F32)


def pack_kernel(
    spans, pressure, area, center, points, modes, nodes, numbers, counts, corner, out, *lents
):
    row = load_rows(pressure[...], area[...], center[...])
    pack_table(row, points, modes, out)
    pack_corner(nodes, numbers, counts, corner)
    if spans:
        pack_lent(spans[0], points.shape[1] // TILE * ROWS, nodes, numbers, counts, out)
    for span, lent in zip(spans[1:], lents):
        pack_lent(span, 0, nodes, numbers, counts, lent)


def lend_kernel(spans, nodes, numbers, counts, corner, *outs):
    pack_corner(nodes, numbers, counts, corner)
    for span, out in zip(spans, outs):
        pack_lent(span, 0, nodes, numbers, counts, out)


def loads_kernel(pressure, area, center, out):
    out[...] = load_rows(pressure[...], area[...], center[...])


def split3(value):
    first = value.astype(BF16).astype(F32)
    rest = value - first
    second = rest.astype(BF16).astype(F32)
    return first, second, rest - second


def spread(ref, at):
    return jnp.broadcast_to(ref[pl.ds(at, 1), :], (8, ref.shape[1]))


def products(rows, scale, order, ends):
    row = lax.broadcasted_iota(jnp.int32, rows[0].shape, 0)
    norm = jnp.zeros(rows[0].shape, F32)
    blocks = []
    for value in rows:
        place = value * (1.0 / RADIUS)
        norm = norm + place * place
        first, second, third = split3(place * scale)
        low = jnp.where((row & 1) == 1, order[1](first, second, third, row), order[0](first, second, third, row))
        blocks.append(low)
    first, second, third = split3(norm)
    blocks.append(ends(first, second, third, row))
    return jnp.concatenate(blocks, axis=0)


def tile_block(rows):
    return products(
        rows,
        -2.0,
        (
            lambda a, b, c, row: jnp.where((row == 2) | (row == 6), b, a),
            lambda a, b, c, row: jnp.where(row == 1, a, jnp.where(row == 3, b, c)),
        ),
        lambda a, b, c, row: jnp.where(
            row == 0, a, jnp.where(row == 1, b, jnp.where(row == 2, c, jnp.where(row < 6, 1.0, 0.0)))
        ),
    )


def line_block(rows):
    return products(
        rows,
        1.0,
        (
            lambda a, b, c, row: jnp.where(row < 4, a, c),
            lambda a, b, c, row: jnp.where(row == 5, a, b),
        ),
        lambda a, b, c, row: jnp.where(
            row < 3, 1.0, jnp.where(row == 3, a, jnp.where(row == 4, b, jnp.where(row == 5, c, 0.0)))
        ),
    )


def build_lists(lines, slots, bits, first, listed, items):
    few = min(4, slots)
    middle = lines * slots + 2 * UNROLL

    def take(line, low, high, ends):
        end_a, end_b = ends
        found = [listed[line, e] for e in range(low, high)]
        live = [1 + lax.shift_right_arithmetic(code, 31) for code in found]
        late = [n & lax.shift_right_logical(code, bits - 1) for n, code in zip(live, found)]
        for code, n, m in zip(found, live, late):
            items[end_a] = code
            items[end_b] = code
            end_a, end_b = end_a + (n - m), end_b + m
        return end_a, end_b

    def one(line, ends):
        ends = take(line, 0, few, ends)
        return lax.cond(
            listed[line, slots] > few,
            lambda ends: take(line, few, slots, ends),
            lambda ends: ends,
            ends,
        )

    end_a, end_b = lax.fori_loop(0, lines, one, (jnp.int32(0), jnp.int32(middle)))
    dummy = (first + lines) << bits
    for e in range(2 * UNROLL):
        items[end_a + e] = dummy
        items[end_b + e] = dummy
    items[2 * middle] = end_a
    items[2 * middle + 1] = end_b - middle


def line_features(lines, points, line_feat):
    def block(l, carry):
        rows = [spread(points, c * lines + l) for c in range(3)]
        at = pl.ds(pl.multiple_of(l * FEATS, FEATS), FEATS)
        line_feat[at, :] = line_block(rows).astype(BF16)
        return carry

    lax.fori_loop(0, lines, block, 0, unroll=4)


def coded(first, bits, placed, number, count):
    row = lax.broadcasted_iota(jnp.int32, number.shape, 0)
    slot = lax.broadcasted_iota(jnp.int32, number.shape, 1)
    code = lax.shift_left(row + first, jnp.full_like(row, bits)) + placed(number)
    return jnp.where(slot < count, code, -1)


def own_kernel(
    keep, bits, placed, span, points, numbers, counts,
    items, line_feat, sent, codes, listed, sem,
):
    planes, rows, slots = numbers.shape
    pack_lent(span, 0, points, numbers, counts, sent)
    slabs = lax.axis_size("slab")
    lends = is_heavy(lax.axis_index("slab"), slabs)
    for x in range(planes):
        count = count_column(counts, x).astype(jnp.int32)
        if x >= keep:
            row = lax.broadcasted_iota(jnp.int32, count.shape, 0)
            count = jnp.where(lends & (row >= 1), 0, count)
        span = slice(x * rows, (x + 1) * rows)
        codes[span, 0:slots] = coded(x * rows, bits, placed, numbers[x], count)
        codes[span, slots : slots + 1] = count
    copy = pltpu.make_async_copy(codes, listed, sem)
    copy.start()
    line_features(planes * rows, points, line_feat)
    copy.wait()
    build_lists(planes * rows, slots, bits, 0, listed, items)


def lent_kernel(
    first, rows, slots, lent, bits, placed, units, bases, *refs
):
    gots, refs = refs[: len(units)], refs[len(units) :]
    corner, items, line_feat, codes, listed, got, sem = refs
    slab, slabs = lax.axis_index("slab"), lax.axis_size("slab")
    value = gots[-1][pl.ds(bases[-1], 4 * lent), :]
    for unit, base, ref in list(zip(units, bases, gots))[:-1]:
        value = jnp.where(is_heavy(slab ^ unit, slabs), ref[pl.ds(base, 4 * lent), :], value)
    got[...] = value
    for c in range(4):
        got[c * lent : c * lent + 1, :] = corner[c : c + 1, :]
    helps = jnp.logical_not(is_heavy(slab, slabs))
    number = got[3 * lent :, 0:slots].astype(jnp.int32)
    count = got[3 * lent :, slots : slots + 1].astype(jnp.int32)
    line = lax.broadcasted_iota(jnp.int32, count.shape, 0)
    count = jnp.where((helps & (lax.rem(line, rows) >= 1)) | (line == 0), count, 0)
    codes[:, 0:slots] = coded(first, bits, placed, number, count)
    codes[:, slots : slots + 1] = count
    copy = pltpu.make_async_copy(codes, listed, sem)
    copy.start()
    line_features(lent, got, line_feat)
    copy.wait()
    build_lists(lent, slots, bits, first, listed, items)


def prepared(kernel, lines, slots, depth, more, scratch, *operands):
    length = lines * slots + 2 * UNROLL
    return pl.pallas_call(
        kernel,
        out_shape=(
            jax.ShapeDtypeStruct((2 * length + 2,), jnp.int32),
            jax.ShapeDtypeStruct((lines * FEATS, depth), BF16),
            *more,
        ),
        in_specs=[vmem()] * len(operands),
        out_specs=(smem(), vmem()) + (vmem(),) * len(more),
        scratch_shapes=[
            pltpu.VMEM((lines, TILE), jnp.int32),
            pltpu.SMEM((lines, TILE), jnp.int32),
        ]
        + scratch
        + [pltpu.SemaphoreType.DMA],
        compiler_params=limited(4),
        cost_estimate=pl.CostEstimate(flops=0, bytes_accessed=8_000_000, transcendentals=0),
    )(*operands)


def add_items(bits, half, lists, table, feats, line_feat, tile_feat, modes, acc, squares):
    tiles = table.shape[0] // ROWS
    at = 0
    for feat in feats:
        line_feat[at : at + feat.shape[0], :] = feat[...]
        at += feat.shape[0]
    line_feat[at:, :] = jnp.zeros((line_feat.shape[0] - at, line_feat.shape[1]), BF16)
    middles = [items.shape[0] // 2 - 1 for items in lists]
    starts = [middle * half for middle in middles]
    first = lists[0][2 * middles[0] + half]
    count = sum(items[2 * middle + half] for items, middle in zip(lists, middles))

    def build(t, carry):
        base = pl.multiple_of(t * ROWS, 8)
        rows = [spread(table, base + 8 * c) for c in range(3)]
        block = tile_block(rows)
        tile_feat[pl.ds(pl.multiple_of(t * TILE, TILE), TILE), :] = block.astype(BF16).T
        value = 4.0 * table[pl.ds(base, ROWS), :]
        high = value.astype(BF16)
        low = (value - high.astype(F32)).astype(BF16)
        at = pl.ds(pl.multiple_of(t * MIX, 16), MIX)
        modes[at, :] = jnp.concatenate([high, low], axis=0)
        return carry

    lax.fori_loop(0, tiles, build, 0, unroll=4)
    mask = tiles - 1

    def unpack(at):
        code = lists[0][starts[0] + jnp.minimum(at, first)]
        other = lists[1][starts[1] + jnp.maximum(at - first, 0)]
        code = jnp.where(at < first, code, other)
        return lax.shift_right_logical(code, bits), code & mask

    def distances(u, at):
        line, tile = unpack(at)
        squares[u][...] = jnp.dot(
            tile_feat[pl.ds(pl.multiple_of(tile * TILE, TILE), TILE), :],
            line_feat[pl.ds(pl.multiple_of(line * FEATS, FEATS), FEATS), :],
            preferred_element_type=F32,
        )

    def gather(u, at):
        line, tile = unpack(at)
        square = jnp.maximum(squares[u][...], TINY)
        near = jnp.maximum(1.0 - square * lax.rsqrt(square), 0.0)
        fourth = near * near
        fourth = fourth * fourth
        phi = fourth * (1.25 - near)
        high = phi.astype(BF16)
        low = (phi - high.astype(F32)).astype(BF16)
        mode = modes[pl.ds(pl.multiple_of(tile * MIX, 16), MIX), :]
        got = jnp.dot(
            jnp.concatenate([mode, mode], axis=1),
            jnp.concatenate([high, low], axis=0),
            preferred_element_type=F32,
        )
        where = pl.ds(pl.multiple_of(line * ROWS, 8), ROWS)
        acc[where, :] = acc[where, :] + (got[0:ROWS] + got[ROWS:MIX])

    def body(j, carry):
        base = j * UNROLL
        for u in range(UNROLL):
            gather(u, base + u)
            distances(u, base + UNROLL + u)
        return carry

    for u in range(UNROLL):
        distances(u, u)
    lax.fori_loop(0, lax.div(count + (UNROLL - 1), jnp.int32(UNROLL)), body, 0)


def load_sum(table):
    tiles = table.shape[0] // ROWS
    return jnp.sum(table[pl.ds(7, tiles, stride=ROWS), :], axis=0, keepdims=True)


def early_kernel(parts, bits, *refs):
    lists, feats = refs[:parts], refs[parts : 2 * parts]
    table, acc, loads, line_feat, tile_feat, modes, *squares = refs[2 * parts :]
    acc[...] = jnp.zeros(acc.shape, F32)
    loads[...] = load_sum(table)
    add_items(bits, 0, lists, table, feats, line_feat, tile_feat, modes, acc, squares)


def late_kernel(own, lent, parts, bits, *refs):
    lists, feats = refs[:parts], refs[parts : 2 * parts]
    table, early, loads, points, corner, motion, inverse, *rest = refs[2 * parts :]
    out_own, out_extra, out_state, out_row, out_plane, *rest = rest
    line_feat, tile_feat, modes, acc, *squares = rest
    total = loads[...] + load_sum(table)
    lane = lax.broadcasted_iota(jnp.int32, (1, 128), 1)
    gravity = jnp.zeros((1, 128), F32)
    for k, pull in enumerate(GRAVITY):
        gravity = jnp.where(lane == k, pull, gravity)
    acceleration = inverse[...] * total + gravity
    out_state[...] = motion[...] + TIME_STEP * acceleration
    step = TIME_STEP * motion[...] + 0.5 * TIME_STEP * TIME_STEP * acceleration
    row = lax.broadcasted_iota(jnp.int32, (8, 128), 0)
    lane = lax.broadcasted_iota(jnp.int32, (8, 128), 1)
    chosen = jnp.where((lane == row - 1) & (lane < 6), jnp.broadcast_to(step, (8, 128)), 0.0)
    weight = jnp.broadcast_to(jnp.sum(chosen, axis=1, keepdims=True), (8, 128))

    acc[...] = early[...]
    add_items(bits, 1, lists, table, feats, line_feat, tile_feat, modes, acc, squares)

    def finish(count, first, out):
        def one(l, carry):
            base = pl.multiple_of((first + l) * ROWS, 8)
            for c in range(3):
                value = jnp.sum(weight * acc[pl.ds(base + 8 * c, 8), :], axis=0, keepdims=True)
                out[pl.ds(c * count + l, 1), :] = value
            return carry

        lax.fori_loop(0, count, one, 0, unroll=4)

    finish(own, 0, out_own)
    finish(lent, own, out_extra)
    rows = out_row.shape[1] // 3
    wide = own // rows
    for c in range(3):
        old = points[c * own : c * own + wide, :]
        out_plane[0, c * wide : (c + 1) * wide, :] = old
        out_plane[1, c * wide : (c + 1) * wide, :] = old + out_own[c * own : c * own + wide, :]
        old = points[pl.ds(c * own, rows, stride=wide), :]
        out_row[0, c * rows : (c + 1) * rows, :] = old
        out_row[1, c * rows : (c + 1) * rows, :] = (
            old + out_own[pl.ds(c * own, rows, stride=wide), :]
        )
    out_plane[0, 3 * wide :, :] = corner[...]
    out_plane[1, 3 * wide :, :] = corner[...]
    for c in range(3):
        at = slice(3 * wide + c, 3 * wide + c + 1)
        out_plane[1, at, :] = corner[c : c + 1, :] + out_extra[c * lent : c * lent + 1, :]


def volume_kernel(
    keep, share, points, shift, *refs
):
    *backs, plane_halo, row_halo, out_shift, out_volume, out_change = refs
    planes, rows, depth = points.shape[1:]
    slab, ctrl = lax.axis_index("slab"), lax.axis_index("ctrl")
    slabs, ctrls = lax.axis_size("slab"), lax.axis_size("ctrl")
    row_id = lax.broadcasted_iota(jnp.int32, (rows, depth), 0)
    lane = lax.broadcasted_iota(jnp.int32, (rows, depth), 1)
    inside = (lane < depth - 1) & (row_id + ctrl * rows < ctrls * rows - 1)
    if backs:
        from_helper = (row_id >= 1) & is_heavy(slab, slabs)
    last_row = row_id == rows - 1

    def next_row(value, edge):
        return jnp.where(last_row, edge, pltpu.roll(value, rows - 1, 0))

    def next_depth(value):
        return pltpu.roll(value, depth - 1, 1)

    def level(x):
        found = []
        for field in range(2):
            parts = []
            for c in range(3):
                if x == planes:
                    here = plane_halo[field, c * rows : (c + 1) * rows, :]
                    edge = plane_halo[field, 3 * rows + c : 3 * rows + c + 1, :]
                else:
                    here = points[c, x]
                    if field == 1:
                        moved = shift[c, x]
                        if backs and x >= keep:
                            back = backs[(x - keep) // share]
                            moved = jnp.where(from_helper, back[c, (x - keep) % share], moved)
                        out_shift[c, x] = moved
                        here = here + moved
                    edge = row_halo[field, c, x : x + 1, :]
                there = next_row(here, edge)
                parts.append((here + there, there - here))
            found.append(parts)
        return found

    before = level(0)
    for x in range(planes):
        after = level(x + 1)
        volumes = []
        for field in range(2):
            edges = []
            for c in range(3):
                both0, step0 = before[field][c]
                both1, step1 = after[field][c]
                along, across, total = both1 - both0, step0 + step1, both0 + both1
                edges.append(
                    (
                        0.25 * (along + next_depth(along)),
                        0.25 * (across + next_depth(across)),
                        0.25 * (next_depth(total) - total),
                    )
                )
            ex, ey, ez = zip(*edges)
            volumes.append(
                ex[0] * (ey[1] * ez[2] - ey[2] * ez[1])
                + ex[1] * (ey[2] * ez[0] - ey[0] * ez[2])
                + ex[2] * (ey[0] * ez[1] - ey[1] * ez[0])
            )
        live = inside & (slab * planes + x < slabs * planes - 1)
        out_volume[x] = jnp.where(live, volumes[1], 0.0)
        out_change[x] = jnp.where(live, volumes[1] - volumes[0], 0.0)
        before = after


def is_heavy(slab, slabs):
    return (8 * slab >= 3 * slabs) & (8 * slab < 5 * slabs)


def local(
    face_pressure,
    face_area,
    face_center,
    motion,
    inverse_mass,
    control_points,
    control_modes,
    node_points,
    tile_list,
    tile_count,
):
    slabs, ctrls = lax.axis_size("slab"), lax.axis_size("ctrl")
    slab, ctrl = lax.axis_index("slab"), lax.axis_index("ctrl")
    _, planes, rows, depth = node_points.shape
    slots = tile_list.shape[2]
    own = planes * rows
    columns = control_points.shape[1]
    tiles = columns * slabs * ctrls // TILE
    bits = max(1, (tiles - 1).bit_length())
    pressure = face_pressure.reshape(1, -1)

    unit = slabs // 8
    share = (planes - 1) // 3
    keep = planes - 3 * share
    lend = slabs % 8 == 0 and slabs & (slabs - 1) == 0 and share > 0
    assert lend, (slabs, planes)
    units = (4 * unit, 2 * unit, unit) if lend else ()
    spans = [tuple(range(keep + g * share, keep + (g + 1) * share)) for g in range(len(units))]
    lent = share * rows if lend else 0
    heavy = [s for s in range(slabs) if is_heavy(s, slabs)]

    direct = columns % TILE == 0 and slabs & (slabs - 1) == 0 and ctrls & (ctrls - 1) == 0
    direct = direct and ctrls > 1 and (columns // TILE) & (columns // TILE - 1) == 0
    own_tiles = columns // TILE
    order = []
    bit = slabs // 2
    while bit:
        order.append((bit, 0))
        bit //= 2
    bit = 1
    while bit < ctrls:
        order.append((0, bit))
        bit *= 2

    def placed(number):
        if not direct:
            return number
        device = lax.axis_index("slab") * ctrls + lax.axis_index("ctrl")
        apart = (number >> (own_tiles.bit_length() - 1)) ^ device
        at = jnp.zeros(number.shape, jnp.int32)
        for turn, (slab_bit, ctrl_bit) in enumerate(order):
            flag = slab_bit * ctrls + ctrl_bit
            at = at + jnp.where((apart & flag) != 0, own_tiles << turn, 0)
        return at + (number & (own_tiles - 1))

    flat_points = node_points.reshape(3 * own, depth)
    *own_lists, last_sent = prepared(
        functools.partial(own_kernel, keep, bits, placed, spans[-1]),
        own, slots, depth, [jax.ShapeDtypeStruct((4 * lent, TILE), F32)], [],
        flat_points, tile_list, tile_count,
    )

    def borrowed(gots, bases):
        kernel = functools.partial(
            lent_kernel, own, rows, slots, lent, bits, placed, units, tuple(bases)
        )
        scratch = [pltpu.VMEM((4 * lent, TILE), F32)]
        return prepared(kernel, lent, slots, depth, [], scratch, *gots, corner)

    gots, bases = [], []
    if direct:
        size = own_tiles * ROWS
        corner, first, *sents = pl.pallas_call(
            functools.partial(pack_kernel, spans[:-1]),
            out_shape=[
                jax.ShapeDtypeStruct((rows_of, TILE), F32)
                for rows_of in [8, size + 4 * lent] + [4 * lent] * (len(units) - 2)
            ],
            in_specs=[vmem()] * 8,
            out_specs=[vmem()] * len(units),
            compiler_params=limited(56),
        )(
            pressure, face_area, face_center, control_points, control_modes,
            flat_points, tile_list, tile_count,
        )
        sents.append(last_sent)
        early = first[:size]
        corner = shifted_back(corner, "ctrl")
        for turn, (slab_bit, ctrl_bit) in enumerate(order[:-1]):
            size = early.shape[0]
            if turn == 2:
                early, own_lists, sents[-1] = lax.optimization_barrier(
                    (early, own_lists, sents[-1])
                )
            if turn == 3:
                early, lent_lists = lax.optimization_barrier((early, lent_lists))
            if lend and slab_bit in units:
                payload = jnp.concatenate([early, sents[len(gots) - 1]], axis=0) if gots else first
                reply = swapped(payload, slab_bit, ctrl_bit)
                gots.append(reply)
                bases.append(size)
                reply = reply[:size]
                if len(gots) == len(units):
                    lent_lists = borrowed(gots, bases)
            else:
                reply = swapped(early, slab_bit, ctrl_bit)
            early = jnp.concatenate([early, reply], axis=0)
        late = swapped(early, *order[-1])
    else:
        loads = pl.pallas_call(
            loads_kernel,
            out_shape=jax.ShapeDtypeStruct((1, TILE), F32),
            in_specs=[vmem()] * 3,
            out_specs=vmem(),
        )(pressure, face_area, face_center)
        loads = lax.psum(loads, ("slab", "ctrl"))
        whole = jnp.concatenate([control_points, control_modes], axis=0)
        whole = lax.all_gather(whole, ("slab", "ctrl"), axis=1, tiled=True)
        whole = whole.reshape(7, 3, tiles, TILE).transpose(2, 1, 0, 3)
        spare = jnp.zeros((tiles, 3, 1, TILE), F32).at[0, 0, 0, :].set(loads[0])
        table = jnp.concatenate([whole, spare], axis=2).reshape(tiles * ROWS, TILE)
        early, late = table[: tiles // 2 * ROWS], table[tiles // 2 * ROWS :]
        corner, *sents = pl.pallas_call(
            functools.partial(lend_kernel, spans),
            out_shape=[jax.ShapeDtypeStruct((8, TILE), F32)]
            + [jax.ShapeDtypeStruct((4 * lent, TILE), F32)] * len(units),
            in_specs=[vmem()] * 3,
            out_specs=[vmem()] * (1 + len(units)),
        )(flat_points, tile_list, tile_count)
        corner = shifted_back(corner, "ctrl")
        gots = [swapped(sent, bit, 0) for sent, bit in zip(sents, units)]
        lent_lists = borrowed(gots, [0] * len(units))
    groups = [own_lists, lent_lists]
    lines = own + lent

    def wide(value):
        return jnp.pad(value, (0, TILE - value.shape[0])).reshape(1, TILE)

    half = tiles // 2
    parts = len(groups)
    lists = [group[0] for group in groups]
    feats = [group[1] for group in groups]
    list_specs = [smem()] * parts + [vmem()] * parts
    scratch = [
        pltpu.VMEM(((lines + 1) * FEATS, depth), BF16),
        pltpu.VMEM((half * TILE, FEATS), BF16),
        pltpu.VMEM((half * MIX, TILE), BF16),
    ]
    squares = [pltpu.VMEM((TILE, depth), F32)] * UNROLL
    partial, part_loads = pl.pallas_call(
        functools.partial(early_kernel, parts, bits),
        out_shape=(
            jax.ShapeDtypeStruct(((lines + 1) * ROWS, depth), F32),
            jax.ShapeDtypeStruct((1, TILE), F32),
        ),
        in_specs=list_specs + [vmem()],
        out_specs=(vmem(), vmem()),
        scratch_shapes=scratch + squares,
        compiler_params=limited(16),
        cost_estimate=pl.CostEstimate(flops=0, bytes_accessed=30_000_000, transcendentals=0),
    )(*lists, *feats, early)
    outs = pl.pallas_call(
        functools.partial(late_kernel, own, lent, parts, bits),
        out_shape=(
            jax.ShapeDtypeStruct((3 * own, depth), F32),
            jax.ShapeDtypeStruct((3 * max(lent, 8), depth), F32),
            jax.ShapeDtypeStruct((1, TILE), F32),
            jax.ShapeDtypeStruct((2, 3 * planes, depth), F32),
            jax.ShapeDtypeStruct((2, 3 * rows + 8, depth), F32),
        ),
        in_specs=list_specs + [vmem()] * 7,
        out_specs=(vmem(),) * 5,
        scratch_shapes=scratch + [pltpu.VMEM(((lines + 1) * ROWS, depth), F32)] + squares,
        compiler_params=limited(16),
    )(
        *lists, *feats, late, partial, part_loads, flat_points, corner,
        wide(motion), wide(inverse_mass),
    )
    shift, lent_shift, state, row_sent, plane_sent = outs

    backs = [
        lax.ppermute(lent_shift, "slab", [(h ^ bit, h) for h in heavy]).reshape(
            3, share, rows, depth
        )
        for bit in units
    ]
    plane_halo = shifted_back(plane_sent, "slab")
    row_halo = shifted_back(row_sent, "ctrl").reshape(2, 3, planes, depth)
    node_shift, volume, change = pl.pallas_call(
        functools.partial(volume_kernel, keep, share),
        out_shape=(
            jax.ShapeDtypeStruct(node_points.shape, F32),
            jax.ShapeDtypeStruct(node_points.shape[1:], F32),
            jax.ShapeDtypeStruct(node_points.shape[1:], F32),
        ),
        in_specs=[vmem()] * (4 + len(backs)),
        out_specs=(vmem(),) * 3,
        compiler_params=limited(8),
    )(node_points, shift.reshape(3, planes, rows, depth), *backs, plane_halo, row_halo)
    return node_shift, volume, change, state[0, : motion.shape[0]]


def solution(mesh):
    placed = (
        P(("slab", "ctrl")),
        P(None, ("slab", "ctrl")),
        P(None, ("slab", "ctrl")),
        P(),
        P(),
        P(None, ("slab", "ctrl")),
        P(None, ("slab", "ctrl")),
        P(None, "slab", "ctrl", None),
        P("slab", "ctrl", None),
        P("slab", "ctrl"),
    )
    return jax.shard_map(
        local,
        mesh=mesh,
        in_specs=placed,
        out_specs=(
            P(None, "slab", "ctrl", None),
            P("slab", "ctrl", None),
            P("slab", "ctrl", None),
            P(),
        ),
        check_vma=False,
    )
```

```python
import functools
import jax
import jax.numpy as jnp
from jax import lax
from jax.experimental import pallas as pl
from jax.experimental.pallas import tpu as pltpu
from jax.sharding import PartitionSpec as P

TILE = 128
TIME_STEP = 0.5
RADIUS = 4.0
GRAVITY = (0.0, 0.0, -0.5, 0.0, 0.0, 0.0)
ROWS = 24
FEATS = 32
UNROLL = 16
MIX = 48
TINY = 1e-30
F32 = jnp.float32
BF16 = jnp.bfloat16


def limited(mib):
    return pltpu.CompilerParams(vmem_limit_bytes=mib << 20)


def vmem():
    return pl.BlockSpec(memory_space=pltpu.VMEM)


def smem():
    return pl.BlockSpec(memory_space=pltpu.SMEM)


def swapped(value, slab_bit, ctrl_bit):
    slabs, ctrls = lax.axis_size("slab"), lax.axis_size("ctrl")
    pairs = [
        (s * ctrls + c, (s ^ slab_bit) * ctrls + (c ^ ctrl_bit))
        for s in range(slabs)
        for c in range(ctrls)
    ]
    return lax.ppermute(value, ("slab", "ctrl"), pairs)


def shifted_back(value, axis):
    return lax.ppermute(value, axis, [(i, i - 1) for i in range(1, lax.axis_size(axis))])


def load_rows(pressure, area, center):
    pushed = pressure * area

    def turned(value, by):
        return jnp.concatenate([value[by:3], value[0:by]], axis=0)

    moment = turned(center, 1) * turned(pushed, 2) - turned(center, 2) * turned(pushed, 1)
    sums = [jnp.sum(pushed, axis=1, keepdims=True), jnp.sum(moment, axis=1, keepdims=True)]
    lane = lax.broadcasted_iota(jnp.int32, (1, 128), 1)
    row = jnp.zeros((1, 128), F32)
    for k in range(6):
        row = jnp.where(lane == k, sums[k // 3][k % 3 : k % 3 + 1, :], row)
    return row


def pack_table(row, points, modes, out):
    for t in range(points.shape[1] // TILE):
        span = slice(t * TILE, (t + 1) * TILE)
        base = t * ROWS
        for c in range(3):
            out[base + 8 * c : base + 8 * c + 1, :] = points[c : c + 1, span]
            for k in range(6):
                at = base + 8 * c + 1 + k
                out[at : at + 1, :] = modes[3 * k + c : 3 * k + c + 1, span]
            at = base + 8 * c + 7
            out[at : at + 1, :] = row if (t == 0 and c == 0) else jnp.zeros((1, 128), F32)


def count_column(counts, x):
    rows = counts.shape[1]
    row = lax.broadcasted_iota(jnp.int32, (rows, rows), 0)
    lane = lax.broadcasted_iota(jnp.int32, (rows, rows), 1)
    many = jnp.broadcast_to(counts[x : x + 1, :].astype(F32), (rows, rows))
    return jnp.sum(jnp.where(row == lane, many, 0.0), axis=1, keepdims=True)


def pack_lent(planes, base, nodes, numbers, counts, out):
    rows, slots = numbers.shape[1:]
    lent = len(planes) * rows
    wide = lax.broadcasted_iota(jnp.int32, (rows, out.shape[1]), 1)
    for i, x in enumerate(planes):
        at = base + i * rows
        for c in range(3):
            first = (c * counts.shape[0] + x) * rows
            out[at + c * lent : at + c * lent + rows, :] = nodes[first : first + rows, :]
        at = at + 3 * lent
        out[at : at + rows, :] = jnp.where(wide == slots, count_column(counts, x), 0.0)
        out[at : at + rows, 0:slots] = numbers[x].astype(F32)


def pack_corner(nodes, numbers, counts, out):
    slots = numbers.shape[2]
    lane = lax.broadcasted_iota(jnp.int32, (1, out.shape[1]), 1)
    out[...] = jnp.zeros(out.shape, F32)
    for c in range(3):
        first = c * counts.shape[0] * counts.shape[1]
        out[c : c + 1, :] = nodes[first : first + 1, :]
    out[3:4, :] = jnp.where(lane == slots, count_column(counts, 0)[0:1], 0.0)
    out[3:4, 0:slots] = numbers[0, 0:1, :].astype(F32)


def pack_kernel(
    spans, pressure, area, center, points, modes, nodes, numbers, counts, corner, out, *lents
):
    row = load_rows(pressure[...], area[...], center[...])
    pack_table(row, points, modes, out)
    pack_corner(nodes, numbers, counts, corner)
    if spans:
        pack_lent(spans[0], points.shape[1] // TILE * ROWS, nodes, numbers, counts, out)
    for span, lent in zip(spans[1:], lents):
        pack_lent(span, 0, nodes, numbers, counts, lent)


def lend_kernel(spans, nodes, numbers, counts, corner, *outs):
    pack_corner(nodes, numbers, counts, corner)
    for span, out in zip(spans, outs):
        pack_lent(span, 0, nodes, numbers, counts, out)


def loads_kernel(pressure, area, center, out):
    out[...] = load_rows(pressure[...], area[...], center[...])


def split3(value):
    first = value.astype(BF16).astype(F32)
    rest = value - first
    second = rest.astype(BF16).astype(F32)
    return first, second, rest - second


def spread(ref, at):
    return jnp.broadcast_to(ref[pl.ds(at, 1), :], (8, ref.shape[1]))


def products(rows, scale, order, ends):
    row = lax.broadcasted_iota(jnp.int32, rows[0].shape, 0)
    norm = jnp.zeros(rows[0].shape, F32)
    blocks = []
    for value in rows:
        place = value * (1.0 / RADIUS)
        norm = norm + place * place
        first, second, third = split3(place * scale)
        low = jnp.where((row & 1) == 1, order[1](first, second, third, row), order[0](first, second, third, row))
        blocks.append(low)
    first, second, third = split3(norm)
    blocks.append(ends(first, second, third, row))
    return jnp.concatenate(blocks, axis=0)


def tile_block(rows):
    return products(
        rows,
        -2.0,
        (
            lambda a, b, c, row: jnp.where((row == 2) | (row == 6), b, a),
            lambda a, b, c, row: jnp.where(row == 1, a, jnp.where(row == 3, b, c)),
        ),
        lambda a, b, c, row: jnp.where(
            row == 0, a, jnp.where(row == 1, b, jnp.where(row == 2, c, jnp.where(row < 6, 1.0, 0.0)))
        ),
    )


def line_block(rows):
    return products(
        rows,
        1.0,
        (
            lambda a, b, c, row: jnp.where(row < 4, a, c),
            lambda a, b, c, row: jnp.where(row == 5, a, b),
        ),
        lambda a, b, c, row: jnp.where(
            row < 3, 1.0, jnp.where(row == 3, a, jnp.where(row == 4, b, jnp.where(row == 5, c, 0.0)))
        ),
    )


def build_lists(lines, slots, bits, first, listed, items):
    few = min(4, slots)
    middle = lines * slots + 2 * UNROLL

    def take(line, low, high, ends):
        end_a, end_b = ends
        found = [listed[line, e] for e in range(low, high)]
        live = [1 + lax.shift_right_arithmetic(code, 31) for code in found]
        late = [n & lax.shift_right_logical(code, bits - 1) for n, code in zip(live, found)]
        for code, n, m in zip(found, live, late):
            items[end_a] = code
            items[end_b] = code
            end_a, end_b = end_a + (n - m), end_b + m
        return end_a, end_b

    def one(line, ends):
        ends = take(line, 0, few, ends)
        return lax.cond(
            listed[line, slots] > few,
            lambda ends: take(line, few, slots, ends),
            lambda ends: ends,
            ends,
        )

    end_a, end_b = lax.fori_loop(0, lines, one, (jnp.int32(0), jnp.int32(middle)))
    dummy = (first + lines) << bits
    for e in range(2 * UNROLL):
        items[end_a + e] = dummy
        items[end_b + e] = dummy
    items[2 * middle] = end_a
    items[2 * middle + 1] = end_b - middle


def line_features(lines, points, line_feat):
    def block(l, carry):
        rows = [spread(points, c * lines + l) for c in range(3)]
        at = pl.ds(pl.multiple_of(l * FEATS, FEATS), FEATS)
        line_feat[at, :] = line_block(rows).astype(BF16)
        return carry

    lax.fori_loop(0, lines, block, 0, unroll=4)


def coded(first, bits, placed, number, count):
    row = lax.broadcasted_iota(jnp.int32, number.shape, 0)
    slot = lax.broadcasted_iota(jnp.int32, number.shape, 1)
    code = lax.shift_left(row + first, jnp.full_like(row, bits)) + placed(number)
    return jnp.where(slot < count, code, -1)


def own_kernel(
    keep, bits, placed, span, points, numbers, counts,
    items, line_feat, sent, codes, listed, sem,
):
    planes, rows, slots = numbers.shape
    pack_lent(span, 0, points, numbers, counts, sent)
    slabs = lax.axis_size("slab")
    lends = is_heavy(lax.axis_index("slab"), slabs)
    for x in range(planes):
        count = count_column(counts, x).astype(jnp.int32)
        if x >= keep:
            row = lax.broadcasted_iota(jnp.int32, count.shape, 0)
            count = jnp.where(lends & (row >= 1), 0, count)
        span = slice(x * rows, (x + 1) * rows)
        codes[span, 0:slots] = coded(x * rows, bits, placed, numbers[x], count)
        codes[span, slots : slots + 1] = count
    copy = pltpu.make_async_copy(codes, listed, sem)
    copy.start()
    line_features(planes * rows, points, line_feat)
    copy.wait()
    build_lists(planes * rows, slots, bits, 0, listed, items)


def lent_kernel(
    first, rows, slots, lent, bits, placed, units, bases, *refs
):
    gots, refs = refs[: len(units)], refs[len(units) :]
    corner, items, line_feat, codes, listed, got, sem = refs
    slab, slabs = lax.axis_index("slab"), lax.axis_size("slab")
    value = gots[-1][pl.ds(bases[-1], 4 * lent), :]
    for unit, base, ref in list(zip(units, bases, gots))[:-1]:
        value = jnp.where(is_heavy(slab ^ unit, slabs), ref[pl.ds(base, 4 * lent), :], value)
    got[...] = value
    for c in range(4):
        got[c * lent : c * lent + 1, :] = corner[c : c + 1, :]
    helps = jnp.logical_not(is_heavy(slab, slabs))
    number = got[3 * lent :, 0:slots].astype(jnp.int32)
    count = got[3 * lent :, slots : slots + 1].astype(jnp.int32)
    line = lax.broadcasted_iota(jnp.int32, count.shape, 0)
    count = jnp.where((helps & (lax.rem(line, rows) >= 1)) | (line == 0), count, 0)
    codes[:, 0:slots] = coded(first, bits, placed, number, count)
    codes[:, slots : slots + 1] = count
    copy = pltpu.make_async_copy(codes, listed, sem)
    copy.start()
    line_features(lent, got, line_feat)
    copy.wait()
    build_lists(lent, slots, bits, first, listed, items)


def prepared(kernel, lines, slots, depth, more, scratch, *operands):
    length = lines * slots + 2 * UNROLL
    return pl.pallas_call(
        kernel,
        out_shape=(
            jax.ShapeDtypeStruct((2 * length + 2,), jnp.int32),
            jax.ShapeDtypeStruct((lines * FEATS, depth), BF16),
            *more,
        ),
        in_specs=[vmem()] * len(operands),
        out_specs=(smem(), vmem()) + (vmem(),) * len(more),
        scratch_shapes=[
            pltpu.VMEM((lines, TILE), jnp.int32),
            pltpu.SMEM((lines, TILE), jnp.int32),
        ]
        + scratch
        + [pltpu.SemaphoreType.DMA],
        compiler_params=limited(4),
        cost_estimate=pl.CostEstimate(flops=0, bytes_accessed=8_000_000, transcendentals=0),
    )(*operands)


def add_items(bits, half, lists, table, feats, line_feat, tile_feat, modes, acc, squares):
    tiles = table.shape[0] // ROWS
    at = 0
    for feat in feats:
        line_feat[at : at + feat.shape[0], :] = feat[...]
        at += feat.shape[0]
    line_feat[at:, :] = jnp.zeros((line_feat.shape[0] - at, line_feat.shape[1]), BF16)
    middles = [items.shape[0] // 2 - 1 for items in lists]
    starts = [middle * half for middle in middles]
    first = lists[0][2 * middles[0] + half]
    count = sum(items[2 * middle + half] for items, middle in zip(lists, middles))

    def build(t, carry):
        base = pl.multiple_of(t * ROWS, 8)
        rows = [spread(table, base + 8 * c) for c in range(3)]
        block = tile_block(rows)
        tile_feat[pl.ds(pl.multiple_of(t * TILE, TILE), TILE), :] = block.astype(BF16).T
        value = 4.0 * table[pl.ds(base, ROWS), :]
        high = value.astype(BF16)
        low = (value - high.astype(F32)).astype(BF16)
        at = pl.ds(pl.multiple_of(t * MIX, 16), MIX)
        modes[at, :] = jnp.concatenate([high, low], axis=0)
        return carry

    lax.fori_loop(0, tiles, build, 0, unroll=4)
    mask = tiles - 1

    def unpack(at):
        code = lists[0][starts[0] + jnp.minimum(at, first)]
        other = lists[1][starts[1] + jnp.maximum(at - first, 0)]
        code = jnp.where(at < first, code, other)
        return lax.shift_right_logical(code, bits), code & mask

    def distances(u, at):
        line, tile = unpack(at)
        squares[u][...] = jnp.dot(
            tile_feat[pl.ds(pl.multiple_of(tile * TILE, TILE), TILE), :],
            line_feat[pl.ds(pl.multiple_of(line * FEATS, FEATS), FEATS), :],
            preferred_element_type=F32,
        )

    def gather(u, at):
        line, tile = unpack(at)
        square = jnp.maximum(squares[u][...], TINY)
        near = jnp.maximum(1.0 - square * lax.rsqrt(square), 0.0)
        fourth = near * near
        fourth = fourth * fourth
        phi = fourth * (1.25 - near)
        high = phi.astype(BF16)
        low = (phi - high.astype(F32)).astype(BF16)
        mode = modes[pl.ds(pl.multiple_of(tile * MIX, 16), MIX), :]
        got = jnp.dot(
            jnp.concatenate([mode, mode], axis=1),
            jnp.concatenate([high, low], axis=0),
            preferred_element_type=F32,
        )
        where = pl.ds(pl.multiple_of(line * ROWS, 8), ROWS)
        acc[where, :] = acc[where, :] + (got[0:ROWS] + got[ROWS:MIX])

    def body(j, carry):
        base = j * UNROLL
        for u in range(UNROLL):
            gather(u, base + u)
            distances(u, base + UNROLL + u)
        return carry

    for u in range(UNROLL):
        distances(u, u)
    lax.fori_loop(0, lax.div(count + (UNROLL - 1), jnp.int32(UNROLL)), body, 0)


def load_sum(table):
    tiles = table.shape[0] // ROWS
    return jnp.sum(table[pl.ds(7, tiles, stride=ROWS), :], axis=0, keepdims=True)


def early_kernel(parts, bits, *refs):
    lists, feats = refs[:parts], refs[parts : 2 * parts]
    table, acc, loads, line_feat, tile_feat, modes, *squares = refs[2 * parts :]
    acc[...] = jnp.zeros(acc.shape, F32)
    loads[...] = load_sum(table)
    add_items(bits, 0, lists, table, feats, line_feat, tile_feat, modes, acc, squares)


def late_kernel(own, lent, parts, bits, *refs):
    lists, feats = refs[:parts], refs[parts : 2 * parts]
    table, early, loads, points, corner, motion, inverse, *rest = refs[2 * parts :]
    out_own, out_extra, out_state, out_row, out_plane, *rest = rest
    line_feat, tile_feat, modes, acc, *squares = rest
    total = loads[...] + load_sum(table)
    lane = lax.broadcasted_iota(jnp.int32, (1, 128), 1)
    gravity = jnp.zeros((1, 128), F32)
    for k, pull in enumerate(GRAVITY):
        gravity = jnp.where(lane == k, pull, gravity)
    acceleration = inverse[...] * total + gravity
    out_state[...] = motion[...] + TIME_STEP * acceleration
    step = TIME_STEP * motion[...] + 0.5 * TIME_STEP * TIME_STEP * acceleration
    row = lax.broadcasted_iota(jnp.int32, (8, 128), 0)
    lane = lax.broadcasted_iota(jnp.int32, (8, 128), 1)
    chosen = jnp.where((lane == row - 1) & (lane < 6), jnp.broadcast_to(step, (8, 128)), 0.0)
    weight = jnp.broadcast_to(jnp.sum(chosen, axis=1, keepdims=True), (8, 128))

    acc[...] = early[...]
    add_items(bits, 1, lists, table, feats, line_feat, tile_feat, modes, acc, squares)

    def finish(count, first, out):
        def one(l, carry):
            base = pl.multiple_of((first + l) * ROWS, 8)
            for c in range(3):
                value = jnp.sum(weight * acc[pl.ds(base + 8 * c, 8), :], axis=0, keepdims=True)
                out[pl.ds(c * count + l, 1), :] = value
            return carry

        lax.fori_loop(0, count, one, 0, unroll=4)

    finish(own, 0, out_own)
    finish(lent, own, out_extra)
    rows = out_row.shape[1] // 3
    wide = own // rows
    for c in range(3):
        old = points[c * own : c * own + wide, :]
        out_plane[0, c * wide : (c + 1) * wide, :] = old
        out_plane[1, c * wide : (c + 1) * wide, :] = old + out_own[c * own : c * own + wide, :]
        old = points[pl.ds(c * own, rows, stride=wide), :]
        out_row[0, c * rows : (c + 1) * rows, :] = old
        out_row[1, c * rows : (c + 1) * rows, :] = (
            old + out_own[pl.ds(c * own, rows, stride=wide), :]
        )
    out_plane[0, 3 * wide :, :] = corner[...]
    out_plane[1, 3 * wide :, :] = corner[...]
    for c in range(3):
        at = slice(3 * wide + c, 3 * wide + c + 1)
        out_plane[1, at, :] = corner[c : c + 1, :] + out_extra[c * lent : c * lent + 1, :]


def volume_kernel(
    keep, share, points, shift, *refs
):
    *backs, plane_halo, row_halo, out_shift, out_volume, out_change = refs
    planes, rows, depth = points.shape[1:]
    slab, ctrl = lax.axis_index("slab"), lax.axis_index("ctrl")
    slabs, ctrls = lax.axis_size("slab"), lax.axis_size("ctrl")
    row_id = lax.broadcasted_iota(jnp.int32, (rows, depth), 0)
    lane = lax.broadcasted_iota(jnp.int32, (rows, depth), 1)
    inside = (lane < depth - 1) & (row_id + ctrl * rows < ctrls * rows - 1)
    if backs:
        from_helper = (row_id >= 1) & is_heavy(slab, slabs)
    last_row = row_id == rows - 1

    def next_row(value, edge):
        return jnp.where(last_row, edge, pltpu.roll(value, rows - 1, 0))

    def next_depth(value):
        return pltpu.roll(value, depth - 1, 1)

    def level(x):
        found = []
        for field in range(2):
            parts = []
            for c in range(3):
                if x == planes:
                    here = plane_halo[field, c * rows : (c + 1) * rows, :]
                    edge = plane_halo[field, 3 * rows + c : 3 * rows + c + 1, :]
                else:
                    here = points[c, x]
                    if field == 1:
                        moved = shift[c, x]
                        if backs and x >= keep:
                            back = backs[(x - keep) // share]
                            moved = jnp.where(from_helper, back[c, (x - keep) % share], moved)
                        out_shift[c, x] = moved
                        here = here + moved
                    edge = row_halo[field, c, x : x + 1, :]
                there = next_row(here, edge)
                parts.append((here + there, there - here))
            found.append(parts)
        return found

    before = level(0)
    for x in range(planes):
        after = level(x + 1)
        volumes = []
        for field in range(2):
            edges = []
            for c in range(3):
                both0, step0 = before[field][c]
                both1, step1 = after[field][c]
                along, across, total = both1 - both0, step0 + step1, both0 + both1
                edges.append(
                    (
                        0.25 * (along + next_depth(along)),
                        0.25 * (across + next_depth(across)),
                        0.25 * (next_depth(total) - total),
                    )
                )
            ex, ey, ez = zip(*edges)
            volumes.append(
                ex[0] * (ey[1] * ez[2] - ey[2] * ez[1])
                + ex[1] * (ey[2] * ez[0] - ey[0] * ez[2])
                + ex[2] * (ey[0] * ez[1] - ey[1] * ez[0])
            )
        live = inside & (slab * planes + x < slabs * planes - 1)
        out_volume[x] = jnp.where(live, volumes[1], 0.0)
        out_change[x] = jnp.where(live, volumes[1] - volumes[0], 0.0)
        before = after


def is_heavy(slab, slabs):
    return (8 * slab >= 3 * slabs) & (8 * slab < 5 * slabs)


def local(
    face_pressure,
    face_area,
    face_center,
    motion,
    inverse_mass,
    control_points,
    control_modes,
    node_points,
    tile_list,
    tile_count,
):
    slabs, ctrls = lax.axis_size("slab"), lax.axis_size("ctrl")
    slab, ctrl = lax.axis_index("slab"), lax.axis_index("ctrl")
    _, planes, rows, depth = node_points.shape
    slots = tile_list.shape[2]
    own = planes * rows
    columns = control_points.shape[1]
    tiles = columns * slabs * ctrls // TILE
    bits = max(1, (tiles - 1).bit_length())
    pressure = face_pressure.reshape(1, -1)

    unit = slabs // 8
    share = (planes - 1) // 3
    keep = planes - 3 * share
    lend = slabs % 8 == 0 and slabs & (slabs - 1) == 0 and share > 0
    assert lend, (slabs, planes)
    units = (4 * unit, 2 * unit, unit) if lend else ()
    spans = [tuple(range(keep + g * share, keep + (g + 1) * share)) for g in range(len(units))]
    lent = share * rows if lend else 0
    heavy = [s for s in range(slabs) if is_heavy(s, slabs)]

    direct = columns % TILE == 0 and slabs & (slabs - 1) == 0 and ctrls & (ctrls - 1) == 0
    direct = direct and ctrls > 1 and (columns // TILE) & (columns // TILE - 1) == 0
    own_tiles = columns // TILE
    order = []
    bit = slabs // 2
    while bit:
        order.append((bit, 0))
        bit //= 2
    bit = 1
    while bit < ctrls:
        order.append((0, bit))
        bit *= 2

    def placed(number):
        if not direct:
            return number
        device = lax.axis_index("slab") * ctrls + lax.axis_index("ctrl")
        apart = (number >> (own_tiles.bit_length() - 1)) ^ device
        at = jnp.zeros(number.shape, jnp.int32)
        for turn, (slab_bit, ctrl_bit) in enumerate(order):
            flag = slab_bit * ctrls + ctrl_bit
            at = at + jnp.where((apart & flag) != 0, own_tiles << turn, 0)
        return at + (number & (own_tiles - 1))

    flat_points = node_points.reshape(3 * own, depth)
    *own_lists, last_sent = prepared(
        functools.partial(own_kernel, keep, bits, placed, spans[-1]),
        own, slots, depth, [jax.ShapeDtypeStruct((4 * lent, TILE), F32)], [],
        flat_points, tile_list, tile_count,
    )

    def borrowed(gots, bases):
        kernel = functools.partial(
            lent_kernel, own, rows, slots, lent, bits, placed, units, tuple(bases)
        )
        scratch = [pltpu.VMEM((4 * lent, TILE), F32)]
        return prepared(kernel, lent, slots, depth, [], scratch, *gots, corner)

    gots, bases = [], []
    if direct:
        size = own_tiles * ROWS
        corner, first, *sents = pl.pallas_call(
            functools.partial(pack_kernel, spans[:-1]),
            out_shape=[
                jax.ShapeDtypeStruct((rows_of, TILE), F32)
                for rows_of in [8, size + 4 * lent] + [4 * lent] * (len(units) - 2)
            ],
            in_specs=[vmem()] * 8,
            out_specs=[vmem()] * len(units),
            compiler_params=limited(56),
        )(
            pressure, face_area, face_center, control_points, control_modes,
            flat_points, tile_list, tile_count,
        )
        sents.append(last_sent)
        early = first[:size]
        corner = shifted_back(corner, "ctrl")
        for turn, (slab_bit, ctrl_bit) in enumerate(order[:-1]):
            size = early.shape[0]
            if turn == 2:
                early, own_lists, sents[-1] = lax.optimization_barrier(
                    (early, own_lists, sents[-1])
                )
            if turn == 3:
                early, corner = lax.optimization_barrier((early, corner))
            if lend and slab_bit in units:
                payload = jnp.concatenate([early, sents[len(gots) - 1]], axis=0) if gots else first
                reply = swapped(payload, slab_bit, ctrl_bit)
                gots.append(reply)
                bases.append(size)
                reply = reply[:size]
            else:
                reply = swapped(early, slab_bit, ctrl_bit)
            early = jnp.concatenate([early, reply], axis=0)
        lent_lists = borrowed(gots, bases)
        early, lent_lists = lax.optimization_barrier((early, lent_lists))
        late = swapped(early, *order[-1])
    else:
        loads = pl.pallas_call(
            loads_kernel,
            out_shape=jax.ShapeDtypeStruct((1, TILE), F32),
            in_specs=[vmem()] * 3,
            out_specs=vmem(),
        )(pressure, face_area, face_center)
        loads = lax.psum(loads, ("slab", "ctrl"))
        whole = jnp.concatenate([control_points, control_modes], axis=0)
        whole = lax.all_gather(whole, ("slab", "ctrl"), axis=1, tiled=True)
        whole = whole.reshape(7, 3, tiles, TILE).transpose(2, 1, 0, 3)
        spare = jnp.zeros((tiles, 3, 1, TILE), F32).at[0, 0, 0, :].set(loads[0])
        table = jnp.concatenate([whole, spare], axis=2).reshape(tiles * ROWS, TILE)
        early, late = table[: tiles // 2 * ROWS], table[tiles // 2 * ROWS :]
        corner, *sents = pl.pallas_call(
            functools.partial(lend_kernel, spans),
            out_shape=[jax.ShapeDtypeStruct((8, TILE), F32)]
            + [jax.ShapeDtypeStruct((4 * lent, TILE), F32)] * len(units),
            in_specs=[vmem()] * 3,
            out_specs=[vmem()] * (1 + len(units)),
        )(flat_points, tile_list, tile_count)
        corner = shifted_back(corner, "ctrl")
        gots = [swapped(sent, bit, 0) for sent, bit in zip(sents, units)]
        lent_lists = borrowed(gots, [0] * len(units))
    groups = [own_lists, lent_lists]
    lines = own + lent

    def wide(value):
        return jnp.pad(value, (0, TILE - value.shape[0])).reshape(1, TILE)

    half = tiles // 2
    parts = len(groups)
    lists = [group[0] for group in groups]
    feats = [group[1] for group in groups]
    list_specs = [smem()] * parts + [vmem()] * parts
    scratch = [
        pltpu.VMEM(((lines + 1) * FEATS, depth), BF16),
        pltpu.VMEM((half * TILE, FEATS), BF16),
        pltpu.VMEM((half * MIX, TILE), BF16),
    ]
    squares = [pltpu.VMEM((TILE, depth), F32)] * UNROLL
    partial, part_loads = pl.pallas_call(
        functools.partial(early_kernel, parts, bits),
        out_shape=(
            jax.ShapeDtypeStruct(((lines + 1) * ROWS, depth), F32),
            jax.ShapeDtypeStruct((1, TILE), F32),
        ),
        in_specs=list_specs + [vmem()],
        out_specs=(vmem(), vmem()),
        scratch_shapes=scratch + squares,
        compiler_params=limited(16),
        cost_estimate=pl.CostEstimate(flops=0, bytes_accessed=30_000_000, transcendentals=0),
    )(*lists, *feats, early)
    outs = pl.pallas_call(
        functools.partial(late_kernel, own, lent, parts, bits),
        out_shape=(
            jax.ShapeDtypeStruct((3 * own, depth), F32),
            jax.ShapeDtypeStruct((3 * max(lent, 8), depth), F32),
            jax.ShapeDtypeStruct((1, TILE), F32),
            jax.ShapeDtypeStruct((2, 3 * planes, depth), F32),
            jax.ShapeDtypeStruct((2, 3 * rows + 8, depth), F32),
        ),
        in_specs=list_specs + [vmem()] * 7,
        out_specs=(vmem(),) * 5,
        scratch_shapes=scratch + [pltpu.VMEM(((lines + 1) * ROWS, depth), F32)] + squares,
        compiler_params=limited(16),
    )(
        *lists, *feats, late, partial, part_loads, flat_points, corner,
        wide(motion), wide(inverse_mass),
    )
    shift, lent_shift, state, row_sent, plane_sent = outs

    backs = [
        lax.ppermute(lent_shift, "slab", [(h ^ bit, h) for h in heavy]).reshape(
            3, share, rows, depth
        )
        for bit in units
    ]
    plane_halo = shifted_back(plane_sent, "slab")
    row_halo = shifted_back(row_sent, "ctrl").reshape(2, 3, planes, depth)
    node_shift, volume, change = pl.pallas_call(
        functools.partial(volume_kernel, keep, share),
        out_shape=(
            jax.ShapeDtypeStruct(node_points.shape, F32),
            jax.ShapeDtypeStruct(node_points.shape[1:], F32),
            jax.ShapeDtypeStruct(node_points.shape[1:], F32),
        ),
        in_specs=[vmem()] * (4 + len(backs)),
        out_specs=(vmem(),) * 3,
        compiler_params=limited(8),
    )(node_points, shift.reshape(3, planes, rows, depth), *backs, plane_halo, row_halo)
    return node_shift, volume, change, state[0, : motion.shape[0]]


def solution(mesh):
    placed = (
        P(("slab", "ctrl")),
        P(None, ("slab", "ctrl")),
        P(None, ("slab", "ctrl")),
        P(),
        P(),
        P(None, ("slab", "ctrl")),
        P(None, ("slab", "ctrl")),
        P(None, "slab", "ctrl", None),
        P("slab", "ctrl", None),
        P("slab", "ctrl"),
    )
    return jax.shard_map(
        local,
        mesh=mesh,
        in_specs=placed,
        out_specs=(
            P(None, "slab", "ctrl", None),
            P("slab", "ctrl", None),
            P("slab", "ctrl", None),
            P(),
        ),
        check_vma=False,
    )
```

```python
import functools
import jax
import jax.numpy as jnp
from jax import lax
from jax.experimental import pallas as pl
from jax.experimental.pallas import tpu as pltpu
from jax.sharding import PartitionSpec as P

TILE = 128
TIME_STEP = 0.5
RADIUS = 4.0
GRAVITY = (0.0, 0.0, -0.5, 0.0, 0.0, 0.0)
ROWS = 24
FEATS = 32
UNROLL = 16
MIX = 48
TINY = 1e-30
F32 = jnp.float32
BF16 = jnp.bfloat16


def limited(mib):
    return pltpu.CompilerParams(vmem_limit_bytes=mib << 20)


def vmem():
    return pl.BlockSpec(memory_space=pltpu.VMEM)


def smem():
    return pl.BlockSpec(memory_space=pltpu.SMEM)


def swapped(value, slab_bit, ctrl_bit):
    slabs, ctrls = lax.axis_size("slab"), lax.axis_size("ctrl")
    pairs = [
        (s * ctrls + c, (s ^ slab_bit) * ctrls + (c ^ ctrl_bit))
        for s in range(slabs)
        for c in range(ctrls)
    ]
    return lax.ppermute(value, ("slab", "ctrl"), pairs)


def shifted_back(value, axis):
    return lax.ppermute(value, axis, [(i, i - 1) for i in range(1, lax.axis_size(axis))])


def load_rows(pressure, area, center):
    pushed = pressure * area

    def turned(value, by):
        return jnp.concatenate([value[by:3], value[0:by]], axis=0)

    moment = turned(center, 1) * turned(pushed, 2) - turned(center, 2) * turned(pushed, 1)
    sums = [jnp.sum(pushed, axis=1, keepdims=True), jnp.sum(moment, axis=1, keepdims=True)]
    lane = lax.broadcasted_iota(jnp.int32, (1, 128), 1)
    row = jnp.zeros((1, 128), F32)
    for k in range(6):
        row = jnp.where(lane == k, sums[k // 3][k % 3 : k % 3 + 1, :], row)
    return row


def pack_table(row, points, modes, out):
    for t in range(points.shape[1] // TILE):
        span = slice(t * TILE, (t + 1) * TILE)
        base = t * ROWS
        for c in range(3):
            out[base + 8 * c : base + 8 * c + 1, :] = points[c : c + 1, span]
            for k in range(6):
                at = base + 8 * c + 1 + k
                out[at : at + 1, :] = modes[3 * k + c : 3 * k + c + 1, span]
            at = base + 8 * c + 7
            out[at : at + 1, :] = row if (t == 0 and c == 0) else jnp.zeros((1, 128), F32)


def count_column(counts, x):
    rows = counts.shape[1]
    row = lax.broadcasted_iota(jnp.int32, (rows, rows), 0)
    lane = lax.broadcasted_iota(jnp.int32, (rows, rows), 1)
    many = jnp.broadcast_to(counts[x : x + 1, :].astype(F32), (rows, rows))
    return jnp.sum(jnp.where(row == lane, many, 0.0), axis=1, keepdims=True)


def marked(numbers, counts, x):
    slot = lax.broadcasted_iota(jnp.int32, numbers.shape[1:], 1).astype(F32)
    return jnp.where(slot < count_column(counts, x), numbers[x].astype(F32) + 1.0, 0.0)


def pack_lent(planes, turn, base, nodes, numbers, counts, out):
    rows, slots = numbers.shape[1:]
    lent = len(planes) * rows
    for i, x in enumerate(planes):
        at = base + i * rows
        for c in range(3):
            first = (c * counts.shape[0] + x) * rows
            out[at + c * lent : at + c * lent + rows, :] = nodes[first : first + rows, :]
    at, y = base + rows, 1 + turn
    for c in range(3):
        first = (c * counts.shape[0] + 1) * rows + y
        out[at + c * lent : at + c * lent + 1, :] = nodes[first : first + 1, :]
    for i, x in enumerate(planes):
        listed = marked(numbers, counts, x)
        if i == 1:
            listed = jnp.concatenate([marked(numbers, counts, 1)[y : y + 1], listed[1:]], axis=0)
        at = base + i * lent
        for row in range(rows):
            out[at : at + 1, row * slots : (row + 1) * slots] = listed[row : row + 1]


def pack_corner(nodes, numbers, counts, out):
    slots = numbers.shape[2]
    out[...] = jnp.zeros(out.shape, F32)
    for c in range(3):
        first = c * counts.shape[0] * counts.shape[1]
        out[c : c + 1, :] = nodes[first : first + 1, :]
    out[3:4, 0:slots] = marked(numbers, counts, 0)[0:1]


def pack_kernel(
    spans, pressure, area, center, points, modes, nodes, numbers, counts, corner, out, *lents
):
    row = load_rows(pressure[...], area[...], center[...])
    pack_table(row, points, modes, out)
    pack_corner(nodes, numbers, counts, corner)
    pack_lent(spans[0], 0, points.shape[1] // TILE * ROWS, nodes, numbers, counts, out)
    for turn, (span, lent) in enumerate(zip(spans[1:], lents)):
        pack_lent(span, turn + 1, 0, nodes, numbers, counts, lent)


def lend_kernel(spans, nodes, numbers, counts, corner, *outs):
    pack_corner(nodes, numbers, counts, corner)
    for turn, (span, out) in enumerate(zip(spans, outs)):
        pack_lent(span, turn, 0, nodes, numbers, counts, out)


def loads_kernel(pressure, area, center, out):
    out[...] = load_rows(pressure[...], area[...], center[...])


def split3(value):
    first = value.astype(BF16).astype(F32)
    rest = value - first
    second = rest.astype(BF16).astype(F32)
    return first, second, rest - second


def spread(ref, at):
    return jnp.broadcast_to(ref[pl.ds(at, 1), :], (8, ref.shape[1]))


def products(rows, scale, order, ends):
    row = lax.broadcasted_iota(jnp.int32, rows[0].shape, 0)
    norm = jnp.zeros(rows[0].shape, F32)
    blocks = []
    for value in rows:
        place = value * (1.0 / RADIUS)
        norm = norm + place * place
        first, second, third = split3(place * scale)
        low = jnp.where((row & 1) == 1, order[1](first, second, third, row), order[0](first, second, third, row))
        blocks.append(low)
    first, second, third = split3(norm)
    blocks.append(ends(first, second, third, row))
    return jnp.concatenate(blocks, axis=0)


def tile_block(rows):
    return products(
        rows,
        -2.0,
        (
            lambda a, b, c, row: jnp.where((row == 2) | (row == 6), b, a),
            lambda a, b, c, row: jnp.where(row == 1, a, jnp.where(row == 3, b, c)),
        ),
        lambda a, b, c, row: jnp.where(
            row == 0, a, jnp.where(row == 1, b, jnp.where(row == 2, c, jnp.where(row < 6, 1.0, 0.0)))
        ),
    )


def line_block(rows):
    return products(
        rows,
        1.0,
        (
            lambda a, b, c, row: jnp.where(row < 4, a, c),
            lambda a, b, c, row: jnp.where(row == 5, a, b),
        ),
        lambda a, b, c, row: jnp.where(
            row < 3, 1.0, jnp.where(row == 3, a, jnp.where(row == 4, b, jnp.where(row == 5, c, 0.0)))
        ),
    )


def build_lists(lines, slots, bits, first, listed, items):
    few = min(4, slots)
    middle = lines * slots + 2 * UNROLL

    def take(line, low, high):
        for e in range(low, high):
            value = listed[line, e]
            items[lax.shift_right_logical(value, 16)] = value

    def one(line, carry):
        take(line, 0, few)

        def rest(step, carry):
            take(line, few, slots)
            return carry

        return lax.fori_loop(0, jnp.where(listed[line, slots] > few, 1, 0), rest, carry)

    lax.fori_loop(0, lines, one, 0)
    end_a, end_b = listed[0, slots + 1], listed[0, slots + 2]
    for e in range(2 * UNROLL):
        items[end_a + e] = (first + lines) << bits
        items[middle + end_b + e] = (first + lines) << bits
    items[2 * middle] = end_a
    items[2 * middle + 1] = end_b


def line_features(lines, points, line_feat):
    def block(l, carry):
        rows = [spread(points, c * lines + l) for c in range(3)]
        at = pl.ds(pl.multiple_of(l * FEATS, FEATS), FEATS)
        line_feat[at, :] = line_block(rows).astype(BF16)
        return carry

    lax.fori_loop(0, lines, block, 0, unroll=4)


def code_items(first, bits, placed, numbers, counts, codes):
    lines, slots = numbers.shape
    row = lax.broadcasted_iota(jnp.int32, (lines, slots), 0)
    slot = lax.broadcasted_iota(jnp.int32, (lines, slots), 1)
    code = lax.shift_left(row + first, jnp.full_like(row, bits)) + placed(numbers)
    late = lax.shift_right_logical(code, jnp.full_like(row, bits - 1)) & 1
    middle = lines * slots + 2 * UNROLL
    high = lax.broadcasted_iota(jnp.int32, (slots, slots), 0)
    wide = lax.broadcasted_iota(jnp.int32, (slots, slots), 1)
    before = jnp.where(high < wide, 1.0, 0.0).astype(BF16)
    high = lax.broadcasted_iota(jnp.int32, (lines, lines), 0)
    wide = lax.broadcasted_iota(jnp.int32, (lines, lines), 1)
    above = jnp.where(wide < high, 1.0, 0.0).astype(BF16)
    place = jnp.full((lines, slots), 2 * middle + 2, jnp.int32)
    ends = []
    for part in range(2):
        chosen = (slot < counts) & (late == part)
        flag = jnp.where(chosen, 1.0, 0.0)
        total = jnp.broadcast_to(jnp.sum(flag, axis=1, keepdims=True), (lines, slots))
        at = jnp.dot(flag.astype(BF16), before, preferred_element_type=F32)
        at = at + jnp.dot(above, total.astype(BF16), preferred_element_type=F32)
        place = jnp.where(chosen, at.astype(jnp.int32) + part * middle, place)
        ends.append(jnp.sum(total[:, 0:1], axis=0, keepdims=True).astype(jnp.int32))
    codes[:, 0:slots] = lax.shift_left(place, jnp.full_like(place, 16)) | code
    codes[:, slots : slots + 1] = counts
    codes[0:1, slots + 1 : slots + 2] = ends[0]
    codes[0:1, slots + 2 : slots + 3] = ends[1]


def own_kernel(
    keep, turns, bits, placed, span, points, numbers, counts,
    items, line_feat, sent, codes, listed, sem,
):
    planes, rows, slots = numbers.shape
    pack_lent(span, turns - 1, 0, points, numbers, counts, sent)
    slabs = lax.axis_size("slab")
    lends = is_heavy(lax.axis_index("slab"), slabs)
    columns = []
    for x in range(planes):
        count = count_column(counts, x).astype(jnp.int32)
        if x >= keep:
            row = lax.broadcasted_iota(jnp.int32, count.shape, 0)
            count = jnp.where(lends & (row >= 1), 0, count)
        if x == 1:
            row = lax.broadcasted_iota(jnp.int32, count.shape, 0)
            count = jnp.where(lends & (row >= 1) & (row <= turns), 0, count)
        columns.append(count)
    number = jnp.concatenate([numbers[x] for x in range(planes)], axis=0)
    code_items(0, bits, placed, number, jnp.concatenate(columns, axis=0), codes)
    copy = pltpu.make_async_copy(codes, listed, sem)
    copy.start()
    line_features(planes * rows, points, line_feat)
    copy.wait()
    build_lists(planes * rows, slots, bits, 0, listed, items)


def lent_kernel(
    first, rows, slots, lent, bits, placed, units, bases, *refs
):
    gots, refs = refs[: len(units)], refs[len(units) :]
    corner, items, line_feat, codes, listed, got, sem = refs
    slab, slabs = lax.axis_index("slab"), lax.axis_size("slab")
    value = gots[-1][pl.ds(bases[-1], 3 * lent), :]
    for unit, base, ref in list(zip(units, bases, gots))[:-1]:
        value = jnp.where(is_heavy(slab ^ unit, slabs), ref[pl.ds(base, 3 * lent), :], value)
    number = [
        value[i * lent : i * lent + 1, y * slots : (y + 1) * slots]
        for i in range(lent // rows)
        for y in range(rows)
    ]
    number = jnp.concatenate([corner[3:4, 0:slots]] + number[1:], axis=0)
    got[...] = value
    for c in range(3):
        got[c * lent : c * lent + 1, :] = corner[c : c + 1, :]
    helps = jnp.logical_not(is_heavy(slab, slabs))
    line = lax.broadcasted_iota(jnp.int32, number.shape, 0)
    taken = (helps & ((lax.rem(line, rows) >= 1) | (line == rows))) | (line == 0)
    number = jnp.where(taken, number, 0.0)
    count = jnp.sum(jnp.where(number > 0.0, 1.0, 0.0), axis=1, keepdims=True).astype(jnp.int32)
    number = jnp.maximum(number - 1.0, 0.0).astype(jnp.int32)
    code_items(first, bits, placed, number, count, codes)
    copy = pltpu.make_async_copy(codes, listed, sem)
    copy.start()
    line_features(lent, got, line_feat)
    copy.wait()
    build_lists(lent, slots, bits, first, listed, items)


def prepared(kernel, lines, slots, depth, more, scratch, *operands):
    length = lines * slots + 2 * UNROLL
    return pl.pallas_call(
        kernel,
        out_shape=(
            jax.ShapeDtypeStruct((2 * length + 3,), jnp.int32),
            jax.ShapeDtypeStruct((lines * FEATS, depth), BF16),
            *more,
        ),
        in_specs=[vmem()] * len(operands),
        out_specs=(smem(), vmem()) + (vmem(),) * len(more),
        scratch_shapes=[
            pltpu.VMEM((lines, TILE), jnp.int32),
            pltpu.SMEM((lines, TILE), jnp.int32),
        ]
        + scratch
        + [pltpu.SemaphoreType.DMA],
        compiler_params=limited(4),
        cost_estimate=pl.CostEstimate(flops=0, bytes_accessed=8_000_000, transcendentals=0),
    )(*operands)


def add_items(bits, half, lists, table, feats, line_feat, tile_feat, modes, acc, squares):
    tiles = table.shape[0] // ROWS
    at = 0
    for feat in feats:
        line_feat[at : at + feat.shape[0], :] = feat[...]
        at += feat.shape[0]
    line_feat[at:, :] = jnp.zeros((line_feat.shape[0] - at, line_feat.shape[1]), BF16)
    middles = [(items.shape[0] - 3) // 2 for items in lists]
    starts = [middle * half for middle in middles]
    first = lists[0][2 * middles[0] + half]
    count = sum(items[2 * middle + half] for items, middle in zip(lists, middles))

    def build(t, carry):
        base = pl.multiple_of(t * ROWS, 8)
        rows = [spread(table, base + 8 * c) for c in range(3)]
        block = tile_block(rows)
        tile_feat[pl.ds(pl.multiple_of(t * TILE, TILE), TILE), :] = block.astype(BF16).T
        value = 4.0 * table[pl.ds(base, ROWS), :]
        high = value.astype(BF16)
        low = (value - high.astype(F32)).astype(BF16)
        at = pl.ds(pl.multiple_of(t * MIX, 16), MIX)
        modes[at, :] = jnp.concatenate([high, low], axis=0)
        return carry

    lax.fori_loop(0, tiles, build, 0, unroll=4)
    mask = tiles - 1

    def unpack(at):
        code = lists[0][starts[0] + jnp.minimum(at, first)]
        other = lists[1][starts[1] + jnp.maximum(at - first, 0)]
        code = jnp.where(at < first, code, other)
        return lax.shift_right_logical(code & 0xFFFF, bits), code & mask

    def distances(u, at):
        line, tile = unpack(at)
        squares[u][...] = jnp.dot(
            tile_feat[pl.ds(pl.multiple_of(tile * TILE, TILE), TILE), :],
            line_feat[pl.ds(pl.multiple_of(line * FEATS, FEATS), FEATS), :],
            preferred_element_type=F32,
        )

    def gather(u, at):
        line, tile = unpack(at)
        square = jnp.maximum(squares[u][...], TINY)
        near = jnp.maximum(1.0 - square * lax.rsqrt(square), 0.0)
        fourth = near * near
        fourth = fourth * fourth
        phi = fourth * (1.25 - near)
        high = phi.astype(BF16)
        low = (phi - high.astype(F32)).astype(BF16)
        mode = modes[pl.ds(pl.multiple_of(tile * MIX, 16), MIX), :]
        got = jnp.dot(
            jnp.concatenate([mode, mode], axis=1),
            jnp.concatenate([high, low], axis=0),
            preferred_element_type=F32,
        )
        where = pl.ds(pl.multiple_of(line * ROWS, 8), ROWS)
        acc[where, :] = acc[where, :] + (got[0:ROWS] + got[ROWS:MIX])

    def body(j, carry):
        base = j * UNROLL
        for u in range(UNROLL):
            gather(u, base + u)
            distances(u, base + UNROLL + u)
        return carry

    for u in range(UNROLL):
        distances(u, u)
    lax.fori_loop(0, lax.div(count + (UNROLL - 1), jnp.int32(UNROLL)), body, 0)


def load_sum(table):
    tiles = table.shape[0] // ROWS
    return jnp.sum(table[pl.ds(7, tiles, stride=ROWS), :], axis=0, keepdims=True)


def early_kernel(parts, bits, *refs):
    lists, feats = refs[:parts], refs[parts : 2 * parts]
    table, acc, loads, line_feat, tile_feat, modes, *squares = refs[2 * parts :]
    acc[...] = jnp.zeros(acc.shape, F32)
    loads[...] = load_sum(table)
    add_items(bits, 0, lists, table, feats, line_feat, tile_feat, modes, acc, squares)


def late_kernel(own, lent, parts, bits, *refs):
    lists, feats = refs[:parts], refs[parts : 2 * parts]
    table, early, loads, points, corner, motion, inverse, *rest = refs[2 * parts :]
    out_own, out_extra, out_state, out_row, out_plane, *rest = rest
    line_feat, tile_feat, modes, acc, *squares = rest
    total = loads[...] + load_sum(table)
    lane = lax.broadcasted_iota(jnp.int32, (1, 128), 1)
    gravity = jnp.zeros((1, 128), F32)
    for k, pull in enumerate(GRAVITY):
        gravity = jnp.where(lane == k, pull, gravity)
    acceleration = inverse[...] * total + gravity
    out_state[...] = motion[...] + TIME_STEP * acceleration
    step = TIME_STEP * motion[...] + 0.5 * TIME_STEP * TIME_STEP * acceleration
    row = lax.broadcasted_iota(jnp.int32, (8, 128), 0)
    lane = lax.broadcasted_iota(jnp.int32, (8, 128), 1)
    chosen = jnp.where((lane == row - 1) & (lane < 6), jnp.broadcast_to(step, (8, 128)), 0.0)
    weight = jnp.broadcast_to(jnp.sum(chosen, axis=1, keepdims=True), (8, 128))

    acc[...] = early[...]
    add_items(bits, 1, lists, table, feats, line_feat, tile_feat, modes, acc, squares)

    def finish(count, first, out):
        def one(l, carry):
            base = pl.multiple_of((first + l) * ROWS, 8)
            for c in range(3):
                value = jnp.sum(weight * acc[pl.ds(base + 8 * c, 8), :], axis=0, keepdims=True)
                out[pl.ds(c * count + l, 1), :] = value
            return carry

        lax.fori_loop(0, count, one, 0, unroll=4)

    finish(own, 0, out_own)
    finish(lent, own, out_extra)
    rows = out_row.shape[1] // 3
    wide = own // rows
    for c in range(3):
        old = points[c * own : c * own + wide, :]
        out_plane[0, c * wide : (c + 1) * wide, :] = old
        out_plane[1, c * wide : (c + 1) * wide, :] = old + out_own[c * own : c * own + wide, :]
        old = points[pl.ds(c * own, rows, stride=wide), :]
        out_row[0, c * rows : (c + 1) * rows, :] = old
        out_row[1, c * rows : (c + 1) * rows, :] = (
            old + out_own[pl.ds(c * own, rows, stride=wide), :]
        )
    out_plane[0, 3 * wide :, :] = corner[...]
    out_plane[1, 3 * wide :, :] = corner[...]
    for c in range(3):
        at = slice(3 * wide + c, 3 * wide + c + 1)
        out_plane[1, at, :] = corner[c : c + 1, :] + out_extra[c * lent : c * lent + 1, :]


def volume_kernel(
    keep, share, points, shift, *refs
):
    *backs, plane_halo, row_halo, out_shift, out_volume, out_change = refs
    planes, rows, depth = points.shape[1:]
    slab, ctrl = lax.axis_index("slab"), lax.axis_index("ctrl")
    slabs, ctrls = lax.axis_size("slab"), lax.axis_size("ctrl")
    row_id = lax.broadcasted_iota(jnp.int32, (rows, depth), 0)
    lane = lax.broadcasted_iota(jnp.int32, (rows, depth), 1)
    inside = (lane < depth - 1) & (row_id + ctrl * rows < ctrls * rows - 1)
    if backs:
        from_helper = (row_id >= 1) & is_heavy(slab, slabs)
    last_row = row_id == rows - 1

    def next_row(value, edge):
        return jnp.where(last_row, edge, pltpu.roll(value, rows - 1, 0))

    def next_depth(value):
        return pltpu.roll(value, depth - 1, 1)

    def level(x):
        found = []
        for field in range(2):
            parts = []
            for c in range(3):
                if x == planes:
                    here = plane_halo[field, c * rows : (c + 1) * rows, :]
                    edge = plane_halo[field, 3 * rows + c : 3 * rows + c + 1, :]
                else:
                    here = points[c, x]
                    if field == 1:
                        moved = shift[c, x]
                        if backs and x >= keep:
                            back = backs[(x - keep) // share]
                            moved = jnp.where(from_helper, back[c, (x - keep) % share], moved)
                        if x == 1:
                            for turn, back in enumerate(backs):
                                here_too = from_helper & (row_id == 1 + turn)
                                moved = jnp.where(here_too, back[c, 1, 0:1, :], moved)
                        out_shift[c, x] = moved
                        here = here + moved
                    edge = row_halo[field, c, x : x + 1, :]
                there = next_row(here, edge)
                parts.append((here + there, there - here))
            found.append(parts)
        return found

    before = level(0)
    for x in range(planes):
        after = level(x + 1)
        volumes = []
        for field in range(2):
            edges = []
            for c in range(3):
                both0, step0 = before[field][c]
                both1, step1 = after[field][c]
                along, across, total = both1 - both0, step0 + step1, both0 + both1
                edges.append(
                    (
                        0.25 * (along + next_depth(along)),
                        0.25 * (across + next_depth(across)),
                        0.25 * (next_depth(total) - total),
                    )
                )
            ex, ey, ez = zip(*edges)
            volumes.append(
                ex[0] * (ey[1] * ez[2] - ey[2] * ez[1])
                + ex[1] * (ey[2] * ez[0] - ey[0] * ez[2])
                + ex[2] * (ey[0] * ez[1] - ey[1] * ez[0])
            )
        live = inside & (slab * planes + x < slabs * planes - 1)
        out_volume[x] = jnp.where(live, volumes[1], 0.0)
        out_change[x] = jnp.where(live, volumes[1] - volumes[0], 0.0)
        before = after


def is_heavy(slab, slabs):
    return (8 * slab >= 3 * slabs) & (8 * slab < 5 * slabs)


def local(
    face_pressure,
    face_area,
    face_center,
    motion,
    inverse_mass,
    control_points,
    control_modes,
    node_points,
    tile_list,
    tile_count,
):
    slabs, ctrls = lax.axis_size("slab"), lax.axis_size("ctrl")
    slab, ctrl = lax.axis_index("slab"), lax.axis_index("ctrl")
    _, planes, rows, depth = node_points.shape
    slots = tile_list.shape[2]
    own = planes * rows
    columns = control_points.shape[1]
    tiles = columns * slabs * ctrls // TILE
    bits = max(1, (tiles - 1).bit_length())
    pressure = face_pressure.reshape(1, -1)

    unit = slabs // 8
    share = (planes - 1) // 3
    keep = planes - 3 * share
    lend = slabs % 8 == 0 and slabs & (slabs - 1) == 0 and share > 1 and keep > 1 and rows > 4
    assert lend and share <= 3 and rows * slots <= TILE, (slabs, planes, rows, slots)
    units = (4 * unit, 2 * unit, unit) if lend else ()
    spans = [tuple(range(keep + g * share, keep + (g + 1) * share)) for g in range(len(units))]
    lent = share * rows if lend else 0
    heavy = [s for s in range(slabs) if is_heavy(s, slabs)]

    direct = columns % TILE == 0 and slabs & (slabs - 1) == 0 and ctrls & (ctrls - 1) == 0
    direct = direct and ctrls > 1 and (columns // TILE) & (columns // TILE - 1) == 0
    own_tiles = columns // TILE
    order = []
    bit = slabs // 2
    while bit:
        order.append((bit, 0))
        bit //= 2
    bit = 1
    while bit < ctrls:
        order.append((0, bit))
        bit *= 2

    def placed(number):
        if not direct:
            return number
        device = lax.axis_index("slab") * ctrls + lax.axis_index("ctrl")
        apart = (number >> (own_tiles.bit_length() - 1)) ^ device
        at = jnp.zeros(number.shape, jnp.int32)
        for turn, (slab_bit, ctrl_bit) in enumerate(order):
            flag = slab_bit * ctrls + ctrl_bit
            at = at + jnp.where((apart & flag) != 0, own_tiles << turn, 0)
        return at + (number & (own_tiles - 1))

    flat_points = node_points.reshape(3 * own, depth)
    *own_lists, last_sent = prepared(
        functools.partial(own_kernel, keep, len(units), bits, placed, spans[-1]),
        own, slots, depth, [jax.ShapeDtypeStruct((3 * lent, TILE), F32)], [],
        flat_points, tile_list, tile_count,
    )

    def borrowed(gots, bases):
        kernel = functools.partial(
            lent_kernel, own, rows, slots, lent, bits, placed, units, tuple(bases)
        )
        scratch = [pltpu.VMEM((3 * lent, TILE), F32)]
        return prepared(kernel, lent, slots, depth, [], scratch, *gots, corner)

    gots, bases = [], []
    if direct:
        size = own_tiles * ROWS
        corner, first, *sents = pl.pallas_call(
            functools.partial(pack_kernel, spans[:-1]),
            out_shape=[
                jax.ShapeDtypeStruct((rows_of, TILE), F32)
                for rows_of in [8, size + 3 * lent] + [3 * lent] * (len(units) - 2)
            ],
            in_specs=[vmem()] * 8,
            out_specs=[vmem()] * len(units),
            compiler_params=limited(56),
        )(
            pressure, face_area, face_center, control_points, control_modes,
            flat_points, tile_list, tile_count,
        )
        sents.append(last_sent)
        early = first[:size]
        corner = shifted_back(corner, "ctrl")
        for turn, (slab_bit, ctrl_bit) in enumerate(order[:-1]):
            size = early.shape[0]
            if turn == 2:
                early, own_lists, sents[-1] = lax.optimization_barrier(
                    (early, own_lists, sents[-1])
                )
            if turn == 3:
                early, corner = lax.optimization_barrier((early, corner))
            if lend and slab_bit in units:
                payload = jnp.concatenate([early, sents[len(gots) - 1]], axis=0) if gots else first
                reply = swapped(payload, slab_bit, ctrl_bit)
                gots.append(reply)
                bases.append(size)
                reply = reply[:size]
            else:
                reply = swapped(early, slab_bit, ctrl_bit)
            early = jnp.concatenate([early, reply], axis=0)
        lent_lists = borrowed(gots, bases)
        late = swapped(early, *order[-1])
    else:
        loads = pl.pallas_call(
            loads_kernel,
            out_shape=jax.ShapeDtypeStruct((1, TILE), F32),
            in_specs=[vmem()] * 3,
            out_specs=vmem(),
        )(pressure, face_area, face_center)
        loads = lax.psum(loads, ("slab", "ctrl"))
        whole = jnp.concatenate([control_points, control_modes], axis=0)
        whole = lax.all_gather(whole, ("slab", "ctrl"), axis=1, tiled=True)
        whole = whole.reshape(7, 3, tiles, TILE).transpose(2, 1, 0, 3)
        spare = jnp.zeros((tiles, 3, 1, TILE), F32).at[0, 0, 0, :].set(loads[0])
        table = jnp.concatenate([whole, spare], axis=2).reshape(tiles * ROWS, TILE)
        early, late = table[: tiles // 2 * ROWS], table[tiles // 2 * ROWS :]
        corner, *sents = pl.pallas_call(
            functools.partial(lend_kernel, spans),
            out_shape=[jax.ShapeDtypeStruct((8, TILE), F32)]
            + [jax.ShapeDtypeStruct((3 * lent, TILE), F32)] * len(units),
            in_specs=[vmem()] * 3,
            out_specs=[vmem()] * (1 + len(units)),
        )(flat_points, tile_list, tile_count)
        corner = shifted_back(corner, "ctrl")
        gots = [swapped(sent, bit, 0) for sent, bit in zip(sents, units)]
        lent_lists = borrowed(gots, [0] * len(units))
    groups = [own_lists, lent_lists]
    lines = own + lent

    def wide(value):
        return jnp.pad(value, (0, TILE - value.shape[0])).reshape(1, TILE)

    half = tiles // 2
    parts = len(groups)
    lists = [group[0] for group in groups]
    feats = [group[1] for group in groups]
    list_specs = [smem()] * parts + [vmem()] * parts
    scratch = [
        pltpu.VMEM(((lines + 1) * FEATS, depth), BF16),
        pltpu.VMEM((half * TILE, FEATS), BF16),
        pltpu.VMEM((half * MIX, TILE), BF16),
    ]
    squares = [pltpu.VMEM((TILE, depth), F32)] * UNROLL
    partial, part_loads = pl.pallas_call(
        functools.partial(early_kernel, parts, bits),
        out_shape=(
            jax.ShapeDtypeStruct(((lines + 1) * ROWS, depth), F32),
            jax.ShapeDtypeStruct((1, TILE), F32),
        ),
        in_specs=list_specs + [vmem()],
        out_specs=(vmem(), vmem()),
        scratch_shapes=scratch + squares,
        compiler_params=limited(16),
        cost_estimate=pl.CostEstimate(flops=0, bytes_accessed=30_000_000, transcendentals=0),
    )(*lists, *feats, early)
    outs = pl.pallas_call(
        functools.partial(late_kernel, own, lent, parts, bits),
        out_shape=(
            jax.ShapeDtypeStruct((3 * own, depth), F32),
            jax.ShapeDtypeStruct((3 * max(lent, 8), depth), F32),
            jax.ShapeDtypeStruct((1, TILE), F32),
            jax.ShapeDtypeStruct((2, 3 * planes, depth), F32),
            jax.ShapeDtypeStruct((2, 3 * rows + 8, depth), F32),
        ),
        in_specs=list_specs + [vmem()] * 7,
        out_specs=(vmem(),) * 5,
        scratch_shapes=scratch + [pltpu.VMEM(((lines + 1) * ROWS, depth), F32)] + squares,
        compiler_params=limited(16),
    )(
        *lists, *feats, late, partial, part_loads, flat_points, corner,
        wide(motion), wide(inverse_mass),
    )
    shift, lent_shift, state, row_sent, plane_sent = outs

    backs = [
        lax.ppermute(lent_shift, "slab", [(h ^ bit, h) for h in heavy]).reshape(
            3, share, rows, depth
        )
        for bit in units
    ]
    plane_halo = shifted_back(plane_sent, "slab")
    row_halo = shifted_back(row_sent, "ctrl").reshape(2, 3, planes, depth)
    node_shift, volume, change = pl.pallas_call(
        functools.partial(volume_kernel, keep, share),
        out_shape=(
            jax.ShapeDtypeStruct(node_points.shape, F32),
            jax.ShapeDtypeStruct(node_points.shape[1:], F32),
            jax.ShapeDtypeStruct(node_points.shape[1:], F32),
        ),
        in_specs=[vmem()] * (4 + len(backs)),
        out_specs=(vmem(),) * 3,
        compiler_params=limited(8),
    )(node_points, shift.reshape(3, planes, rows, depth), *backs, plane_halo, row_halo)
    return node_shift, volume, change, state[0, : motion.shape[0]]


def solution(mesh):
    placed = (
        P(("slab", "ctrl")),
        P(None, ("slab", "ctrl")),
        P(None, ("slab", "ctrl")),
        P(),
        P(),
        P(None, ("slab", "ctrl")),
        P(None, ("slab", "ctrl")),
        P(None, "slab", "ctrl", None),
        P("slab", "ctrl", None),
        P("slab", "ctrl"),
    )
    return jax.shard_map(
        local,
        mesh=mesh,
        in_specs=placed,
        out_specs=(
            P(None, "slab", "ctrl", None),
            P("slab", "ctrl", None),
            P("slab", "ctrl", None),
            P(),
        ),
        check_vma=False,
    )
```

```python
import functools
import jax
import jax.numpy as jnp
from jax import lax
from jax.experimental import pallas as pl
from jax.experimental.pallas import tpu as pltpu
from jax.sharding import PartitionSpec as P

TILE = 128
TIME_STEP = 0.5
RADIUS = 4.0
GRAVITY = (0.0, 0.0, -0.5, 0.0, 0.0, 0.0)
ROWS = 24
FEATS = 32
UNROLL = 20
MIX = 48
TINY = 1e-30
F32 = jnp.float32
BF16 = jnp.bfloat16


def limited(mib):
    return pltpu.CompilerParams(vmem_limit_bytes=mib << 20)


def vmem():
    return pl.BlockSpec(memory_space=pltpu.VMEM)


def smem():
    return pl.BlockSpec(memory_space=pltpu.SMEM)


def swapped(value, slab_bit, ctrl_bit):
    slabs, ctrls = lax.axis_size("slab"), lax.axis_size("ctrl")
    pairs = [
        (s * ctrls + c, (s ^ slab_bit) * ctrls + (c ^ ctrl_bit))
        for s in range(slabs)
        for c in range(ctrls)
    ]
    return lax.ppermute(value, ("slab", "ctrl"), pairs)


def shifted_back(value, axis):
    return lax.ppermute(value, axis, [(i, i - 1) for i in range(1, lax.axis_size(axis))])


def load_rows(pressure, area, center):
    pushed = pressure * area

    def turned(value, by):
        return jnp.concatenate([value[by:3], value[0:by]], axis=0)

    moment = turned(center, 1) * turned(pushed, 2) - turned(center, 2) * turned(pushed, 1)
    sums = [jnp.sum(pushed, axis=1, keepdims=True), jnp.sum(moment, axis=1, keepdims=True)]
    lane = lax.broadcasted_iota(jnp.int32, (1, 128), 1)
    row = jnp.zeros((1, 128), F32)
    for k in range(6):
        row = jnp.where(lane == k, sums[k // 3][k % 3 : k % 3 + 1, :], row)
    return row


def pack_table(row, points, modes, out):
    for t in range(points.shape[1] // TILE):
        span = slice(t * TILE, (t + 1) * TILE)
        base = t * ROWS
        for c in range(3):
            out[base + 8 * c : base + 8 * c + 1, :] = points[c : c + 1, span]
            for k in range(6):
                at = base + 8 * c + 1 + k
                out[at : at + 1, :] = modes[3 * k + c : 3 * k + c + 1, span]
            at = base + 8 * c + 7
            out[at : at + 1, :] = row if (t == 0 and c == 0) else jnp.zeros((1, 128), F32)


def count_column(counts, x):
    rows = counts.shape[1]
    row = lax.broadcasted_iota(jnp.int32, (rows, rows), 0)
    lane = lax.broadcasted_iota(jnp.int32, (rows, rows), 1)
    many = jnp.broadcast_to(counts[x : x + 1, :].astype(F32), (rows, rows))
    return jnp.sum(jnp.where(row == lane, many, 0.0), axis=1, keepdims=True)


def marked(numbers, counts, x):
    slot = lax.broadcasted_iota(jnp.int32, numbers.shape[1:], 1).astype(F32)
    return jnp.where(slot < count_column(counts, x), numbers[x].astype(F32) + 1.0, 0.0)


def pack_lent(planes, turn, base, nodes, numbers, counts, out):
    rows, slots = numbers.shape[1:]
    lent = len(planes) * rows
    for i, x in enumerate(planes):
        at = base + i * rows
        for c in range(3):
            first = (c * counts.shape[0] + x) * rows
            out[at + c * lent : at + c * lent + rows, :] = nodes[first : first + rows, :]
    at, y = base + rows, 1 + turn
    for c in range(3):
        first = (c * counts.shape[0] + 1) * rows + y
        out[at + c * lent : at + c * lent + 1, :] = nodes[first : first + 1, :]
    for i, x in enumerate(planes):
        listed = marked(numbers, counts, x)
        if i == 1:
            listed = jnp.concatenate([marked(numbers, counts, 1)[y : y + 1], listed[1:]], axis=0)
        at = base + i * lent
        for row in range(rows):
            out[at : at + 1, row * slots : (row + 1) * slots] = listed[row : row + 1]


def pack_corner(nodes, numbers, counts, out):
    slots = numbers.shape[2]
    out[...] = jnp.zeros(out.shape, F32)
    for c in range(3):
        first = c * counts.shape[0] * counts.shape[1]
        out[c : c + 1, :] = nodes[first : first + 1, :]
    out[3:4, 0:slots] = marked(numbers, counts, 0)[0:1]


def pack_kernel(
    spans, pressure, area, center, points, modes, nodes, numbers, counts, corner, out, *lents
):
    row = load_rows(pressure[...], area[...], center[...])
    pack_table(row, points, modes, out)
    pack_corner(nodes, numbers, counts, corner)
    pack_lent(spans[0], 0, points.shape[1] // TILE * ROWS, nodes, numbers, counts, out)
    for turn, (span, lent) in enumerate(zip(spans[1:], lents)):
        pack_lent(span, turn + 1, 0, nodes, numbers, counts, lent)


def lend_kernel(spans, nodes, numbers, counts, corner, *outs):
    pack_corner(nodes, numbers, counts, corner)
    for turn, (span, out) in enumerate(zip(spans, outs)):
        pack_lent(span, turn, 0, nodes, numbers, counts, out)


def loads_kernel(pressure, area, center, out):
    out[...] = load_rows(pressure[...], area[...], center[...])


def split3(value):
    first = value.astype(BF16).astype(F32)
    rest = value - first
    second = rest.astype(BF16).astype(F32)
    return first, second, rest - second


def spread(ref, at):
    return jnp.broadcast_to(ref[pl.ds(at, 1), :], (8, ref.shape[1]))


def products(rows, scale, order, ends):
    row = lax.broadcasted_iota(jnp.int32, rows[0].shape, 0)
    norm = jnp.zeros(rows[0].shape, F32)
    blocks = []
    for value in rows:
        place = value * (1.0 / RADIUS)
        norm = norm + place * place
        first, second, third = split3(place * scale)
        low = jnp.where((row & 1) == 1, order[1](first, second, third, row), order[0](first, second, third, row))
        blocks.append(low)
    first, second, third = split3(norm)
    blocks.append(ends(first, second, third, row))
    return jnp.concatenate(blocks, axis=0)


def tile_block(rows):
    return products(
        rows,
        -2.0,
        (
            lambda a, b, c, row: jnp.where((row == 2) | (row == 6), b, a),
            lambda a, b, c, row: jnp.where(row == 1, a, jnp.where(row == 3, b, c)),
        ),
        lambda a, b, c, row: jnp.where(
            row == 0, a, jnp.where(row == 1, b, jnp.where(row == 2, c, jnp.where(row < 6, 1.0, 0.0)))
        ),
    )


def line_block(rows):
    return products(
        rows,
        1.0,
        (
            lambda a, b, c, row: jnp.where(row < 4, a, c),
            lambda a, b, c, row: jnp.where(row == 5, a, b),
        ),
        lambda a, b, c, row: jnp.where(
            row < 3, 1.0, jnp.where(row == 3, a, jnp.where(row == 4, b, jnp.where(row == 5, c, 0.0)))
        ),
    )


def build_lists(lines, slots, bits, first, listed, items):
    few = min(4, slots)
    middle = lines * slots + 2 * UNROLL

    def take(line, low, high):
        for e in range(low, high):
            value = listed[line, e]
            items[lax.shift_right_logical(value, 16)] = value

    def one(line, carry):
        take(line, 0, few)

        def rest(step, carry):
            take(line, few, slots)
            return carry

        return lax.fori_loop(0, jnp.where(listed[line, slots] > few, 1, 0), rest, carry)

    lax.fori_loop(0, lines, one, 0)
    end_a, end_b = listed[0, slots + 1], listed[0, slots + 2]
    for e in range(2 * UNROLL):
        items[end_a + e] = (first + lines) << bits
        items[middle + end_b + e] = (first + lines) << bits
    items[2 * middle] = end_a
    items[2 * middle + 1] = end_b


def line_features(lines, points, line_feat):
    def block(l, carry):
        rows = [spread(points, c * lines + l) for c in range(3)]
        at = pl.ds(pl.multiple_of(l * FEATS, FEATS), FEATS)
        line_feat[at, :] = line_block(rows).astype(BF16)
        return carry

    lax.fori_loop(0, lines, block, 0, unroll=4)


def code_items(first, bits, placed, numbers, counts, codes):
    lines, slots = numbers.shape
    row = lax.broadcasted_iota(jnp.int32, (lines, slots), 0)
    slot = lax.broadcasted_iota(jnp.int32, (lines, slots), 1)
    code = lax.shift_left(row + first, jnp.full_like(row, bits)) + placed(numbers)
    late = lax.shift_right_logical(code, jnp.full_like(row, bits - 1)) & 1
    middle = lines * slots + 2 * UNROLL
    high = lax.broadcasted_iota(jnp.int32, (slots, slots), 0)
    wide = lax.broadcasted_iota(jnp.int32, (slots, slots), 1)
    before = jnp.where(high < wide, 1.0, 0.0).astype(BF16)
    high = lax.broadcasted_iota(jnp.int32, (lines, lines), 0)
    wide = lax.broadcasted_iota(jnp.int32, (lines, lines), 1)
    above = jnp.where(wide < high, 1.0, 0.0).astype(BF16)
    place = jnp.full((lines, slots), 2 * middle + 2, jnp.int32)
    ends = []
    for part in range(2):
        chosen = (slot < counts) & (late == part)
        flag = jnp.where(chosen, 1.0, 0.0)
        total = jnp.broadcast_to(jnp.sum(flag, axis=1, keepdims=True), (lines, slots))
        at = jnp.dot(flag.astype(BF16), before, preferred_element_type=F32)
        at = at + jnp.dot(above, total.astype(BF16), preferred_element_type=F32)
        place = jnp.where(chosen, at.astype(jnp.int32) + part * middle, place)
        ends.append(jnp.sum(total[:, 0:1], axis=0, keepdims=True).astype(jnp.int32))
    codes[:, 0:slots] = lax.shift_left(place, jnp.full_like(place, 16)) | code
    codes[:, slots : slots + 1] = counts
    codes[0:1, slots + 1 : slots + 2] = ends[0]
    codes[0:1, slots + 2 : slots + 3] = ends[1]


def own_kernel(
    keep, turns, bits, placed, span, points, numbers, counts,
    items, line_feat, sent, codes, listed, sem,
):
    planes, rows, slots = numbers.shape
    pack_lent(span, turns - 1, 0, points, numbers, counts, sent)
    slabs = lax.axis_size("slab")
    lends = is_heavy(lax.axis_index("slab"), slabs)
    columns = []
    for x in range(planes):
        count = count_column(counts, x).astype(jnp.int32)
        if x >= keep:
            row = lax.broadcasted_iota(jnp.int32, count.shape, 0)
            count = jnp.where(lends & (row >= 1), 0, count)
        if x == 1:
            row = lax.broadcasted_iota(jnp.int32, count.shape, 0)
            count = jnp.where(lends & (row >= 1) & (row <= turns), 0, count)
        columns.append(count)
    number = jnp.concatenate([numbers[x] for x in range(planes)], axis=0)
    code_items(0, bits, placed, number, jnp.concatenate(columns, axis=0), codes)
    copy = pltpu.make_async_copy(codes, listed, sem)
    copy.start()
    line_features(planes * rows, points, line_feat)
    copy.wait()
    build_lists(planes * rows, slots, bits, 0, listed, items)


def read_lent(first, rows, slots, lent, bits, placed, units, bases, gots, corner, got, codes):
    slab, slabs = lax.axis_index("slab"), lax.axis_size("slab")
    value = gots[-1][pl.ds(bases[-1], 3 * lent), :]
    for unit, base, ref in list(zip(units, bases, gots))[:-1]:
        value = jnp.where(is_heavy(slab ^ unit, slabs), ref[pl.ds(base, 3 * lent), :], value)
    number = [
        value[i * lent : i * lent + 1, y * slots : (y + 1) * slots]
        for i in range(lent // rows)
        for y in range(rows)
    ]
    number = jnp.concatenate([corner[3:4, 0:slots]] + number[1:], axis=0)
    got[...] = value
    for c in range(3):
        got[c * lent : c * lent + 1, :] = corner[c : c + 1, :]
    helps = jnp.logical_not(is_heavy(slab, slabs))
    line = lax.broadcasted_iota(jnp.int32, number.shape, 0)
    taken = (helps & ((lax.rem(line, rows) >= 1) | (line == rows))) | (line == 0)
    number = jnp.where(taken, number, 0.0)
    count = jnp.sum(jnp.where(number > 0.0, 1.0, 0.0), axis=1, keepdims=True).astype(jnp.int32)
    number = jnp.maximum(number - 1.0, 0.0).astype(jnp.int32)
    code_items(first, bits, placed, number, count, codes)


def prepared(kernel, lines, slots, depth, more, scratch, *operands):
    length = lines * slots + 2 * UNROLL
    return pl.pallas_call(
        kernel,
        out_shape=(
            jax.ShapeDtypeStruct((2 * length + 3,), jnp.int32),
            jax.ShapeDtypeStruct((lines * FEATS, depth), BF16),
            *more,
        ),
        in_specs=[vmem()] * len(operands),
        out_specs=(smem(), vmem()) + (vmem(),) * len(more),
        scratch_shapes=[
            pltpu.VMEM((lines, TILE), jnp.int32),
            pltpu.SMEM((lines, TILE), jnp.int32),
        ]
        + scratch
        + [pltpu.SemaphoreType.DMA],
        compiler_params=limited(4),
        cost_estimate=pl.CostEstimate(flops=0, bytes_accessed=8_000_000, transcendentals=0),
    )(*operands)


def add_items(bits, half, lists, table, feats, line_feat, tile_feat, modes, acc, squares, ready):
    tiles = table.shape[0] // ROWS
    at = 0
    for feat in feats:
        line_feat[at : at + feat.shape[0], :] = feat[...]
        at += feat.shape[0]
    line_feat[at:, :] = jnp.zeros((line_feat.shape[0] - at, line_feat.shape[1]), BF16)

    def build(t, carry):
        base = pl.multiple_of(t * ROWS, 8)
        rows = [spread(table, base + 8 * c) for c in range(3)]
        block = tile_block(rows)
        tile_feat[pl.ds(pl.multiple_of(t * TILE, TILE), TILE), :] = block.astype(BF16).T
        value = 4.0 * table[pl.ds(base, ROWS), :]
        high = value.astype(BF16)
        low = (value - high.astype(F32)).astype(BF16)
        at = pl.ds(pl.multiple_of(t * MIX, 16), MIX)
        modes[at, :] = jnp.concatenate([high, low], axis=0)
        return carry

    lax.fori_loop(0, tiles, build, 0, unroll=4)
    mask = tiles - 1
    ready()
    middles = [(items.shape[0] - 3) // 2 for items in lists]
    starts = [middle * half for middle in middles]
    first = lists[0][2 * middles[0] + half]
    count = sum(items[2 * middle + half] for items, middle in zip(lists, middles))

    def unpack(at):
        code = lists[0][starts[0] + jnp.minimum(at, first)]
        other = lists[1][starts[1] + jnp.maximum(at - first, 0)]
        code = jnp.where(at < first, code, other)
        return lax.shift_right_logical(code & 0xFFFF, bits), code & mask

    def distances(u, at):
        line, tile = unpack(at)
        squares[u][...] = jnp.dot(
            tile_feat[pl.ds(pl.multiple_of(tile * TILE, TILE), TILE), :],
            line_feat[pl.ds(pl.multiple_of(line * FEATS, FEATS), FEATS), :],
            preferred_element_type=F32,
        )

    def gather(u, at):
        line, tile = unpack(at)
        square = jnp.maximum(squares[u][...], TINY)
        near = jnp.maximum(1.0 - square * lax.rsqrt(square), 0.0)
        fourth = near * near
        fourth = fourth * fourth
        phi = fourth * (1.25 - near)
        high = phi.astype(BF16)
        low = (phi - high.astype(F32)).astype(BF16)
        mode = modes[pl.ds(pl.multiple_of(tile * MIX, 16), MIX), :]
        got = jnp.dot(
            jnp.concatenate([mode, mode], axis=1),
            jnp.concatenate([high, low], axis=0),
            preferred_element_type=F32,
        )
        where = pl.ds(pl.multiple_of(line * ROWS, 8), ROWS)
        acc[where, :] = acc[where, :] + (got[0:ROWS] + got[ROWS:MIX])

    def body(j, carry):
        base = j * UNROLL
        for u in range(UNROLL):
            gather(u, base + u)
            distances(u, base + UNROLL + u)
        return carry

    for u in range(UNROLL):
        distances(u, u)
    lax.fori_loop(0, lax.div(count + (UNROLL - 1), jnp.int32(UNROLL)), body, 0)


def load_sum(table):
    tiles = table.shape[0] // ROWS
    return jnp.sum(table[pl.ds(7, tiles, stride=ROWS), :], axis=0, keepdims=True)


def early_kernel(own, rows, slots, lent, bits, placed, units, bases, *refs):
    own_items, own_feat, *refs = refs
    gots, refs = refs[: len(units)], refs[len(units) :]
    corner, table, acc, loads, items, lent_feat, *refs = refs
    line_feat, tile_feat, modes, codes, listed, got, sem, *squares = refs
    read_lent(own, rows, slots, lent, bits, placed, units, bases, gots, corner, got, codes)
    copy = pltpu.make_async_copy(codes, listed, sem)
    copy.start()
    line_features(lent, got, lent_feat)
    acc[...] = jnp.zeros(acc.shape, F32)
    loads[...] = load_sum(table)

    def ready():
        copy.wait()
        build_lists(lent, slots, bits, own, listed, items)

    add_items(
        bits, 0, (own_items, items), table, (own_feat, lent_feat),
        line_feat, tile_feat, modes, acc, squares, ready,
    )


def late_kernel(own, lent, parts, bits, *refs):
    lists, feats = refs[:parts], refs[parts : 2 * parts]
    table, early, loads, points, corner, motion, inverse, *rest = refs[2 * parts :]
    out_own, out_extra, out_state, out_row, out_plane, *rest = rest
    line_feat, tile_feat, modes, acc, *squares = rest
    total = loads[...] + load_sum(table)
    lane = lax.broadcasted_iota(jnp.int32, (1, 128), 1)
    gravity = jnp.zeros((1, 128), F32)
    for k, pull in enumerate(GRAVITY):
        gravity = jnp.where(lane == k, pull, gravity)
    acceleration = inverse[...] * total + gravity
    out_state[...] = motion[...] + TIME_STEP * acceleration
    step = TIME_STEP * motion[...] + 0.5 * TIME_STEP * TIME_STEP * acceleration
    row = lax.broadcasted_iota(jnp.int32, (8, 128), 0)
    lane = lax.broadcasted_iota(jnp.int32, (8, 128), 1)
    chosen = jnp.where((lane == row - 1) & (lane < 6), jnp.broadcast_to(step, (8, 128)), 0.0)
    weight = jnp.broadcast_to(jnp.sum(chosen, axis=1, keepdims=True), (8, 128))

    acc[...] = early[...]
    add_items(
        bits, 1, lists, table, feats, line_feat, tile_feat, modes, acc, squares, lambda: None
    )

    def finish(count, first, out):
        def one(l, carry):
            base = pl.multiple_of((first + l) * ROWS, 8)
            for c in range(3):
                value = jnp.sum(weight * acc[pl.ds(base + 8 * c, 8), :], axis=0, keepdims=True)
                out[pl.ds(c * count + l, 1), :] = value
            return carry

        lax.fori_loop(0, count, one, 0, unroll=4)

    finish(own, 0, out_own)
    finish(lent, own, out_extra)
    rows = out_row.shape[1] // 3
    wide = own // rows
    for c in range(3):
        old = points[c * own : c * own + wide, :]
        out_plane[0, c * wide : (c + 1) * wide, :] = old
        out_plane[1, c * wide : (c + 1) * wide, :] = old + out_own[c * own : c * own + wide, :]
        old = points[pl.ds(c * own, rows, stride=wide), :]
        out_row[0, c * rows : (c + 1) * rows, :] = old
        out_row[1, c * rows : (c + 1) * rows, :] = (
            old + out_own[pl.ds(c * own, rows, stride=wide), :]
        )
    out_plane[0, 3 * wide :, :] = corner[...]
    out_plane[1, 3 * wide :, :] = corner[...]
    for c in range(3):
        at = slice(3 * wide + c, 3 * wide + c + 1)
        out_plane[1, at, :] = corner[c : c + 1, :] + out_extra[c * lent : c * lent + 1, :]


def volume_kernel(
    keep, share, points, shift, *refs
):
    *backs, plane_halo, row_halo, out_shift, out_volume, out_change = refs
    planes, rows, depth = points.shape[1:]
    slab, ctrl = lax.axis_index("slab"), lax.axis_index("ctrl")
    slabs, ctrls = lax.axis_size("slab"), lax.axis_size("ctrl")
    row_id = lax.broadcasted_iota(jnp.int32, (rows, depth), 0)
    lane = lax.broadcasted_iota(jnp.int32, (rows, depth), 1)
    inside = (lane < depth - 1) & (row_id + ctrl * rows < ctrls * rows - 1)
    if backs:
        from_helper = (row_id >= 1) & is_heavy(slab, slabs)
    last_row = row_id == rows - 1

    def next_row(value, edge):
        return jnp.where(last_row, edge, pltpu.roll(value, rows - 1, 0))

    def next_depth(value):
        return pltpu.roll(value, depth - 1, 1)

    def level(x):
        found = []
        for field in range(2):
            parts = []
            for c in range(3):
                if x == planes:
                    here = plane_halo[field, c * rows : (c + 1) * rows, :]
                    edge = plane_halo[field, 3 * rows + c : 3 * rows + c + 1, :]
                else:
                    here = points[c, x]
                    if field == 1:
                        moved = shift[c, x]
                        if backs and x >= keep:
                            back = backs[(x - keep) // share]
                            moved = jnp.where(from_helper, back[c, (x - keep) % share], moved)
                        if x == 1:
                            for turn, back in enumerate(backs):
                                here_too = from_helper & (row_id == 1 + turn)
                                moved = jnp.where(here_too, back[c, 1, 0:1, :], moved)
                        out_shift[c, x] = moved
                        here = here + moved
                    edge = row_halo[field, c, x : x + 1, :]
                there = next_row(here, edge)
                parts.append((here + there, there - here))
            found.append(parts)
        return found

    before = level(0)
    for x in range(planes):
        after = level(x + 1)
        volumes = []
        for field in range(2):
            edges = []
            for c in range(3):
                both0, step0 = before[field][c]
                both1, step1 = after[field][c]
                along, across, total = both1 - both0, step0 + step1, both0 + both1
                edges.append(
                    (
                        0.25 * (along + next_depth(along)),
                        0.25 * (across + next_depth(across)),
                        0.25 * (next_depth(total) - total),
                    )
                )
            ex, ey, ez = zip(*edges)
            volumes.append(
                ex[0] * (ey[1] * ez[2] - ey[2] * ez[1])
                + ex[1] * (ey[2] * ez[0] - ey[0] * ez[2])
                + ex[2] * (ey[0] * ez[1] - ey[1] * ez[0])
            )
        live = inside & (slab * planes + x < slabs * planes - 1)
        out_volume[x] = jnp.where(live, volumes[1], 0.0)
        out_change[x] = jnp.where(live, volumes[1] - volumes[0], 0.0)
        before = after


def is_heavy(slab, slabs):
    return (8 * slab >= 3 * slabs) & (8 * slab < 5 * slabs)


def local(
    face_pressure,
    face_area,
    face_center,
    motion,
    inverse_mass,
    control_points,
    control_modes,
    node_points,
    tile_list,
    tile_count,
):
    slabs, ctrls = lax.axis_size("slab"), lax.axis_size("ctrl")
    slab, ctrl = lax.axis_index("slab"), lax.axis_index("ctrl")
    _, planes, rows, depth = node_points.shape
    slots = tile_list.shape[2]
    own = planes * rows
    columns = control_points.shape[1]
    tiles = columns * slabs * ctrls // TILE
    bits = max(1, (tiles - 1).bit_length())
    pressure = face_pressure.reshape(1, -1)

    unit = slabs // 8
    share = (planes - 1) // 3
    keep = planes - 3 * share
    lend = slabs % 8 == 0 and slabs & (slabs - 1) == 0 and share > 1 and keep > 1 and rows > 4
    assert lend and share <= 3 and rows * slots <= TILE, (slabs, planes, rows, slots)
    units = (4 * unit, 2 * unit, unit) if lend else ()
    spans = [tuple(range(keep + g * share, keep + (g + 1) * share)) for g in range(len(units))]
    lent = share * rows if lend else 0
    heavy = [s for s in range(slabs) if is_heavy(s, slabs)]

    direct = columns % TILE == 0 and slabs & (slabs - 1) == 0 and ctrls & (ctrls - 1) == 0
    direct = direct and ctrls > 1 and (columns // TILE) & (columns // TILE - 1) == 0
    own_tiles = columns // TILE
    order = []
    bit = slabs // 2
    while bit:
        order.append((bit, 0))
        bit //= 2
    bit = 1
    while bit < ctrls:
        order.append((0, bit))
        bit *= 2

    def placed(number):
        if not direct:
            return number
        device = lax.axis_index("slab") * ctrls + lax.axis_index("ctrl")
        apart = (number >> (own_tiles.bit_length() - 1)) ^ device
        at = jnp.zeros(number.shape, jnp.int32)
        for turn, (slab_bit, ctrl_bit) in enumerate(order):
            flag = slab_bit * ctrls + ctrl_bit
            at = at + jnp.where((apart & flag) != 0, own_tiles << turn, 0)
        return at + (number & (own_tiles - 1))

    flat_points = node_points.reshape(3 * own, depth)
    *own_lists, last_sent = prepared(
        functools.partial(own_kernel, keep, len(units), bits, placed, spans[-1]),
        own, slots, depth, [jax.ShapeDtypeStruct((3 * lent, TILE), F32)], [],
        flat_points, tile_list, tile_count,
    )

    gots, bases = [], []
    if direct:
        size = own_tiles * ROWS
        corner, first, *sents = pl.pallas_call(
            functools.partial(pack_kernel, spans[:-1]),
            out_shape=[
                jax.ShapeDtypeStruct((rows_of, TILE), F32)
                for rows_of in [8, size + 3 * lent] + [3 * lent] * (len(units) - 2)
            ],
            in_specs=[vmem()] * 8,
            out_specs=[vmem()] * len(units),
            compiler_params=limited(56),
        )(
            pressure, face_area, face_center, control_points, control_modes,
            flat_points, tile_list, tile_count,
        )
        sents.append(last_sent)
        early = first[:size]
        corner = shifted_back(corner, "ctrl")
        for turn, (slab_bit, ctrl_bit) in enumerate(order[:-1]):
            size = early.shape[0]
            if turn == 2:
                early, own_lists, sents[-1] = lax.optimization_barrier(
                    (early, own_lists, sents[-1])
                )
            if turn == 3:
                early, corner = lax.optimization_barrier((early, corner))
            if lend and slab_bit in units:
                payload = jnp.concatenate([early, sents[len(gots) - 1]], axis=0) if gots else first
                reply = swapped(payload, slab_bit, ctrl_bit)
                gots.append(reply)
                bases.append(size)
                reply = reply[:size]
            else:
                reply = swapped(early, slab_bit, ctrl_bit)
            early = jnp.concatenate([early, reply], axis=0)
        late = swapped(early, *order[-1])
    else:
        loads = pl.pallas_call(
            loads_kernel,
            out_shape=jax.ShapeDtypeStruct((1, TILE), F32),
            in_specs=[vmem()] * 3,
            out_specs=vmem(),
        )(pressure, face_area, face_center)
        loads = lax.psum(loads, ("slab", "ctrl"))
        whole = jnp.concatenate([control_points, control_modes], axis=0)
        whole = lax.all_gather(whole, ("slab", "ctrl"), axis=1, tiled=True)
        whole = whole.reshape(7, 3, tiles, TILE).transpose(2, 1, 0, 3)
        spare = jnp.zeros((tiles, 3, 1, TILE), F32).at[0, 0, 0, :].set(loads[0])
        table = jnp.concatenate([whole, spare], axis=2).reshape(tiles * ROWS, TILE)
        early, late = table[: tiles // 2 * ROWS], table[tiles // 2 * ROWS :]
        corner, *sents = pl.pallas_call(
            functools.partial(lend_kernel, spans),
            out_shape=[jax.ShapeDtypeStruct((8, TILE), F32)]
            + [jax.ShapeDtypeStruct((3 * lent, TILE), F32)] * len(units),
            in_specs=[vmem()] * 3,
            out_specs=[vmem()] * (1 + len(units)),
        )(flat_points, tile_list, tile_count)
        corner = shifted_back(corner, "ctrl")
        gots = [swapped(sent, bit, 0) for sent, bit in zip(sents, units)]
        bases = [0] * len(units)
    lines = own + lent

    def wide(value):
        return jnp.pad(value, (0, TILE - value.shape[0])).reshape(1, TILE)

    half = tiles // 2
    length = lent * slots + 2 * UNROLL
    scratch = [
        pltpu.VMEM(((lines + 1) * FEATS, depth), BF16),
        pltpu.VMEM((half * TILE, FEATS), BF16),
        pltpu.VMEM((half * MIX, TILE), BF16),
    ]
    squares = [pltpu.VMEM((TILE, depth), F32)] * UNROLL
    partial, part_loads, *lent_lists = pl.pallas_call(
        functools.partial(
            early_kernel, own, rows, slots, lent, bits, placed, units, tuple(bases)
        ),
        out_shape=(
            jax.ShapeDtypeStruct(((lines + 1) * ROWS, depth), F32),
            jax.ShapeDtypeStruct((1, TILE), F32),
            jax.ShapeDtypeStruct((2 * length + 3,), jnp.int32),
            jax.ShapeDtypeStruct((lent * FEATS, depth), BF16),
        ),
        in_specs=[smem()] + [vmem()] * (3 + len(units)),
        out_specs=(vmem(), vmem(), smem(), vmem()),
        scratch_shapes=scratch
        + [
            pltpu.VMEM((lent, TILE), jnp.int32),
            pltpu.SMEM((lent, TILE), jnp.int32),
            pltpu.VMEM((3 * lent, TILE), F32),
            pltpu.SemaphoreType.DMA,
        ]
        + squares,
        compiler_params=limited(16),
        cost_estimate=pl.CostEstimate(flops=0, bytes_accessed=30_000_000, transcendentals=0),
    )(*own_lists, *gots, corner, early)
    groups = [own_lists, lent_lists]
    parts = len(groups)
    lists = [group[0] for group in groups]
    feats = [group[1] for group in groups]
    list_specs = [smem()] * parts + [vmem()] * parts
    outs = pl.pallas_call(
        functools.partial(late_kernel, own, lent, parts, bits),
        out_shape=(
            jax.ShapeDtypeStruct((3 * own, depth), F32),
            jax.ShapeDtypeStruct((3 * max(lent, 8), depth), F32),
            jax.ShapeDtypeStruct((1, TILE), F32),
            jax.ShapeDtypeStruct((2, 3 * planes, depth), F32),
            jax.ShapeDtypeStruct((2, 3 * rows + 8, depth), F32),
        ),
        in_specs=list_specs + [vmem()] * 7,
        out_specs=(vmem(),) * 5,
        scratch_shapes=scratch + [pltpu.VMEM(((lines + 1) * ROWS, depth), F32)] + squares,
        compiler_params=limited(16),
    )(
        *lists, *feats, late, partial, part_loads, flat_points, corner,
        wide(motion), wide(inverse_mass),
    )
    shift, lent_shift, state, row_sent, plane_sent = outs

    backs = [
        lax.ppermute(lent_shift, "slab", [(h ^ bit, h) for h in heavy]).reshape(
            3, share, rows, depth
        )
        for bit in units
    ]
    plane_halo = shifted_back(plane_sent, "slab")
    row_halo = shifted_back(row_sent, "ctrl").reshape(2, 3, planes, depth)
    node_shift, volume, change = pl.pallas_call(
        functools.partial(volume_kernel, keep, share),
        out_shape=(
            jax.ShapeDtypeStruct(node_points.shape, F32),
            jax.ShapeDtypeStruct(node_points.shape[1:], F32),
            jax.ShapeDtypeStruct(node_points.shape[1:], F32),
        ),
        in_specs=[vmem()] * (4 + len(backs)),
        out_specs=(vmem(),) * 3,
        compiler_params=limited(8),
    )(node_points, shift.reshape(3, planes, rows, depth), *backs, plane_halo, row_halo)
    return node_shift, volume, change, state[0, : motion.shape[0]]


def solution(mesh):
    placed = (
        P(("slab", "ctrl")),
        P(None, ("slab", "ctrl")),
        P(None, ("slab", "ctrl")),
        P(),
        P(),
        P(None, ("slab", "ctrl")),
        P(None, ("slab", "ctrl")),
        P(None, "slab", "ctrl", None),
        P("slab", "ctrl", None),
        P("slab", "ctrl"),
    )
    return jax.shard_map(
        local,
        mesh=mesh,
        in_specs=placed,
        out_specs=(
            P(None, "slab", "ctrl", None),
            P("slab", "ctrl", None),
            P("slab", "ctrl", None),
            P(),
        ),
        check_vma=False,
    )
```

```python
import functools
import jax
import jax.numpy as jnp
from jax import lax
from jax.experimental import pallas as pl
from jax.experimental.pallas import tpu as pltpu
from jax.sharding import PartitionSpec as P

TILE = 128
TIME_STEP = 0.5
RADIUS = 4.0
GRAVITY = (0.0, 0.0, -0.5, 0.0, 0.0, 0.0)
ROWS = 24
FEATS = 32
UNROLL = 20
MIX = 48
TINY = 1e-30
F32 = jnp.float32
BF16 = jnp.bfloat16


def limited(mib):
    return pltpu.CompilerParams(vmem_limit_bytes=mib << 20)


def vmem():
    return pl.BlockSpec(memory_space=pltpu.VMEM)


def smem():
    return pl.BlockSpec(memory_space=pltpu.SMEM)


def swapped(value, slab_bit, ctrl_bit):
    slabs, ctrls = lax.axis_size("slab"), lax.axis_size("ctrl")
    pairs = [
        (s * ctrls + c, (s ^ slab_bit) * ctrls + (c ^ ctrl_bit))
        for s in range(slabs)
        for c in range(ctrls)
    ]
    return lax.ppermute(value, ("slab", "ctrl"), pairs)


def shifted_back(value, axis):
    return lax.ppermute(value, axis, [(i, i - 1) for i in range(1, lax.axis_size(axis))])


def load_rows(pressure, area, center):
    pushed = pressure * area

    def turned(value, by):
        return jnp.concatenate([value[by:3], value[0:by]], axis=0)

    moment = turned(center, 1) * turned(pushed, 2) - turned(center, 2) * turned(pushed, 1)
    sums = [jnp.sum(pushed, axis=1, keepdims=True), jnp.sum(moment, axis=1, keepdims=True)]
    lane = lax.broadcasted_iota(jnp.int32, (1, 128), 1)
    row = jnp.zeros((1, 128), F32)
    for k in range(6):
        row = jnp.where(lane == k, sums[k // 3][k % 3 : k % 3 + 1, :], row)
    return row


def pack_table(row, points, modes, out):
    for t in range(points.shape[1] // TILE):
        span = slice(t * TILE, (t + 1) * TILE)
        base = t * ROWS
        for c in range(3):
            out[base + 8 * c : base + 8 * c + 1, :] = points[c : c + 1, span]
            for k in range(6):
                at = base + 8 * c + 1 + k
                out[at : at + 1, :] = modes[3 * k + c : 3 * k + c + 1, span]
            at = base + 8 * c + 7
            out[at : at + 1, :] = row if (t == 0 and c == 0) else jnp.zeros((1, 128), F32)


def count_column(counts, x):
    rows = counts.shape[1]
    row = lax.broadcasted_iota(jnp.int32, (rows, rows), 0)
    lane = lax.broadcasted_iota(jnp.int32, (rows, rows), 1)
    many = jnp.broadcast_to(counts[x : x + 1, :].astype(F32), (rows, rows))
    return jnp.sum(jnp.where(row == lane, many, 0.0), axis=1, keepdims=True)


def marked(numbers, counts, x):
    slot = lax.broadcasted_iota(jnp.int32, numbers.shape[1:], 1).astype(F32)
    return jnp.where(slot < count_column(counts, x), numbers[x].astype(F32) + 1.0, 0.0)


def pack_lent(planes, turn, base, nodes, numbers, counts, out):
    rows, slots = numbers.shape[1:]
    lent = len(planes) * rows
    for i, x in enumerate(planes):
        at = base + i * rows
        for c in range(3):
            first = (c * counts.shape[0] + x) * rows
            out[at + c * lent : at + c * lent + rows, :] = nodes[first : first + rows, :]
    at, y = base + rows, 1 + turn
    for c in range(3):
        first = (c * counts.shape[0] + 1) * rows + y
        out[at + c * lent : at + c * lent + 1, :] = nodes[first : first + 1, :]
    for i, x in enumerate(planes):
        listed = marked(numbers, counts, x)
        if i == 1:
            listed = jnp.concatenate([marked(numbers, counts, 1)[y : y + 1], listed[1:]], axis=0)
        at = base + i * lent
        for row in range(rows):
            out[at : at + 1, row * slots : (row + 1) * slots] = listed[row : row + 1]


def pack_corner(nodes, numbers, counts, out):
    slots = numbers.shape[2]
    out[...] = jnp.zeros(out.shape, F32)
    for c in range(3):
        first = c * counts.shape[0] * counts.shape[1]
        out[c : c + 1, :] = nodes[first : first + 1, :]
    out[3:4, 0:slots] = marked(numbers, counts, 0)[0:1]


def pack_kernel(
    spans, pressure, area, center, points, modes, nodes, numbers, counts, corner, out, *lents
):
    row = load_rows(pressure[...], area[...], center[...])
    pack_table(row, points, modes, out)
    pack_corner(nodes, numbers, counts, corner)
    pack_lent(spans[0], 0, points.shape[1] // TILE * ROWS, nodes, numbers, counts, out)
    for turn, (span, lent) in enumerate(zip(spans[1:], lents)):
        pack_lent(span, turn + 1, 0, nodes, numbers, counts, lent)


def lend_kernel(spans, nodes, numbers, counts, corner, *outs):
    pack_corner(nodes, numbers, counts, corner)
    for turn, (span, out) in enumerate(zip(spans, outs)):
        pack_lent(span, turn, 0, nodes, numbers, counts, out)


def loads_kernel(pressure, area, center, out):
    out[...] = load_rows(pressure[...], area[...], center[...])


def split3(value):
    first = value.astype(BF16).astype(F32)
    rest = value - first
    second = rest.astype(BF16).astype(F32)
    return first, second, rest - second


def spread(ref, at):
    return jnp.broadcast_to(ref[pl.ds(at, 1), :], (8, ref.shape[1]))


def products(rows, scale, order, ends):
    row = lax.broadcasted_iota(jnp.int32, rows[0].shape, 0)
    norm = jnp.zeros(rows[0].shape, F32)
    blocks = []
    for value in rows:
        place = value * (1.0 / RADIUS)
        norm = norm + place * place
        first, second, third = split3(place * scale)
        low = jnp.where((row & 1) == 1, order[1](first, second, third, row), order[0](first, second, third, row))
        blocks.append(low)
    first, second, third = split3(norm)
    blocks.append(ends(first, second, third, row))
    return jnp.concatenate(blocks, axis=0)


def tile_block(rows):
    return products(
        rows,
        -2.0,
        (
            lambda a, b, c, row: jnp.where((row == 2) | (row == 6), b, a),
            lambda a, b, c, row: jnp.where(row == 1, a, jnp.where(row == 3, b, c)),
        ),
        lambda a, b, c, row: jnp.where(
            row == 0, a, jnp.where(row == 1, b, jnp.where(row == 2, c, jnp.where(row < 6, 1.0, 0.0)))
        ),
    )


def line_block(rows):
    return products(
        rows,
        1.0,
        (
            lambda a, b, c, row: jnp.where(row < 4, a, c),
            lambda a, b, c, row: jnp.where(row == 5, a, b),
        ),
        lambda a, b, c, row: jnp.where(
            row < 3, 1.0, jnp.where(row == 3, a, jnp.where(row == 4, b, jnp.where(row == 5, c, 0.0)))
        ),
    )


def build_lists(lines, slots, bits, first, listed, items):
    few = min(4, slots)
    middle = lines * slots + 2 * UNROLL

    def take(line, low, high):
        for e in range(low, high):
            value = listed[line, e]
            items[lax.shift_right_logical(value, 16)] = value

    def one(line, carry):
        take(line, 0, few)

        def rest(step, carry):
            take(line, few, slots)
            return carry

        return lax.fori_loop(0, jnp.where(listed[line, slots] > few, 1, 0), rest, carry)

    lax.fori_loop(0, lines, one, 0)
    end_a, end_b = listed[0, slots + 1], listed[0, slots + 2]
    for e in range(2 * UNROLL):
        items[end_a + e] = (first + lines) << bits
        items[middle + end_b + e] = (first + lines) << bits
    items[2 * middle] = end_a
    items[2 * middle + 1] = end_b


def line_features(lines, points, line_feat):
    def block(l, carry):
        rows = [spread(points, c * lines + l) for c in range(3)]
        at = pl.ds(pl.multiple_of(l * FEATS, FEATS), FEATS)
        line_feat[at, :] = line_block(rows).astype(BF16)
        return carry

    lax.fori_loop(0, lines, block, 0, unroll=4)


def code_items(first, bits, placed, numbers, counts, codes):
    lines, slots = numbers.shape
    row = lax.broadcasted_iota(jnp.int32, (lines, slots), 0)
    slot = lax.broadcasted_iota(jnp.int32, (lines, slots), 1)
    code = lax.shift_left(row + first, jnp.full_like(row, bits)) + placed(numbers)
    late = lax.shift_right_logical(code, jnp.full_like(row, bits - 1)) & 1
    middle = lines * slots + 2 * UNROLL
    high = lax.broadcasted_iota(jnp.int32, (slots, slots), 0)
    wide = lax.broadcasted_iota(jnp.int32, (slots, slots), 1)
    before = jnp.where(high < wide, 1.0, 0.0).astype(BF16)
    high = lax.broadcasted_iota(jnp.int32, (lines, lines), 0)
    wide = lax.broadcasted_iota(jnp.int32, (lines, lines), 1)
    above = jnp.where(wide < high, 1.0, 0.0).astype(BF16)
    place = jnp.full((lines, slots), 2 * middle + 2, jnp.int32)
    ends = []
    for part in range(2):
        chosen = (slot < counts) & (late == part)
        flag = jnp.where(chosen, 1.0, 0.0)
        total = jnp.broadcast_to(jnp.sum(flag, axis=1, keepdims=True), (lines, slots))
        at = jnp.dot(flag.astype(BF16), before, preferred_element_type=F32)
        at = at + jnp.dot(above, total.astype(BF16), preferred_element_type=F32)
        place = jnp.where(chosen, at.astype(jnp.int32) + part * middle, place)
        ends.append(jnp.sum(total[:, 0:1], axis=0, keepdims=True).astype(jnp.int32))
    codes[:, 0:slots] = lax.shift_left(place, jnp.full_like(place, 16)) | code
    codes[:, slots : slots + 1] = counts
    codes[0:1, slots + 1 : slots + 2] = ends[0]
    codes[0:1, slots + 2 : slots + 3] = ends[1]


def own_kernel(
    keep, turns, bits, placed, span, points, numbers, counts,
    items, line_feat, sent, codes, listed, sem,
):
    planes, rows, slots = numbers.shape
    pack_lent(span, turns - 1, 0, points, numbers, counts, sent)
    slabs = lax.axis_size("slab")
    lends = is_heavy(lax.axis_index("slab"), slabs)
    columns = []
    for x in range(planes):
        count = count_column(counts, x).astype(jnp.int32)
        if x >= keep:
            row = lax.broadcasted_iota(jnp.int32, count.shape, 0)
            count = jnp.where(lends & (row >= 1), 0, count)
        if x == 1:
            row = lax.broadcasted_iota(jnp.int32, count.shape, 0)
            count = jnp.where(lends & (row >= 1) & (row <= turns), 0, count)
        columns.append(count)
    number = jnp.concatenate([numbers[x] for x in range(planes)], axis=0)
    code_items(0, bits, placed, number, jnp.concatenate(columns, axis=0), codes)
    copy = pltpu.make_async_copy(codes, listed, sem)
    copy.start()
    line_features(planes * rows, points, line_feat)
    copy.wait()
    build_lists(planes * rows, slots, bits, 0, listed, items)


def read_lent(first, rows, slots, lent, bits, placed, units, bases, gots, corner, got, codes):
    slab, slabs = lax.axis_index("slab"), lax.axis_size("slab")
    value = gots[-1][pl.ds(bases[-1], 3 * lent), :]
    for unit, base, ref in list(zip(units, bases, gots))[:-1]:
        value = jnp.where(is_heavy(slab ^ unit, slabs), ref[pl.ds(base, 3 * lent), :], value)
    number = [
        value[i * lent : i * lent + 1, y * slots : (y + 1) * slots]
        for i in range(lent // rows)
        for y in range(rows)
    ]
    number = jnp.concatenate([corner[3:4, 0:slots]] + number[1:], axis=0)
    got[...] = value
    for c in range(3):
        got[c * lent : c * lent + 1, :] = corner[c : c + 1, :]
    helps = jnp.logical_not(is_heavy(slab, slabs))
    line = lax.broadcasted_iota(jnp.int32, number.shape, 0)
    taken = (helps & ((lax.rem(line, rows) >= 1) | (line == rows))) | (line == 0)
    number = jnp.where(taken, number, 0.0)
    count = jnp.sum(jnp.where(number > 0.0, 1.0, 0.0), axis=1, keepdims=True).astype(jnp.int32)
    number = jnp.maximum(number - 1.0, 0.0).astype(jnp.int32)
    code_items(first, bits, placed, number, count, codes)


def prepared(kernel, lines, slots, depth, more, scratch, *operands):
    length = lines * slots + 2 * UNROLL
    return pl.pallas_call(
        kernel,
        out_shape=(
            jax.ShapeDtypeStruct((2 * length + 3,), jnp.int32),
            jax.ShapeDtypeStruct((lines * FEATS, depth), BF16),
            *more,
        ),
        in_specs=[vmem()] * len(operands),
        out_specs=(smem(), vmem()) + (vmem(),) * len(more),
        scratch_shapes=[
            pltpu.VMEM((lines, TILE), jnp.int32),
            pltpu.SMEM((lines, TILE), jnp.int32),
        ]
        + scratch
        + [pltpu.SemaphoreType.DMA],
        compiler_params=limited(4),
        cost_estimate=pl.CostEstimate(flops=0, bytes_accessed=8_000_000, transcendentals=0),
    )(*operands)


def add_items(bits, half, lists, table, feats, line_feat, tile_feat, modes, acc, squares, ready):
    tiles = table.shape[0] // ROWS
    at = 0
    for feat in feats:
        line_feat[at : at + feat.shape[0], :] = feat[...]
        at += feat.shape[0]
    line_feat[at:, :] = jnp.zeros((line_feat.shape[0] - at, line_feat.shape[1]), BF16)

    def build(t, carry):
        base = pl.multiple_of(t * ROWS, 8)
        rows = [spread(table, base + 8 * c) for c in range(3)]
        block = tile_block(rows)
        tile_feat[pl.ds(pl.multiple_of(t * TILE, TILE), TILE), :] = block.astype(BF16).T
        value = 4.0 * table[pl.ds(base, ROWS), :]
        high = value.astype(BF16)
        low = (value - high.astype(F32)).astype(BF16)
        at = pl.ds(pl.multiple_of(t * MIX, 16), MIX)
        modes[at, :] = jnp.concatenate([high, low], axis=0)
        return carry

    lax.fori_loop(0, tiles, build, 0, unroll=4)
    mask = tiles - 1
    ready()
    middles = [(items.shape[0] - 3) // 2 for items in lists]
    starts = [middle * half for middle in middles]
    first = lists[0][2 * middles[0] + half]
    count = sum(items[2 * middle + half] for items, middle in zip(lists, middles))

    def unpack(at):
        code = lists[0][starts[0] + jnp.minimum(at, first)]
        other = lists[1][starts[1] + jnp.maximum(at - first, 0)]
        code = jnp.where(at < first, code, other)
        return lax.shift_right_logical(code & 0xFFFF, bits), code & mask

    def distances(u, at):
        line, tile = unpack(at)
        squares[u][...] = jnp.dot(
            tile_feat[pl.ds(pl.multiple_of(tile * TILE, TILE), TILE), :],
            line_feat[pl.ds(pl.multiple_of(line * FEATS, FEATS), FEATS), :],
            preferred_element_type=F32,
        )

    def gather(u, at):
        line, tile = unpack(at)
        square = jnp.maximum(squares[u][...], TINY)
        near = jnp.maximum(1.0 - square * lax.rsqrt(square), 0.0)
        fourth = near * near
        fourth = fourth * fourth
        phi = fourth * (1.25 - near)
        high = phi.astype(BF16)
        low = (phi - high.astype(F32)).astype(BF16)
        mode = modes[pl.ds(pl.multiple_of(tile * MIX, 16), MIX), :]
        got = jnp.dot(
            jnp.concatenate([mode, mode], axis=1),
            jnp.concatenate([high, low], axis=0),
            preferred_element_type=F32,
        )
        where = pl.ds(pl.multiple_of(line * ROWS, 8), ROWS)
        acc[where, :] = acc[where, :] + (got[0:ROWS] + got[ROWS:MIX])

    def body(j, carry):
        base = j * UNROLL
        for u in range(UNROLL):
            gather(u, base + u)
            distances(u, base + UNROLL + u)
        return carry

    for u in range(UNROLL):
        distances(u, u)
    lax.fori_loop(0, lax.div(count + (UNROLL - 1), jnp.int32(UNROLL)), body, 0)


def load_sum(table):
    tiles = table.shape[0] // ROWS
    return jnp.sum(table[pl.ds(7, tiles, stride=ROWS), :], axis=0, keepdims=True)


def early_kernel(own, rows, slots, lent, bits, placed, units, bases, *refs):
    own_items, own_feat, *refs = refs
    gots, refs = refs[: len(units)], refs[len(units) :]
    corner, table, acc, loads, items, lent_feat, *refs = refs
    line_feat, tile_feat, modes, codes, listed, got, sem, *squares = refs
    read_lent(own, rows, slots, lent, bits, placed, units, bases, gots, corner, got, codes)
    copy = pltpu.make_async_copy(codes, listed, sem)
    copy.start()
    line_features(lent, got, lent_feat)
    acc[...] = jnp.zeros(acc.shape, F32)
    loads[...] = load_sum(table)

    def ready():
        copy.wait()
        build_lists(lent, slots, bits, own, listed, items)

    add_items(
        bits, 0, (own_items, items), table, (own_feat, lent_feat),
        line_feat, tile_feat, modes, acc, squares, ready,
    )


def late_kernel(own, lent, parts, bits, *refs):
    lists, feats = refs[:parts], refs[parts : 2 * parts]
    table, early, loads, points, corner, motion, inverse, *rest = refs[2 * parts :]
    out_own, out_extra, out_state, out_row, out_plane, *rest = rest
    line_feat, tile_feat, modes, acc, *squares = rest
    total = loads[...] + load_sum(table)
    lane = lax.broadcasted_iota(jnp.int32, (1, 128), 1)
    gravity = jnp.zeros((1, 128), F32)
    for k, pull in enumerate(GRAVITY):
        gravity = jnp.where(lane == k, pull, gravity)
    acceleration = inverse[...] * total + gravity
    out_state[...] = motion[...] + TIME_STEP * acceleration
    step = TIME_STEP * motion[...] + 0.5 * TIME_STEP * TIME_STEP * acceleration
    acc[...] = early[...]
    add_items(
        bits, 1, lists, table, feats, line_feat, tile_feat, modes, acc, squares, lambda: None
    )

    def finish(count, first, out):
        for c in range(3):
            value = jnp.zeros((count, out.shape[1]), F32)
            for k in range(6):
                at = first * ROWS + 8 * c + 1 + k
                value = value + step[:, k : k + 1] * acc[pl.ds(at, count, stride=ROWS), :]
            out[c * count : (c + 1) * count, :] = value

    finish(own, 0, out_own)
    finish(lent, own, out_extra)
    rows = out_row.shape[1] // 3
    wide = own // rows
    for c in range(3):
        old = points[c * own : c * own + wide, :]
        out_plane[0, c * wide : (c + 1) * wide, :] = old
        out_plane[1, c * wide : (c + 1) * wide, :] = old + out_own[c * own : c * own + wide, :]
        old = points[pl.ds(c * own, rows, stride=wide), :]
        out_row[0, c * rows : (c + 1) * rows, :] = old
        out_row[1, c * rows : (c + 1) * rows, :] = (
            old + out_own[pl.ds(c * own, rows, stride=wide), :]
        )
    out_plane[0, 3 * wide :, :] = corner[...]
    out_plane[1, 3 * wide :, :] = corner[...]
    for c in range(3):
        at = slice(3 * wide + c, 3 * wide + c + 1)
        out_plane[1, at, :] = corner[c : c + 1, :] + out_extra[c * lent : c * lent + 1, :]


def volume_kernel(
    keep, share, points, shift, *refs
):
    *backs, plane_halo, row_halo, out_shift, out_volume, out_change = refs
    planes, rows, depth = points.shape[1:]
    slab, ctrl = lax.axis_index("slab"), lax.axis_index("ctrl")
    slabs, ctrls = lax.axis_size("slab"), lax.axis_size("ctrl")
    row_id = lax.broadcasted_iota(jnp.int32, (rows, depth), 0)
    lane = lax.broadcasted_iota(jnp.int32, (rows, depth), 1)
    inside = (lane < depth - 1) & (row_id + ctrl * rows < ctrls * rows - 1)
    if backs:
        from_helper = (row_id >= 1) & is_heavy(slab, slabs)
    last_row = row_id == rows - 1

    def next_row(value, edge):
        return jnp.where(last_row, edge, pltpu.roll(value, rows - 1, 0))

    def next_depth(value):
        return pltpu.roll(value, depth - 1, 1)

    def level(x):
        found = []
        for field in range(2):
            parts = []
            for c in range(3):
                if x == planes:
                    here = plane_halo[field, c * rows : (c + 1) * rows, :]
                    edge = plane_halo[field, 3 * rows + c : 3 * rows + c + 1, :]
                else:
                    here = points[c, x]
                    if field == 1:
                        moved = shift[c, x]
                        if backs and x >= keep:
                            back = backs[(x - keep) // share]
                            moved = jnp.where(from_helper, back[c, (x - keep) % share], moved)
                        if x == 1:
                            for turn, back in enumerate(backs):
                                here_too = from_helper & (row_id == 1 + turn)
                                moved = jnp.where(here_too, back[c, 1, 0:1, :], moved)
                        out_shift[c, x] = moved
                        here = here + moved
                    edge = row_halo[field, c, x : x + 1, :]
                there = next_row(here, edge)
                parts.append((here + there, there - here))
            found.append(parts)
        return found

    before = level(0)
    for x in range(planes):
        after = level(x + 1)
        volumes = []
        for field in range(2):
            edges = []
            for c in range(3):
                both0, step0 = before[field][c]
                both1, step1 = after[field][c]
                along, across, total = both1 - both0, step0 + step1, both0 + both1
                edges.append(
                    (
                        0.25 * (along + next_depth(along)),
                        0.25 * (across + next_depth(across)),
                        0.25 * (next_depth(total) - total),
                    )
                )
            ex, ey, ez = zip(*edges)
            volumes.append(
                ex[0] * (ey[1] * ez[2] - ey[2] * ez[1])
                + ex[1] * (ey[2] * ez[0] - ey[0] * ez[2])
                + ex[2] * (ey[0] * ez[1] - ey[1] * ez[0])
            )
        live = inside & (slab * planes + x < slabs * planes - 1)
        out_volume[x] = jnp.where(live, volumes[1], 0.0)
        out_change[x] = jnp.where(live, volumes[1] - volumes[0], 0.0)
        before = after


def is_heavy(slab, slabs):
    return (8 * slab >= 3 * slabs) & (8 * slab < 5 * slabs)


def local(
    face_pressure,
    face_area,
    face_center,
    motion,
    inverse_mass,
    control_points,
    control_modes,
    node_points,
    tile_list,
    tile_count,
):
    slabs, ctrls = lax.axis_size("slab"), lax.axis_size("ctrl")
    slab, ctrl = lax.axis_index("slab"), lax.axis_index("ctrl")
    _, planes, rows, depth = node_points.shape
    slots = tile_list.shape[2]
    own = planes * rows
    columns = control_points.shape[1]
    tiles = columns * slabs * ctrls // TILE
    bits = max(1, (tiles - 1).bit_length())
    pressure = face_pressure.reshape(1, -1)

    unit = slabs // 8
    share = (planes - 1) // 3
    keep = planes - 3 * share
    lend = slabs % 8 == 0 and slabs & (slabs - 1) == 0 and share > 1 and keep > 1 and rows > 4
    assert lend and share <= 3 and rows * slots <= TILE, (slabs, planes, rows, slots)
    units = (4 * unit, 2 * unit, unit) if lend else ()
    spans = [tuple(range(keep + g * share, keep + (g + 1) * share)) for g in range(len(units))]
    lent = share * rows if lend else 0
    heavy = [s for s in range(slabs) if is_heavy(s, slabs)]

    direct = columns % TILE == 0 and slabs & (slabs - 1) == 0 and ctrls & (ctrls - 1) == 0
    direct = direct and ctrls > 1 and (columns // TILE) & (columns // TILE - 1) == 0
    own_tiles = columns // TILE
    order = []
    bit = slabs // 2
    while bit:
        order.append((bit, 0))
        bit //= 2
    bit = 1
    while bit < ctrls:
        order.append((0, bit))
        bit *= 2

    def placed(number):
        if not direct:
            return number
        device = lax.axis_index("slab") * ctrls + lax.axis_index("ctrl")
        apart = (number >> (own_tiles.bit_length() - 1)) ^ device
        at = jnp.zeros(number.shape, jnp.int32)
        for turn, (slab_bit, ctrl_bit) in enumerate(order):
            flag = slab_bit * ctrls + ctrl_bit
            at = at + jnp.where((apart & flag) != 0, own_tiles << turn, 0)
        return at + (number & (own_tiles - 1))

    flat_points = node_points.reshape(3 * own, depth)
    *own_lists, last_sent = prepared(
        functools.partial(own_kernel, keep, len(units), bits, placed, spans[-1]),
        own, slots, depth, [jax.ShapeDtypeStruct((3 * lent, TILE), F32)], [],
        flat_points, tile_list, tile_count,
    )

    gots, bases = [], []
    if direct:
        size = own_tiles * ROWS
        corner, first, *sents = pl.pallas_call(
            functools.partial(pack_kernel, spans[:-1]),
            out_shape=[
                jax.ShapeDtypeStruct((rows_of, TILE), F32)
                for rows_of in [8, size + 3 * lent] + [3 * lent] * (len(units) - 2)
            ],
            in_specs=[vmem()] * 8,
            out_specs=[vmem()] * len(units),
            compiler_params=limited(56),
        )(
            pressure, face_area, face_center, control_points, control_modes,
            flat_points, tile_list, tile_count,
        )
        sents.append(last_sent)
        early = first[:size]
        corner = shifted_back(corner, "ctrl")
        for turn, (slab_bit, ctrl_bit) in enumerate(order[:-1]):
            size = early.shape[0]
            if turn == 2:
                early, own_lists, sents[-1] = lax.optimization_barrier(
                    (early, own_lists, sents[-1])
                )
            if turn == 3:
                early, corner = lax.optimization_barrier((early, corner))
            if lend and slab_bit in units:
                payload = jnp.concatenate([early, sents[len(gots) - 1]], axis=0) if gots else first
                reply = swapped(payload, slab_bit, ctrl_bit)
                gots.append(reply)
                bases.append(size)
                reply = reply[:size]
            else:
                reply = swapped(early, slab_bit, ctrl_bit)
            early = jnp.concatenate([early, reply], axis=0)
        late = swapped(early, *order[-1])
    else:
        loads = pl.pallas_call(
            loads_kernel,
            out_shape=jax.ShapeDtypeStruct((1, TILE), F32),
            in_specs=[vmem()] * 3,
            out_specs=vmem(),
        )(pressure, face_area, face_center)
        loads = lax.psum(loads, ("slab", "ctrl"))
        whole = jnp.concatenate([control_points, control_modes], axis=0)
        whole = lax.all_gather(whole, ("slab", "ctrl"), axis=1, tiled=True)
        whole = whole.reshape(7, 3, tiles, TILE).transpose(2, 1, 0, 3)
        spare = jnp.zeros((tiles, 3, 1, TILE), F32).at[0, 0, 0, :].set(loads[0])
        table = jnp.concatenate([whole, spare], axis=2).reshape(tiles * ROWS, TILE)
        early, late = table[: tiles // 2 * ROWS], table[tiles // 2 * ROWS :]
        corner, *sents = pl.pallas_call(
            functools.partial(lend_kernel, spans),
            out_shape=[jax.ShapeDtypeStruct((8, TILE), F32)]
            + [jax.ShapeDtypeStruct((3 * lent, TILE), F32)] * len(units),
            in_specs=[vmem()] * 3,
            out_specs=[vmem()] * (1 + len(units)),
        )(flat_points, tile_list, tile_count)
        corner = shifted_back(corner, "ctrl")
        gots = [swapped(sent, bit, 0) for sent, bit in zip(sents, units)]
        bases = [0] * len(units)
    lines = own + lent

    def wide(value):
        return jnp.pad(value, (0, TILE - value.shape[0])).reshape(1, TILE)

    half = tiles // 2
    length = lent * slots + 2 * UNROLL
    scratch = [
        pltpu.VMEM(((lines + 1) * FEATS, depth), BF16),
        pltpu.VMEM((half * TILE, FEATS), BF16),
        pltpu.VMEM((half * MIX, TILE), BF16),
    ]
    squares = [pltpu.VMEM((TILE, depth), F32)] * UNROLL
    partial, part_loads, *lent_lists = pl.pallas_call(
        functools.partial(
            early_kernel, own, rows, slots, lent, bits, placed, units, tuple(bases)
        ),
        out_shape=(
            jax.ShapeDtypeStruct(((lines + 1) * ROWS, depth), F32),
            jax.ShapeDtypeStruct((1, TILE), F32),
            jax.ShapeDtypeStruct((2 * length + 3,), jnp.int32),
            jax.ShapeDtypeStruct((lent * FEATS, depth), BF16),
        ),
        in_specs=[smem()] + [vmem()] * (3 + len(units)),
        out_specs=(vmem(), vmem(), smem(), vmem()),
        scratch_shapes=scratch
        + [
            pltpu.VMEM((lent, TILE), jnp.int32),
            pltpu.SMEM((lent, TILE), jnp.int32),
            pltpu.VMEM((3 * lent, TILE), F32),
            pltpu.SemaphoreType.DMA,
        ]
        + squares,
        compiler_params=limited(16),
        cost_estimate=pl.CostEstimate(flops=0, bytes_accessed=30_000_000, transcendentals=0),
    )(*own_lists, *gots, corner, early)
    groups = [own_lists, lent_lists]
    parts = len(groups)
    lists = [group[0] for group in groups]
    feats = [group[1] for group in groups]
    list_specs = [smem()] * parts + [vmem()] * parts
    outs = pl.pallas_call(
        functools.partial(late_kernel, own, lent, parts, bits),
        out_shape=(
            jax.ShapeDtypeStruct((3 * own, depth), F32),
            jax.ShapeDtypeStruct((3 * max(lent, 8), depth), F32),
            jax.ShapeDtypeStruct((1, TILE), F32),
            jax.ShapeDtypeStruct((2, 3 * planes, depth), F32),
            jax.ShapeDtypeStruct((2, 3 * rows + 8, depth), F32),
        ),
        in_specs=list_specs + [vmem()] * 7,
        out_specs=(vmem(),) * 5,
        scratch_shapes=scratch + [pltpu.VMEM(((lines + 1) * ROWS, depth), F32)] + squares,
        compiler_params=limited(16),
    )(
        *lists, *feats, late, partial, part_loads, flat_points, corner,
        wide(motion), wide(inverse_mass),
    )
    shift, lent_shift, state, row_sent, plane_sent = outs

    backs = [
        lax.ppermute(lent_shift, "slab", [(h ^ bit, h) for h in heavy]).reshape(
            3, share, rows, depth
        )
        for bit in units
    ]
    plane_halo = shifted_back(plane_sent, "slab")
    row_halo = shifted_back(row_sent, "ctrl").reshape(2, 3, planes, depth)
    node_shift, volume, change = pl.pallas_call(
        functools.partial(volume_kernel, keep, share),
        out_shape=(
            jax.ShapeDtypeStruct(node_points.shape, F32),
            jax.ShapeDtypeStruct(node_points.shape[1:], F32),
            jax.ShapeDtypeStruct(node_points.shape[1:], F32),
        ),
        in_specs=[vmem()] * (4 + len(backs)),
        out_specs=(vmem(),) * 3,
        compiler_params=limited(8),
    )(node_points, shift.reshape(3, planes, rows, depth), *backs, plane_halo, row_halo)
    return node_shift, volume, change, state[0, : motion.shape[0]]


def solution(mesh):
    placed = (
        P(("slab", "ctrl")),
        P(None, ("slab", "ctrl")),
        P(None, ("slab", "ctrl")),
        P(),
        P(),
        P(None, ("slab", "ctrl")),
        P(None, ("slab", "ctrl")),
        P(None, "slab", "ctrl", None),
        P("slab", "ctrl", None),
        P("slab", "ctrl"),
    )
    return jax.shard_map(
        local,
        mesh=mesh,
        in_specs=placed,
        out_specs=(
            P(None, "slab", "ctrl", None),
            P("slab", "ctrl", None),
            P("slab", "ctrl", None),
            P(),
        ),
        check_vma=False,
    )
```

```python
import functools
import jax
import jax.numpy as jnp
from jax import lax
from jax.experimental import pallas as pl
from jax.experimental.pallas import tpu as pltpu
from jax.sharding import PartitionSpec as P

TILE = 128
TIME_STEP = 0.5
RADIUS = 4.0
GRAVITY = (0.0, 0.0, -0.5, 0.0, 0.0, 0.0)
ROWS = 24
FEATS = 32
UNROLL = 20
MIX = 48
TINY = 1e-30
F32 = jnp.float32
BF16 = jnp.bfloat16


def limited(mib):
    return pltpu.CompilerParams(vmem_limit_bytes=mib << 20)


def vmem():
    return pl.BlockSpec(memory_space=pltpu.VMEM)


def smem():
    return pl.BlockSpec(memory_space=pltpu.SMEM)


def swapped(value, slab_bit, ctrl_bit):
    slabs, ctrls = lax.axis_size("slab"), lax.axis_size("ctrl")
    pairs = [
        (s * ctrls + c, (s ^ slab_bit) * ctrls + (c ^ ctrl_bit))
        for s in range(slabs)
        for c in range(ctrls)
    ]
    return lax.ppermute(value, ("slab", "ctrl"), pairs)


def shifted_back(value, axis):
    return lax.ppermute(value, axis, [(i, i - 1) for i in range(1, lax.axis_size(axis))])


def load_rows(pressure, area, center):
    pushed = pressure * area

    def turned(value, by):
        return jnp.concatenate([value[by:3], value[0:by]], axis=0)

    moment = turned(center, 1) * turned(pushed, 2) - turned(center, 2) * turned(pushed, 1)
    sums = [jnp.sum(pushed, axis=1, keepdims=True), jnp.sum(moment, axis=1, keepdims=True)]
    lane = lax.broadcasted_iota(jnp.int32, (1, 128), 1)
    row = jnp.zeros((1, 128), F32)
    for k in range(6):
        row = jnp.where(lane == k, sums[k // 3][k % 3 : k % 3 + 1, :], row)
    return row


def pack_table(row, points, modes, out):
    for t in range(points.shape[1] // TILE):
        span = slice(t * TILE, (t + 1) * TILE)
        base = t * ROWS
        for c in range(3):
            out[base + 8 * c : base + 8 * c + 1, :] = points[c : c + 1, span]
            for k in range(6):
                at = base + 8 * c + 1 + k
                out[at : at + 1, :] = modes[3 * k + c : 3 * k + c + 1, span]
            at = base + 8 * c + 7
            out[at : at + 1, :] = row if (t == 0 and c == 0) else jnp.zeros((1, 128), F32)


def count_column(counts, x):
    rows = counts.shape[1]
    row = lax.broadcasted_iota(jnp.int32, (rows, rows), 0)
    lane = lax.broadcasted_iota(jnp.int32, (rows, rows), 1)
    many = jnp.broadcast_to(counts[x : x + 1, :].astype(F32), (rows, rows))
    return jnp.sum(jnp.where(row == lane, many, 0.0), axis=1, keepdims=True)


def marked(numbers, counts, x):
    slot = lax.broadcasted_iota(jnp.int32, numbers.shape[1:], 1).astype(F32)
    return jnp.where(slot < count_column(counts, x), numbers[x].astype(F32) + 1.0, 0.0)


def pack_lent(planes, turn, base, nodes, numbers, counts, out):
    rows, slots = numbers.shape[1:]
    lent = len(planes) * rows
    for i, x in enumerate(planes):
        at = base + i * rows
        for c in range(3):
            first = (c * counts.shape[0] + x) * rows
            out[at + c * lent : at + c * lent + rows, :] = nodes[first : first + rows, :]
    at, y = base + rows, 1 + turn
    for c in range(3):
        first = (c * counts.shape[0] + 1) * rows + y
        out[at + c * lent : at + c * lent + 1, :] = nodes[first : first + 1, :]
    for i, x in enumerate(planes):
        listed = marked(numbers, counts, x)
        if i == 1:
            listed = jnp.concatenate([marked(numbers, counts, 1)[y : y + 1], listed[1:]], axis=0)
        at = base + i * lent
        for row in range(rows):
            out[at : at + 1, row * slots : (row + 1) * slots] = listed[row : row + 1]


def pack_corner(nodes, numbers, counts, out):
    slots = numbers.shape[2]
    out[...] = jnp.zeros(out.shape, F32)
    for c in range(3):
        first = c * counts.shape[0] * counts.shape[1]
        out[c : c + 1, :] = nodes[first : first + 1, :]
    out[3:4, 0:slots] = marked(numbers, counts, 0)[0:1]


def pack_kernel(
    spans, pressure, area, center, points, modes, nodes, numbers, counts, corner, out, *lents
):
    row = load_rows(pressure[...], area[...], center[...])
    pack_table(row, points, modes, out)
    pack_corner(nodes, numbers, counts, corner)
    pack_lent(spans[0], 0, points.shape[1] // TILE * ROWS, nodes, numbers, counts, out)
    for turn, (span, lent) in enumerate(zip(spans[1:], lents)):
        pack_lent(span, turn + 1, 0, nodes, numbers, counts, lent)


def lend_kernel(spans, nodes, numbers, counts, corner, *outs):
    pack_corner(nodes, numbers, counts, corner)
    for turn, (span, out) in enumerate(zip(spans, outs)):
        pack_lent(span, turn, 0, nodes, numbers, counts, out)


def loads_kernel(pressure, area, center, out):
    out[...] = load_rows(pressure[...], area[...], center[...])


def split3(value):
    first = value.astype(BF16).astype(F32)
    rest = value - first
    second = rest.astype(BF16).astype(F32)
    return first, second, rest - second


def spread(ref, at):
    return jnp.broadcast_to(ref[pl.ds(at, 1), :], (8, ref.shape[1]))


def products(rows, scale, order, ends):
    row = lax.broadcasted_iota(jnp.int32, rows[0].shape, 0)
    norm = jnp.zeros(rows[0].shape, F32)
    blocks = []
    for value in rows:
        place = value * (1.0 / RADIUS)
        norm = norm + place * place
        first, second, third = split3(place * scale)
        low = jnp.where((row & 1) == 1, order[1](first, second, third, row), order[0](first, second, third, row))
        blocks.append(low)
    first, second, third = split3(norm)
    blocks.append(ends(first, second, third, row))
    return jnp.concatenate(blocks, axis=0)


def tile_block(rows):
    return products(
        rows,
        -2.0,
        (
            lambda a, b, c, row: jnp.where((row == 2) | (row == 6), b, a),
            lambda a, b, c, row: jnp.where(row == 1, a, jnp.where(row == 3, b, c)),
        ),
        lambda a, b, c, row: jnp.where(
            row == 0, a, jnp.where(row == 1, b, jnp.where(row == 2, c, jnp.where(row < 6, 1.0, 0.0)))
        ),
    )


def line_block(rows):
    return products(
        rows,
        1.0,
        (
            lambda a, b, c, row: jnp.where(row < 4, a, c),
            lambda a, b, c, row: jnp.where(row == 5, a, b),
        ),
        lambda a, b, c, row: jnp.where(
            row < 3, 1.0, jnp.where(row == 3, a, jnp.where(row == 4, b, jnp.where(row == 5, c, 0.0)))
        ),
    )


def build_lists(lines, slots, bits, first, listed, items):
    few = min(4, slots)
    middle = lines * slots + 2 * UNROLL

    def take(line, low, high):
        for e in range(low, high):
            value = listed[line, e]
            items[lax.shift_right_logical(value, 16)] = value

    def one(line, carry):
        take(line, 0, few)

        def rest(step, carry):
            take(line, few, slots)
            return carry

        return lax.fori_loop(0, jnp.where(listed[line, slots] > few, 1, 0), rest, carry)

    lax.fori_loop(0, lines, one, 0)
    end_a, end_b = listed[0, slots + 1], listed[0, slots + 2]
    for e in range(2 * UNROLL):
        items[end_a + e] = (first + lines) << bits
        items[middle + end_b + e] = (first + lines) << bits
    items[2 * middle] = end_a
    items[2 * middle + 1] = end_b


def line_features(lines, points, line_feat):
    def block(l, carry):
        rows = [spread(points, c * lines + l) for c in range(3)]
        at = pl.ds(pl.multiple_of(l * FEATS, FEATS), FEATS)
        line_feat[at, :] = line_block(rows).astype(BF16)
        return carry

    lax.fori_loop(0, lines, block, 0, unroll=4)


def code_items(first, bits, placed, numbers, counts, codes):
    lines, slots = numbers.shape
    row = lax.broadcasted_iota(jnp.int32, (lines, slots), 0)
    slot = lax.broadcasted_iota(jnp.int32, (lines, slots), 1)
    code = lax.shift_left(row + first, jnp.full_like(row, bits)) + placed(numbers)
    late = lax.shift_right_logical(code, jnp.full_like(row, bits - 1)) & 1
    middle = lines * slots + 2 * UNROLL
    high = lax.broadcasted_iota(jnp.int32, (slots, slots), 0)
    wide = lax.broadcasted_iota(jnp.int32, (slots, slots), 1)
    before = jnp.where(high < wide, 1.0, 0.0).astype(BF16)
    high = lax.broadcasted_iota(jnp.int32, (lines, lines), 0)
    wide = lax.broadcasted_iota(jnp.int32, (lines, lines), 1)
    above = jnp.where(wide < high, 1.0, 0.0).astype(BF16)
    place = jnp.full((lines, slots), 2 * middle + 2, jnp.int32)
    ends = []
    for part in range(2):
        chosen = (slot < counts) & (late == part)
        flag = jnp.where(chosen, 1.0, 0.0)
        total = jnp.broadcast_to(jnp.sum(flag, axis=1, keepdims=True), (lines, slots))
        at = jnp.dot(flag.astype(BF16), before, preferred_element_type=F32)
        at = at + jnp.dot(above, total.astype(BF16), preferred_element_type=F32)
        place = jnp.where(chosen, at.astype(jnp.int32) + part * middle, place)
        ends.append(jnp.sum(total[:, 0:1], axis=0, keepdims=True).astype(jnp.int32))
    codes[:, 0:slots] = lax.shift_left(place, jnp.full_like(place, 16)) | code
    codes[:, slots : slots + 1] = counts
    codes[0:1, slots + 1 : slots + 2] = ends[0]
    codes[0:1, slots + 2 : slots + 3] = ends[1]


def own_kernel(
    keep, turns, bits, placed, span, points, numbers, counts,
    items, line_feat, sent, codes, listed, sem,
):
    planes, rows, slots = numbers.shape
    pack_lent(span, turns - 1, 0, points, numbers, counts, sent)
    slabs = lax.axis_size("slab")
    lends = is_heavy(lax.axis_index("slab"), slabs)
    columns = []
    for x in range(planes):
        count = count_column(counts, x).astype(jnp.int32)
        if x >= keep:
            row = lax.broadcasted_iota(jnp.int32, count.shape, 0)
            count = jnp.where(lends & (row >= 1), 0, count)
        if x == 1:
            row = lax.broadcasted_iota(jnp.int32, count.shape, 0)
            count = jnp.where(lends & (row >= 1) & (row <= turns), 0, count)
        columns.append(count)
    number = jnp.concatenate([numbers[x] for x in range(planes)], axis=0)
    code_items(0, bits, placed, number, jnp.concatenate(columns, axis=0), codes)
    copy = pltpu.make_async_copy(codes, listed, sem)
    copy.start()
    line_features(planes * rows, points, line_feat)
    copy.wait()
    build_lists(planes * rows, slots, bits, 0, listed, items)


def read_lent(first, rows, slots, lent, bits, placed, units, bases, gots, corner, got, codes):
    slab, slabs = lax.axis_index("slab"), lax.axis_size("slab")
    value = gots[-1][pl.ds(bases[-1], 3 * lent), :]
    for unit, base, ref in list(zip(units, bases, gots))[:-1]:
        value = jnp.where(is_heavy(slab ^ unit, slabs), ref[pl.ds(base, 3 * lent), :], value)
    number = [
        value[i * lent : i * lent + 1, y * slots : (y + 1) * slots]
        for i in range(lent // rows)
        for y in range(rows)
    ]
    number = jnp.concatenate([corner[3:4, 0:slots]] + number[1:], axis=0)
    got[...] = value
    for c in range(3):
        got[c * lent : c * lent + 1, :] = corner[c : c + 1, :]
    helps = jnp.logical_not(is_heavy(slab, slabs))
    line = lax.broadcasted_iota(jnp.int32, number.shape, 0)
    taken = (helps & ((lax.rem(line, rows) >= 1) | (line == rows))) | (line == 0)
    number = jnp.where(taken, number, 0.0)
    count = jnp.sum(jnp.where(number > 0.0, 1.0, 0.0), axis=1, keepdims=True).astype(jnp.int32)
    number = jnp.maximum(number - 1.0, 0.0).astype(jnp.int32)
    code_items(first, bits, placed, number, count, codes)


def prepared(kernel, lines, slots, depth, more, scratch, *operands):
    length = lines * slots + 2 * UNROLL
    return pl.pallas_call(
        kernel,
        out_shape=(
            jax.ShapeDtypeStruct((2 * length + 3,), jnp.int32),
            jax.ShapeDtypeStruct((lines * FEATS, depth), BF16),
            *more,
        ),
        in_specs=[vmem()] * len(operands),
        out_specs=(smem(), vmem()) + (vmem(),) * len(more),
        scratch_shapes=[
            pltpu.VMEM((lines, TILE), jnp.int32),
            pltpu.SMEM((lines, TILE), jnp.int32),
        ]
        + scratch
        + [pltpu.SemaphoreType.DMA],
        compiler_params=limited(4),
        cost_estimate=pl.CostEstimate(flops=0, bytes_accessed=8_000_000, transcendentals=0),
    )(*operands)


def add_items(bits, half, lists, table, feats, line_feat, tile_feat, modes, acc, squares, ready):
    tiles = table.shape[0] // ROWS
    at = 0
    for feat in feats:
        line_feat[at : at + feat.shape[0], :] = feat[...]
        at += feat.shape[0]
    line_feat[at:, :] = jnp.zeros((line_feat.shape[0] - at, line_feat.shape[1]), BF16)

    def build(t, carry):
        base = pl.multiple_of(t * ROWS, 8)
        rows = [spread(table, base + 8 * c) for c in range(3)]
        block = tile_block(rows)
        tile_feat[pl.ds(pl.multiple_of(t * TILE, TILE), TILE), :] = block.astype(BF16).T
        value = 4.0 * table[pl.ds(base, ROWS), :]
        high = value.astype(BF16)
        low = (value - high.astype(F32)).astype(BF16)
        at = pl.ds(pl.multiple_of(t * MIX, 16), MIX)
        modes[at, :] = jnp.concatenate([high, low], axis=0)
        return carry

    lax.fori_loop(0, tiles, build, 0, unroll=8)
    mask = tiles - 1
    ready()
    middles = [(items.shape[0] - 3) // 2 for items in lists]
    starts = [middle * half for middle in middles]
    first = lists[0][2 * middles[0] + half]
    count = sum(items[2 * middle + half] for items, middle in zip(lists, middles))

    def unpack(at):
        code = lists[0][starts[0] + jnp.minimum(at, first)]
        other = lists[1][starts[1] + jnp.maximum(at - first, 0)]
        code = jnp.where(at < first, code, other)
        return lax.shift_right_logical(code & 0xFFFF, bits), code & mask

    def distances(u, at):
        line, tile = unpack(at)
        squares[u][...] = jnp.dot(
            tile_feat[pl.ds(pl.multiple_of(tile * TILE, TILE), TILE), :],
            line_feat[pl.ds(pl.multiple_of(line * FEATS, FEATS), FEATS), :],
            preferred_element_type=F32,
        )

    def gather(u, at):
        line, tile = unpack(at)
        square = jnp.maximum(squares[u][...], TINY)
        near = jnp.maximum(1.0 - square * lax.rsqrt(square), 0.0)
        fourth = near * near
        fourth = fourth * fourth
        phi = fourth * (1.25 - near)
        high = phi.astype(BF16)
        low = (phi - high.astype(F32)).astype(BF16)
        mode = modes[pl.ds(pl.multiple_of(tile * MIX, 16), MIX), :]
        got = jnp.dot(
            jnp.concatenate([mode, mode], axis=1),
            jnp.concatenate([high, low], axis=0),
            preferred_element_type=F32,
        )
        where = pl.ds(pl.multiple_of(line * ROWS, 8), ROWS)
        acc[where, :] = acc[where, :] + (got[0:ROWS] + got[ROWS:MIX])

    def body(j, carry):
        base = j * UNROLL
        for u in range(UNROLL):
            gather(u, base + u)
            distances(u, base + UNROLL + u)
        return carry

    for u in range(UNROLL):
        distances(u, u)
    lax.fori_loop(0, lax.div(count + (UNROLL - 1), jnp.int32(UNROLL)), body, 0)


def load_sum(table):
    tiles = table.shape[0] // ROWS
    return jnp.sum(table[pl.ds(7, tiles, stride=ROWS), :], axis=0, keepdims=True)


def early_kernel(own, rows, slots, lent, bits, placed, units, bases, *refs):
    own_items, own_feat, *refs = refs
    gots, refs = refs[: len(units)], refs[len(units) :]
    corner, table, acc, loads, items, lent_feat, *refs = refs
    line_feat, tile_feat, modes, codes, listed, got, sem, *squares = refs
    read_lent(own, rows, slots, lent, bits, placed, units, bases, gots, corner, got, codes)
    copy = pltpu.make_async_copy(codes, listed, sem)
    copy.start()
    line_features(lent, got, lent_feat)
    acc[...] = jnp.zeros(acc.shape, F32)
    loads[...] = load_sum(table)

    def ready():
        copy.wait()
        build_lists(lent, slots, bits, own, listed, items)

    add_items(
        bits, 0, (own_items, items), table, (own_feat, lent_feat),
        line_feat, tile_feat, modes, acc, squares, ready,
    )


def late_kernel(own, lent, parts, bits, *refs):
    lists, feats = refs[:parts], refs[parts : 2 * parts]
    table, early, loads, points, corner, motion, inverse, *rest = refs[2 * parts :]
    out_own, out_extra, out_state, out_row, out_plane, *rest = rest
    line_feat, tile_feat, modes, acc, *squares = rest
    total = loads[...] + load_sum(table)
    lane = lax.broadcasted_iota(jnp.int32, (1, 128), 1)
    gravity = jnp.zeros((1, 128), F32)
    for k, pull in enumerate(GRAVITY):
        gravity = jnp.where(lane == k, pull, gravity)
    acceleration = inverse[...] * total + gravity
    out_state[...] = motion[...] + TIME_STEP * acceleration
    step = TIME_STEP * motion[...] + 0.5 * TIME_STEP * TIME_STEP * acceleration
    acc[...] = early[...]
    add_items(
        bits, 1, lists, table, feats, line_feat, tile_feat, modes, acc, squares, lambda: None
    )

    def finish(count, first, out):
        for c in range(3):
            value = jnp.zeros((count, out.shape[1]), F32)
            for k in range(6):
                at = first * ROWS + 8 * c + 1 + k
                value = value + step[:, k : k + 1] * acc[pl.ds(at, count, stride=ROWS), :]
            out[c * count : (c + 1) * count, :] = value

    finish(own, 0, out_own)
    finish(lent, own, out_extra)
    rows = out_row.shape[1] // 3
    wide = own // rows
    for c in range(3):
        old = points[c * own : c * own + wide, :]
        out_plane[0, c * wide : (c + 1) * wide, :] = old
        out_plane[1, c * wide : (c + 1) * wide, :] = old + out_own[c * own : c * own + wide, :]
        old = points[pl.ds(c * own, rows, stride=wide), :]
        out_row[0, c * rows : (c + 1) * rows, :] = old
        out_row[1, c * rows : (c + 1) * rows, :] = (
            old + out_own[pl.ds(c * own, rows, stride=wide), :]
        )
    out_plane[0, 3 * wide :, :] = corner[...]
    out_plane[1, 3 * wide :, :] = corner[...]
    for c in range(3):
        at = slice(3 * wide + c, 3 * wide + c + 1)
        out_plane[1, at, :] = corner[c : c + 1, :] + out_extra[c * lent : c * lent + 1, :]


def volume_kernel(
    keep, share, points, shift, *refs
):
    *backs, plane_halo, row_halo, out_shift, out_volume, out_change = refs
    planes, rows, depth = points.shape[1:]
    slab, ctrl = lax.axis_index("slab"), lax.axis_index("ctrl")
    slabs, ctrls = lax.axis_size("slab"), lax.axis_size("ctrl")
    row_id = lax.broadcasted_iota(jnp.int32, (rows, depth), 0)
    lane = lax.broadcasted_iota(jnp.int32, (rows, depth), 1)
    inside = (lane < depth - 1) & (row_id + ctrl * rows < ctrls * rows - 1)
    if backs:
        from_helper = (row_id >= 1) & is_heavy(slab, slabs)
    last_row = row_id == rows - 1

    def next_row(value, edge):
        return jnp.where(last_row, edge, pltpu.roll(value, rows - 1, 0))

    def next_depth(value):
        return pltpu.roll(value, depth - 1, 1)

    def level(x):
        found = []
        for field in range(2):
            parts = []
            for c in range(3):
                if x == planes:
                    here = plane_halo[field, c * rows : (c + 1) * rows, :]
                    edge = plane_halo[field, 3 * rows + c : 3 * rows + c + 1, :]
                else:
                    here = points[c, x]
                    if field == 1:
                        moved = shift[c, x]
                        if backs and x >= keep:
                            back = backs[(x - keep) // share]
                            moved = jnp.where(from_helper, back[c, (x - keep) % share], moved)
                        if x == 1:
                            for turn, back in enumerate(backs):
                                here_too = from_helper & (row_id == 1 + turn)
                                moved = jnp.where(here_too, back[c, 1, 0:1, :], moved)
                        out_shift[c, x] = moved
                        here = here + moved
                    edge = row_halo[field, c, x : x + 1, :]
                there = next_row(here, edge)
                parts.append((here + there, there - here))
            found.append(parts)
        return found

    before = level(0)
    for x in range(planes):
        after = level(x + 1)
        volumes = []
        for field in range(2):
            edges = []
            for c in range(3):
                both0, step0 = before[field][c]
                both1, step1 = after[field][c]
                along, across, total = both1 - both0, step0 + step1, both0 + both1
                edges.append(
                    (
                        0.25 * (along + next_depth(along)),
                        0.25 * (across + next_depth(across)),
                        0.25 * (next_depth(total) - total),
                    )
                )
            ex, ey, ez = zip(*edges)
            volumes.append(
                ex[0] * (ey[1] * ez[2] - ey[2] * ez[1])
                + ex[1] * (ey[2] * ez[0] - ey[0] * ez[2])
                + ex[2] * (ey[0] * ez[1] - ey[1] * ez[0])
            )
        live = inside & (slab * planes + x < slabs * planes - 1)
        out_volume[x] = jnp.where(live, volumes[1], 0.0)
        out_change[x] = jnp.where(live, volumes[1] - volumes[0], 0.0)
        before = after


def is_heavy(slab, slabs):
    return (8 * slab >= 3 * slabs) & (8 * slab < 5 * slabs)


def local(
    face_pressure,
    face_area,
    face_center,
    motion,
    inverse_mass,
    control_points,
    control_modes,
    node_points,
    tile_list,
    tile_count,
):
    slabs, ctrls = lax.axis_size("slab"), lax.axis_size("ctrl")
    slab, ctrl = lax.axis_index("slab"), lax.axis_index("ctrl")
    _, planes, rows, depth = node_points.shape
    slots = tile_list.shape[2]
    own = planes * rows
    columns = control_points.shape[1]
    tiles = columns * slabs * ctrls // TILE
    bits = max(1, (tiles - 1).bit_length())
    pressure = face_pressure.reshape(1, -1)

    unit = slabs // 8
    share = (planes - 1) // 3
    keep = planes - 3 * share
    lend = slabs % 8 == 0 and slabs & (slabs - 1) == 0 and share > 1 and keep > 1 and rows > 4
    assert lend and share <= 3 and rows * slots <= TILE, (slabs, planes, rows, slots)
    units = (4 * unit, 2 * unit, unit) if lend else ()
    spans = [tuple(range(keep + g * share, keep + (g + 1) * share)) for g in range(len(units))]
    lent = share * rows if lend else 0
    heavy = [s for s in range(slabs) if is_heavy(s, slabs)]

    direct = columns % TILE == 0 and slabs & (slabs - 1) == 0 and ctrls & (ctrls - 1) == 0
    direct = direct and ctrls > 1 and (columns // TILE) & (columns // TILE - 1) == 0
    own_tiles = columns // TILE
    order = []
    bit = slabs // 2
    while bit:
        order.append((bit, 0))
        bit //= 2
    bit = 1
    while bit < ctrls:
        order.append((0, bit))
        bit *= 2

    def placed(number):
        if not direct:
            return number
        device = lax.axis_index("slab") * ctrls + lax.axis_index("ctrl")
        apart = (number >> (own_tiles.bit_length() - 1)) ^ device
        at = jnp.zeros(number.shape, jnp.int32)
        for turn, (slab_bit, ctrl_bit) in enumerate(order):
            flag = slab_bit * ctrls + ctrl_bit
            at = at + jnp.where((apart & flag) != 0, own_tiles << turn, 0)
        return at + (number & (own_tiles - 1))

    flat_points = node_points.reshape(3 * own, depth)
    *own_lists, last_sent = prepared(
        functools.partial(own_kernel, keep, len(units), bits, placed, spans[-1]),
        own, slots, depth, [jax.ShapeDtypeStruct((3 * lent, TILE), F32)], [],
        flat_points, tile_list, tile_count,
    )

    gots, bases = [], []
    if direct:
        size = own_tiles * ROWS
        corner, first, *sents = pl.pallas_call(
            functools.partial(pack_kernel, spans[:-1]),
            out_shape=[
                jax.ShapeDtypeStruct((rows_of, TILE), F32)
                for rows_of in [8, size + 3 * lent] + [3 * lent] * (len(units) - 2)
            ],
            in_specs=[vmem()] * 8,
            out_specs=[vmem()] * len(units),
            compiler_params=limited(56),
        )(
            pressure, face_area, face_center, control_points, control_modes,
            flat_points, tile_list, tile_count,
        )
        sents.append(last_sent)
        early = first[:size]
        corner = shifted_back(corner, "ctrl")
        for turn, (slab_bit, ctrl_bit) in enumerate(order[:-1]):
            size = early.shape[0]
            if turn == 2:
                early, own_lists, sents[-1] = lax.optimization_barrier(
                    (early, own_lists, sents[-1])
                )
            if turn == 3:
                early, corner = lax.optimization_barrier((early, corner))
            if lend and slab_bit in units:
                payload = jnp.concatenate([early, sents[len(gots) - 1]], axis=0) if gots else first
                reply = swapped(payload, slab_bit, ctrl_bit)
                gots.append(reply)
                bases.append(size)
                reply = reply[:size]
            else:
                reply = swapped(early, slab_bit, ctrl_bit)
            early = jnp.concatenate([early, reply], axis=0)
        late = swapped(early, *order[-1])
    else:
        loads = pl.pallas_call(
            loads_kernel,
            out_shape=jax.ShapeDtypeStruct((1, TILE), F32),
            in_specs=[vmem()] * 3,
            out_specs=vmem(),
        )(pressure, face_area, face_center)
        loads = lax.psum(loads, ("slab", "ctrl"))
        whole = jnp.concatenate([control_points, control_modes], axis=0)
        whole = lax.all_gather(whole, ("slab", "ctrl"), axis=1, tiled=True)
        whole = whole.reshape(7, 3, tiles, TILE).transpose(2, 1, 0, 3)
        spare = jnp.zeros((tiles, 3, 1, TILE), F32).at[0, 0, 0, :].set(loads[0])
        table = jnp.concatenate([whole, spare], axis=2).reshape(tiles * ROWS, TILE)
        early, late = table[: tiles // 2 * ROWS], table[tiles // 2 * ROWS :]
        corner, *sents = pl.pallas_call(
            functools.partial(lend_kernel, spans),
            out_shape=[jax.ShapeDtypeStruct((8, TILE), F32)]
            + [jax.ShapeDtypeStruct((3 * lent, TILE), F32)] * len(units),
            in_specs=[vmem()] * 3,
            out_specs=[vmem()] * (1 + len(units)),
        )(flat_points, tile_list, tile_count)
        corner = shifted_back(corner, "ctrl")
        gots = [swapped(sent, bit, 0) for sent, bit in zip(sents, units)]
        bases = [0] * len(units)
    lines = own + lent

    def wide(value):
        return jnp.pad(value, (0, TILE - value.shape[0])).reshape(1, TILE)

    half = tiles // 2
    length = lent * slots + 2 * UNROLL
    scratch = [
        pltpu.VMEM(((lines + 1) * FEATS, depth), BF16),
        pltpu.VMEM((half * TILE, FEATS), BF16),
        pltpu.VMEM((half * MIX, TILE), BF16),
    ]
    squares = [pltpu.VMEM((TILE, depth), F32)] * UNROLL
    partial, part_loads, *lent_lists = pl.pallas_call(
        functools.partial(
            early_kernel, own, rows, slots, lent, bits, placed, units, tuple(bases)
        ),
        out_shape=(
            jax.ShapeDtypeStruct(((lines + 1) * ROWS, depth), F32),
            jax.ShapeDtypeStruct((1, TILE), F32),
            jax.ShapeDtypeStruct((2 * length + 3,), jnp.int32),
            jax.ShapeDtypeStruct((lent * FEATS, depth), BF16),
        ),
        in_specs=[smem()] + [vmem()] * (3 + len(units)),
        out_specs=(vmem(), vmem(), smem(), vmem()),
        scratch_shapes=scratch
        + [
            pltpu.VMEM((lent, TILE), jnp.int32),
            pltpu.SMEM((lent, TILE), jnp.int32),
            pltpu.VMEM((3 * lent, TILE), F32),
            pltpu.SemaphoreType.DMA,
        ]
        + squares,
        compiler_params=limited(16),
        cost_estimate=pl.CostEstimate(flops=0, bytes_accessed=30_000_000, transcendentals=0),
    )(*own_lists, *gots, corner, early)
    groups = [own_lists, lent_lists]
    parts = len(groups)
    lists = [group[0] for group in groups]
    feats = [group[1] for group in groups]
    list_specs = [smem()] * parts + [vmem()] * parts
    outs = pl.pallas_call(
        functools.partial(late_kernel, own, lent, parts, bits),
        out_shape=(
            jax.ShapeDtypeStruct((3 * own, depth), F32),
            jax.ShapeDtypeStruct((3 * max(lent, 8), depth), F32),
            jax.ShapeDtypeStruct((1, TILE), F32),
            jax.ShapeDtypeStruct((2, 3 * planes, depth), F32),
            jax.ShapeDtypeStruct((2, 3 * rows + 8, depth), F32),
        ),
        in_specs=list_specs + [vmem()] * 7,
        out_specs=(vmem(),) * 5,
        scratch_shapes=scratch + [pltpu.VMEM(((lines + 1) * ROWS, depth), F32)] + squares,
        compiler_params=limited(16),
    )(
        *lists, *feats, late, partial, part_loads, flat_points, corner,
        wide(motion), wide(inverse_mass),
    )
    shift, lent_shift, state, row_sent, plane_sent = outs

    backs = [
        lax.ppermute(lent_shift, "slab", [(h ^ bit, h) for h in heavy]).reshape(
            3, share, rows, depth
        )
        for bit in units
    ]
    plane_halo = shifted_back(plane_sent, "slab")
    row_halo = shifted_back(row_sent, "ctrl").reshape(2, 3, planes, depth)
    node_shift, volume, change = pl.pallas_call(
        functools.partial(volume_kernel, keep, share),
        out_shape=(
            jax.ShapeDtypeStruct(node_points.shape, F32),
            jax.ShapeDtypeStruct(node_points.shape[1:], F32),
            jax.ShapeDtypeStruct(node_points.shape[1:], F32),
        ),
        in_specs=[vmem()] * (4 + len(backs)),
        out_specs=(vmem(),) * 3,
        compiler_params=limited(8),
    )(node_points, shift.reshape(3, planes, rows, depth), *backs, plane_halo, row_halo)
    return node_shift, volume, change, state[0, : motion.shape[0]]


def solution(mesh):
    placed = (
        P(("slab", "ctrl")),
        P(None, ("slab", "ctrl")),
        P(None, ("slab", "ctrl")),
        P(),
        P(),
        P(None, ("slab", "ctrl")),
        P(None, ("slab", "ctrl")),
        P(None, "slab", "ctrl", None),
        P("slab", "ctrl", None),
        P("slab", "ctrl"),
    )
    return jax.shard_map(
        local,
        mesh=mesh,
        in_specs=placed,
        out_specs=(
            P(None, "slab", "ctrl", None),
            P("slab", "ctrl", None),
            P("slab", "ctrl", None),
            P(),
        ),
        check_vma=False,
    )
```

```python
import functools
import jax
import jax.numpy as jnp
from jax import lax
from jax.experimental import pallas as pl
from jax.experimental.pallas import tpu as pltpu
from jax.sharding import PartitionSpec as P

TILE = 128
TIME_STEP = 0.5
RADIUS = 4.0
GRAVITY = (0.0, 0.0, -0.5, 0.0, 0.0, 0.0)
ROWS = 24
FEATS = 32
UNROLL = 20
MIX = 48
TINY = 1e-30
F32 = jnp.float32
BF16 = jnp.bfloat16


def limited(mib):
    return pltpu.CompilerParams(vmem_limit_bytes=mib << 20)


def vmem():
    return pl.BlockSpec(memory_space=pltpu.VMEM)


def smem():
    return pl.BlockSpec(memory_space=pltpu.SMEM)


def swapped(value, slab_bit, ctrl_bit):
    slabs, ctrls = lax.axis_size("slab"), lax.axis_size("ctrl")
    pairs = [
        (s * ctrls + c, (s ^ slab_bit) * ctrls + (c ^ ctrl_bit))
        for s in range(slabs)
        for c in range(ctrls)
    ]
    return lax.ppermute(value, ("slab", "ctrl"), pairs)


def shifted_back(value, axis):
    return lax.ppermute(value, axis, [(i, i - 1) for i in range(1, lax.axis_size(axis))])


def load_rows(pressure, area, center):
    pushed = pressure * area

    def turned(value, by):
        return jnp.concatenate([value[by:3], value[0:by]], axis=0)

    moment = turned(center, 1) * turned(pushed, 2) - turned(center, 2) * turned(pushed, 1)
    sums = [jnp.sum(pushed, axis=1, keepdims=True), jnp.sum(moment, axis=1, keepdims=True)]
    lane = lax.broadcasted_iota(jnp.int32, (1, 128), 1)
    row = jnp.zeros((1, 128), F32)
    for k in range(6):
        row = jnp.where(lane == k, sums[k // 3][k % 3 : k % 3 + 1, :], row)
    return row


def pack_table(row, points, modes, out):
    for t in range(points.shape[1] // TILE):
        span = slice(t * TILE, (t + 1) * TILE)
        base = t * ROWS
        for c in range(3):
            out[base + 8 * c : base + 8 * c + 1, :] = points[c : c + 1, span]
            for k in range(6):
                at = base + 8 * c + 1 + k
                out[at : at + 1, :] = modes[3 * k + c : 3 * k + c + 1, span]
            at = base + 8 * c + 7
            out[at : at + 1, :] = row if (t == 0 and c == 0) else jnp.zeros((1, 128), F32)


def count_column(counts, x):
    rows = counts.shape[1]
    row = lax.broadcasted_iota(jnp.int32, (rows, rows), 0)
    lane = lax.broadcasted_iota(jnp.int32, (rows, rows), 1)
    many = jnp.broadcast_to(counts[x : x + 1, :].astype(F32), (rows, rows))
    return jnp.sum(jnp.where(row == lane, many, 0.0), axis=1, keepdims=True)


def marked(numbers, counts, x):
    slot = lax.broadcasted_iota(jnp.int32, numbers.shape[1:], 1).astype(F32)
    return jnp.where(slot < count_column(counts, x), numbers[x].astype(F32) + 1.0, 0.0)


def pack_lent(planes, turn, base, nodes, numbers, counts, out):
    rows, slots = numbers.shape[1:]
    lent = len(planes) * rows
    for i, x in enumerate(planes):
        at = base + i * rows
        for c in range(3):
            first = (c * counts.shape[0] + x) * rows
            out[at + c * lent : at + c * lent + rows, :] = nodes[first : first + rows, :]
    at, y = base + rows, 1 + turn
    for c in range(3):
        first = (c * counts.shape[0] + 1) * rows + y
        out[at + c * lent : at + c * lent + 1, :] = nodes[first : first + 1, :]
    for i, x in enumerate(planes):
        listed = marked(numbers, counts, x)
        if i == 1:
            listed = jnp.concatenate([marked(numbers, counts, 1)[y : y + 1], listed[1:]], axis=0)
        at = base + i * lent
        for row in range(rows):
            out[at : at + 1, row * slots : (row + 1) * slots] = listed[row : row + 1]


def pack_corner(nodes, numbers, counts, out):
    slots = numbers.shape[2]
    out[...] = jnp.zeros(out.shape, F32)
    for c in range(3):
        first = c * counts.shape[0] * counts.shape[1]
        out[c : c + 1, :] = nodes[first : first + 1, :]
    out[3:4, 0:slots] = marked(numbers, counts, 0)[0:1]


def pack_kernel(
    spans, pressure, area, center, points, modes, nodes, numbers, counts, corner, out, *lents
):
    row = load_rows(pressure[...], area[...], center[...])
    pack_table(row, points, modes, out)
    pack_corner(nodes, numbers, counts, corner)
    pack_lent(spans[0], 0, points.shape[1] // TILE * ROWS, nodes, numbers, counts, out)
    for turn, (span, lent) in enumerate(zip(spans[1:], lents)):
        pack_lent(span, turn + 1, 0, nodes, numbers, counts, lent)


def lend_kernel(spans, nodes, numbers, counts, corner, *outs):
    pack_corner(nodes, numbers, counts, corner)
    for turn, (span, out) in enumerate(zip(spans, outs)):
        pack_lent(span, turn, 0, nodes, numbers, counts, out)


def loads_kernel(pressure, area, center, out):
    out[...] = load_rows(pressure[...], area[...], center[...])


def split3(value):
    first = value.astype(BF16).astype(F32)
    rest = value - first
    second = rest.astype(BF16).astype(F32)
    return first, second, rest - second


def spread(ref, at):
    return jnp.broadcast_to(ref[pl.ds(at, 1), :], (8, ref.shape[1]))


def products(rows, scale, order, ends):
    row = lax.broadcasted_iota(jnp.int32, rows[0].shape, 0)
    norm = jnp.zeros(rows[0].shape, F32)
    blocks = []
    for value in rows:
        place = value * (1.0 / RADIUS)
        norm = norm + place * place
        first, second, third = split3(place * scale)
        low = jnp.where((row & 1) == 1, order[1](first, second, third, row), order[0](first, second, third, row))
        blocks.append(low)
    first, second, third = split3(norm)
    blocks.append(ends(first, second, third, row))
    return jnp.concatenate(blocks, axis=0)


def tile_block(rows):
    return products(
        rows,
        -2.0,
        (
            lambda a, b, c, row: jnp.where((row == 2) | (row == 6), b, a),
            lambda a, b, c, row: jnp.where(row == 1, a, jnp.where(row == 3, b, c)),
        ),
        lambda a, b, c, row: jnp.where(
            row == 0, a, jnp.where(row == 1, b, jnp.where(row == 2, c, jnp.where(row < 6, 1.0, 0.0)))
        ),
    )


def line_block(rows):
    return products(
        rows,
        1.0,
        (
            lambda a, b, c, row: jnp.where(row < 4, a, c),
            lambda a, b, c, row: jnp.where(row == 5, a, b),
        ),
        lambda a, b, c, row: jnp.where(
            row < 3, 1.0, jnp.where(row == 3, a, jnp.where(row == 4, b, jnp.where(row == 5, c, 0.0)))
        ),
    )


def build_lists(lines, slots, bits, first, listed, items):
    few = min(4, slots)
    middle = lines * slots + 2 * UNROLL

    def take(line, low, high):
        for e in range(low, high):
            value = listed[line, e]
            items[lax.shift_right_logical(value, 16)] = value

    def one(line, carry):
        take(line, 0, few)

        def rest(step, carry):
            take(line, few, slots)
            return carry

        return lax.fori_loop(0, jnp.where(listed[line, slots] > few, 1, 0), rest, carry)

    lax.fori_loop(0, lines, one, 0)
    end_a, end_b = listed[0, slots + 1], listed[0, slots + 2]
    for e in range(2 * UNROLL):
        items[end_a + e] = (first + lines) << bits
        items[middle + end_b + e] = (first + lines) << bits
    items[2 * middle] = end_a
    items[2 * middle + 1] = end_b


def line_features(lines, points, line_feat):
    def block(l, carry):
        rows = [spread(points, c * lines + l) for c in range(3)]
        at = pl.ds(pl.multiple_of(l * FEATS, FEATS), FEATS)
        line_feat[at, :] = line_block(rows).astype(BF16)
        return carry

    lax.fori_loop(0, lines, block, 0, unroll=8)


def code_items(first, bits, placed, numbers, counts, codes):
    lines, slots = numbers.shape
    row = lax.broadcasted_iota(jnp.int32, (lines, slots), 0)
    slot = lax.broadcasted_iota(jnp.int32, (lines, slots), 1)
    code = lax.shift_left(row + first, jnp.full_like(row, bits)) + placed(numbers)
    late = lax.shift_right_logical(code, jnp.full_like(row, bits - 1)) & 1
    middle = lines * slots + 2 * UNROLL
    high = lax.broadcasted_iota(jnp.int32, (slots, slots), 0)
    wide = lax.broadcasted_iota(jnp.int32, (slots, slots), 1)
    before = jnp.where(high < wide, 1.0, 0.0).astype(BF16)
    high = lax.broadcasted_iota(jnp.int32, (lines, lines), 0)
    wide = lax.broadcasted_iota(jnp.int32, (lines, lines), 1)
    above = jnp.where(wide < high, 1.0, 0.0).astype(BF16)
    place = jnp.full((lines, slots), 2 * middle + 2, jnp.int32)
    ends = []
    for part in range(2):
        chosen = (slot < counts) & (late == part)
        flag = jnp.where(chosen, 1.0, 0.0)
        total = jnp.broadcast_to(jnp.sum(flag, axis=1, keepdims=True), (lines, slots))
        at = jnp.dot(flag.astype(BF16), before, preferred_element_type=F32)
        at = at + jnp.dot(above, total.astype(BF16), preferred_element_type=F32)
        place = jnp.where(chosen, at.astype(jnp.int32) + part * middle, place)
        ends.append(jnp.sum(total[:, 0:1], axis=0, keepdims=True).astype(jnp.int32))
    codes[:, 0:slots] = lax.shift_left(place, jnp.full_like(place, 16)) | code
    codes[:, slots : slots + 1] = counts
    codes[0:1, slots + 1 : slots + 2] = ends[0]
    codes[0:1, slots + 2 : slots + 3] = ends[1]


def own_kernel(
    keep, turns, bits, placed, span, points, numbers, counts,
    items, line_feat, sent, codes, listed, sem,
):
    planes, rows, slots = numbers.shape
    pack_lent(span, turns - 1, 0, points, numbers, counts, sent)
    slabs = lax.axis_size("slab")
    lends = is_heavy(lax.axis_index("slab"), slabs)
    columns = []
    for x in range(planes):
        count = count_column(counts, x).astype(jnp.int32)
        if x >= keep:
            row = lax.broadcasted_iota(jnp.int32, count.shape, 0)
            count = jnp.where(lends & (row >= 1), 0, count)
        if x == 1:
            row = lax.broadcasted_iota(jnp.int32, count.shape, 0)
            count = jnp.where(lends & (row >= 1) & (row <= turns), 0, count)
        columns.append(count)
    number = jnp.concatenate([numbers[x] for x in range(planes)], axis=0)
    code_items(0, bits, placed, number, jnp.concatenate(columns, axis=0), codes)
    copy = pltpu.make_async_copy(codes, listed, sem)
    copy.start()
    line_features(planes * rows, points, line_feat)
    copy.wait()
    build_lists(planes * rows, slots, bits, 0, listed, items)


def read_lent(first, rows, slots, lent, bits, placed, units, bases, gots, corner, got, codes):
    slab, slabs = lax.axis_index("slab"), lax.axis_size("slab")
    value = gots[-1][pl.ds(bases[-1], 3 * lent), :]
    for unit, base, ref in list(zip(units, bases, gots))[:-1]:
        value = jnp.where(is_heavy(slab ^ unit, slabs), ref[pl.ds(base, 3 * lent), :], value)
    number = [
        value[i * lent : i * lent + 1, y * slots : (y + 1) * slots]
        for i in range(lent // rows)
        for y in range(rows)
    ]
    number = jnp.concatenate([corner[3:4, 0:slots]] + number[1:], axis=0)
    got[...] = value
    for c in range(3):
        got[c * lent : c * lent + 1, :] = corner[c : c + 1, :]
    helps = jnp.logical_not(is_heavy(slab, slabs))
    line = lax.broadcasted_iota(jnp.int32, number.shape, 0)
    taken = (helps & ((lax.rem(line, rows) >= 1) | (line == rows))) | (line == 0)
    number = jnp.where(taken, number, 0.0)
    count = jnp.sum(jnp.where(number > 0.0, 1.0, 0.0), axis=1, keepdims=True).astype(jnp.int32)
    number = jnp.maximum(number - 1.0, 0.0).astype(jnp.int32)
    code_items(first, bits, placed, number, count, codes)


def prepared(kernel, lines, slots, depth, more, scratch, *operands):
    length = lines * slots + 2 * UNROLL
    return pl.pallas_call(
        kernel,
        out_shape=(
            jax.ShapeDtypeStruct((2 * length + 3,), jnp.int32),
            jax.ShapeDtypeStruct((lines * FEATS, depth), BF16),
            *more,
        ),
        in_specs=[vmem()] * len(operands),
        out_specs=(smem(), vmem()) + (vmem(),) * len(more),
        scratch_shapes=[
            pltpu.VMEM((lines, TILE), jnp.int32),
            pltpu.SMEM((lines, TILE), jnp.int32),
        ]
        + scratch
        + [pltpu.SemaphoreType.DMA],
        compiler_params=limited(4),
        cost_estimate=pl.CostEstimate(flops=0, bytes_accessed=8_000_000, transcendentals=0),
    )(*operands)


def add_items(bits, half, lists, table, feats, line_feat, tile_feat, modes, acc, squares, ready):
    tiles = table.shape[0] // ROWS
    at = 0
    for feat in feats:
        line_feat[at : at + feat.shape[0], :] = feat[...]
        at += feat.shape[0]
    line_feat[at:, :] = jnp.zeros((line_feat.shape[0] - at, line_feat.shape[1]), BF16)

    def build(t, carry):
        base = pl.multiple_of(t * ROWS, 8)
        rows = [spread(table, base + 8 * c) for c in range(3)]
        block = tile_block(rows)
        tile_feat[pl.ds(pl.multiple_of(t * TILE, TILE), TILE), :] = block.astype(BF16).T
        value = 4.0 * table[pl.ds(base, ROWS), :]
        high = value.astype(BF16)
        low = (value - high.astype(F32)).astype(BF16)
        at = pl.ds(pl.multiple_of(t * MIX, 16), MIX)
        modes[at, :] = jnp.concatenate([high, low], axis=0)
        return carry

    lax.fori_loop(0, tiles, build, 0, unroll=8)
    mask = tiles - 1
    ready()
    middles = [(items.shape[0] - 3) // 2 for items in lists]
    starts = [middle * half for middle in middles]
    first = lists[0][2 * middles[0] + half]
    count = sum(items[2 * middle + half] for items, middle in zip(lists, middles))

    def unpack(at):
        code = lists[0][starts[0] + jnp.minimum(at, first)]
        other = lists[1][starts[1] + jnp.maximum(at - first, 0)]
        code = jnp.where(at < first, code, other)
        return lax.shift_right_logical(code & 0xFFFF, bits), code & mask

    def distances(u, at):
        line, tile = unpack(at)
        squares[u][...] = jnp.dot(
            tile_feat[pl.ds(pl.multiple_of(tile * TILE, TILE), TILE), :],
            line_feat[pl.ds(pl.multiple_of(line * FEATS, FEATS), FEATS), :],
            preferred_element_type=F32,
        )

    def gather(u, at):
        line, tile = unpack(at)
        square = jnp.maximum(squares[u][...], TINY)
        near = jnp.maximum(1.0 - square * lax.rsqrt(square), 0.0)
        fourth = near * near
        fourth = fourth * fourth
        phi = fourth * (1.25 - near)
        high = phi.astype(BF16)
        low = (phi - high.astype(F32)).astype(BF16)
        mode = modes[pl.ds(pl.multiple_of(tile * MIX, 16), MIX), :]
        got = jnp.dot(
            jnp.concatenate([mode, mode], axis=1),
            jnp.concatenate([high, low], axis=0),
            preferred_element_type=F32,
        )
        where = pl.ds(pl.multiple_of(line * ROWS, 8), ROWS)
        acc[where, :] = acc[where, :] + (got[0:ROWS] + got[ROWS:MIX])

    def body(j, carry):
        base = j * UNROLL
        for u in range(UNROLL):
            gather(u, base + u)
            distances(u, base + UNROLL + u)
        return carry

    for u in range(UNROLL):
        distances(u, u)
    lax.fori_loop(0, lax.div(count + (UNROLL - 1), jnp.int32(UNROLL)), body, 0)


def load_sum(table):
    tiles = table.shape[0] // ROWS
    return jnp.sum(table[pl.ds(7, tiles, stride=ROWS), :], axis=0, keepdims=True)


def early_kernel(own, rows, slots, lent, bits, placed, units, bases, *refs):
    own_items, own_feat, *refs = refs
    gots, refs = refs[: len(units)], refs[len(units) :]
    corner, table, acc, loads, items, lent_feat, *refs = refs
    line_feat, tile_feat, modes, codes, listed, got, sem, *squares = refs
    read_lent(own, rows, slots, lent, bits, placed, units, bases, gots, corner, got, codes)
    copy = pltpu.make_async_copy(codes, listed, sem)
    copy.start()
    line_features(lent, got, lent_feat)
    acc[...] = jnp.zeros(acc.shape, F32)
    loads[...] = load_sum(table)

    def ready():
        copy.wait()
        build_lists(lent, slots, bits, own, listed, items)

    add_items(
        bits, 0, (own_items, items), table, (own_feat, lent_feat),
        line_feat, tile_feat, modes, acc, squares, ready,
    )


def late_kernel(own, lent, parts, bits, *refs):
    lists, feats = refs[:parts], refs[parts : 2 * parts]
    table, early, loads, points, corner, motion, inverse, *rest = refs[2 * parts :]
    out_own, out_extra, out_state, out_row, out_plane, *rest = rest
    line_feat, tile_feat, modes, acc, *squares = rest
    total = loads[...] + load_sum(table)
    lane = lax.broadcasted_iota(jnp.int32, (1, 128), 1)
    gravity = jnp.zeros((1, 128), F32)
    for k, pull in enumerate(GRAVITY):
        gravity = jnp.where(lane == k, pull, gravity)
    acceleration = inverse[...] * total + gravity
    out_state[...] = motion[...] + TIME_STEP * acceleration
    step = TIME_STEP * motion[...] + 0.5 * TIME_STEP * TIME_STEP * acceleration
    acc[...] = early[...]
    add_items(
        bits, 1, lists, table, feats, line_feat, tile_feat, modes, acc, squares, lambda: None
    )

    def finish(count, first, out):
        for c in range(3):
            value = jnp.zeros((count, out.shape[1]), F32)
            for k in range(6):
                at = first * ROWS + 8 * c + 1 + k
                value = value + step[:, k : k + 1] * acc[pl.ds(at, count, stride=ROWS), :]
            out[c * count : (c + 1) * count, :] = value

    finish(own, 0, out_own)
    finish(lent, own, out_extra)
    rows = out_row.shape[1] // 3
    wide = own // rows
    for c in range(3):
        old = points[c * own : c * own + wide, :]
        out_plane[0, c * wide : (c + 1) * wide, :] = old
        out_plane[1, c * wide : (c + 1) * wide, :] = old + out_own[c * own : c * own + wide, :]
        old = points[pl.ds(c * own, rows, stride=wide), :]
        out_row[0, c * rows : (c + 1) * rows, :] = old
        out_row[1, c * rows : (c + 1) * rows, :] = (
            old + out_own[pl.ds(c * own, rows, stride=wide), :]
        )
    out_plane[0, 3 * wide :, :] = corner[...]
    out_plane[1, 3 * wide :, :] = corner[...]
    for c in range(3):
        at = slice(3 * wide + c, 3 * wide + c + 1)
        out_plane[1, at, :] = corner[c : c + 1, :] + out_extra[c * lent : c * lent + 1, :]


def volume_kernel(
    keep, share, points, shift, *refs
):
    *backs, plane_halo, row_halo, out_shift, out_volume, out_change = refs
    planes, rows, depth = points.shape[1:]
    slab, ctrl = lax.axis_index("slab"), lax.axis_index("ctrl")
    slabs, ctrls = lax.axis_size("slab"), lax.axis_size("ctrl")
    row_id = lax.broadcasted_iota(jnp.int32, (rows, depth), 0)
    lane = lax.broadcasted_iota(jnp.int32, (rows, depth), 1)
    inside = (lane < depth - 1) & (row_id + ctrl * rows < ctrls * rows - 1)
    if backs:
        from_helper = (row_id >= 1) & is_heavy(slab, slabs)
    last_row = row_id == rows - 1

    def next_row(value, edge):
        return jnp.where(last_row, edge, pltpu.roll(value, rows - 1, 0))

    def next_depth(value):
        return pltpu.roll(value, depth - 1, 1)

    def level(x):
        found = []
        for field in range(2):
            parts = []
            for c in range(3):
                if x == planes:
                    here = plane_halo[field, c * rows : (c + 1) * rows, :]
                    edge = plane_halo[field, 3 * rows + c : 3 * rows + c + 1, :]
                else:
                    here = points[c, x]
                    if field == 1:
                        moved = shift[c, x]
                        if backs and x >= keep:
                            back = backs[(x - keep) // share]
                            moved = jnp.where(from_helper, back[c, (x - keep) % share], moved)
                        if x == 1:
                            for turn, back in enumerate(backs):
                                here_too = from_helper & (row_id == 1 + turn)
                                moved = jnp.where(here_too, back[c, 1, 0:1, :], moved)
                        out_shift[c, x] = moved
                        here = here + moved
                    edge = row_halo[field, c, x : x + 1, :]
                there = next_row(here, edge)
                parts.append((here + there, there - here))
            found.append(parts)
        return found

    before = level(0)
    for x in range(planes):
        after = level(x + 1)
        volumes = []
        for field in range(2):
            edges = []
            for c in range(3):
                both0, step0 = before[field][c]
                both1, step1 = after[field][c]
                along, across, total = both1 - both0, step0 + step1, both0 + both1
                edges.append(
                    (
                        0.25 * (along + next_depth(along)),
                        0.25 * (across + next_depth(across)),
                        0.25 * (next_depth(total) - total),
                    )
                )
            ex, ey, ez = zip(*edges)
            volumes.append(
                ex[0] * (ey[1] * ez[2] - ey[2] * ez[1])
                + ex[1] * (ey[2] * ez[0] - ey[0] * ez[2])
                + ex[2] * (ey[0] * ez[1] - ey[1] * ez[0])
            )
        live = inside & (slab * planes + x < slabs * planes - 1)
        out_volume[x] = jnp.where(live, volumes[1], 0.0)
        out_change[x] = jnp.where(live, volumes[1] - volumes[0], 0.0)
        before = after


def is_heavy(slab, slabs):
    return (8 * slab >= 3 * slabs) & (8 * slab < 5 * slabs)


def local(
    face_pressure,
    face_area,
    face_center,
    motion,
    inverse_mass,
    control_points,
    control_modes,
    node_points,
    tile_list,
    tile_count,
):
    slabs, ctrls = lax.axis_size("slab"), lax.axis_size("ctrl")
    slab, ctrl = lax.axis_index("slab"), lax.axis_index("ctrl")
    _, planes, rows, depth = node_points.shape
    slots = tile_list.shape[2]
    own = planes * rows
    columns = control_points.shape[1]
    tiles = columns * slabs * ctrls // TILE
    bits = max(1, (tiles - 1).bit_length())
    pressure = face_pressure.reshape(1, -1)

    unit = slabs // 8
    share = (planes - 1) // 3
    keep = planes - 3 * share
    lend = slabs % 8 == 0 and slabs & (slabs - 1) == 0 and share > 1 and keep > 1 and rows > 4
    assert lend and share <= 3 and rows * slots <= TILE, (slabs, planes, rows, slots)
    units = (4 * unit, 2 * unit, unit) if lend else ()
    spans = [tuple(range(keep + g * share, keep + (g + 1) * share)) for g in range(len(units))]
    lent = share * rows if lend else 0
    heavy = [s for s in range(slabs) if is_heavy(s, slabs)]

    direct = columns % TILE == 0 and slabs & (slabs - 1) == 0 and ctrls & (ctrls - 1) == 0
    direct = direct and ctrls > 1 and (columns // TILE) & (columns // TILE - 1) == 0
    own_tiles = columns // TILE
    order = []
    bit = slabs // 2
    while bit:
        order.append((bit, 0))
        bit //= 2
    bit = 1
    while bit < ctrls:
        order.append((0, bit))
        bit *= 2

    def placed(number):
        if not direct:
            return number
        device = lax.axis_index("slab") * ctrls + lax.axis_index("ctrl")
        apart = (number >> (own_tiles.bit_length() - 1)) ^ device
        at = jnp.zeros(number.shape, jnp.int32)
        for turn, (slab_bit, ctrl_bit) in enumerate(order):
            flag = slab_bit * ctrls + ctrl_bit
            at = at + jnp.where((apart & flag) != 0, own_tiles << turn, 0)
        return at + (number & (own_tiles - 1))

    flat_points = node_points.reshape(3 * own, depth)
    *own_lists, last_sent = prepared(
        functools.partial(own_kernel, keep, len(units), bits, placed, spans[-1]),
        own, slots, depth, [jax.ShapeDtypeStruct((3 * lent, TILE), F32)], [],
        flat_points, tile_list, tile_count,
    )

    gots, bases = [], []
    if direct:
        size = own_tiles * ROWS
        corner, first, *sents = pl.pallas_call(
            functools.partial(pack_kernel, spans[:-1]),
            out_shape=[
                jax.ShapeDtypeStruct((rows_of, TILE), F32)
                for rows_of in [8, size + 3 * lent] + [3 * lent] * (len(units) - 2)
            ],
            in_specs=[vmem()] * 8,
            out_specs=[vmem()] * len(units),
            compiler_params=limited(56),
        )(
            pressure, face_area, face_center, control_points, control_modes,
            flat_points, tile_list, tile_count,
        )
        sents.append(last_sent)
        early = first[:size]
        corner = shifted_back(corner, "ctrl")
        for turn, (slab_bit, ctrl_bit) in enumerate(order[:-1]):
            size = early.shape[0]
            if turn == 2:
                early, own_lists, sents[-1] = lax.optimization_barrier(
                    (early, own_lists, sents[-1])
                )
            if turn == 3:
                early, corner = lax.optimization_barrier((early, corner))
            if lend and slab_bit in units:
                payload = jnp.concatenate([early, sents[len(gots) - 1]], axis=0) if gots else first
                reply = swapped(payload, slab_bit, ctrl_bit)
                gots.append(reply)
                bases.append(size)
                reply = reply[:size]
            else:
                reply = swapped(early, slab_bit, ctrl_bit)
            early = jnp.concatenate([early, reply], axis=0)
        late = swapped(early, *order[-1])
    else:
        loads = pl.pallas_call(
            loads_kernel,
            out_shape=jax.ShapeDtypeStruct((1, TILE), F32),
            in_specs=[vmem()] * 3,
            out_specs=vmem(),
        )(pressure, face_area, face_center)
        loads = lax.psum(loads, ("slab", "ctrl"))
        whole = jnp.concatenate([control_points, control_modes], axis=0)
        whole = lax.all_gather(whole, ("slab", "ctrl"), axis=1, tiled=True)
        whole = whole.reshape(7, 3, tiles, TILE).transpose(2, 1, 0, 3)
        spare = jnp.zeros((tiles, 3, 1, TILE), F32).at[0, 0, 0, :].set(loads[0])
        table = jnp.concatenate([whole, spare], axis=2).reshape(tiles * ROWS, TILE)
        early, late = table[: tiles // 2 * ROWS], table[tiles // 2 * ROWS :]
        corner, *sents = pl.pallas_call(
            functools.partial(lend_kernel, spans),
            out_shape=[jax.ShapeDtypeStruct((8, TILE), F32)]
            + [jax.ShapeDtypeStruct((3 * lent, TILE), F32)] * len(units),
            in_specs=[vmem()] * 3,
            out_specs=[vmem()] * (1 + len(units)),
        )(flat_points, tile_list, tile_count)
        corner = shifted_back(corner, "ctrl")
        gots = [swapped(sent, bit, 0) for sent, bit in zip(sents, units)]
        bases = [0] * len(units)
    lines = own + lent

    def wide(value):
        return jnp.pad(value, (0, TILE - value.shape[0])).reshape(1, TILE)

    half = tiles // 2
    length = lent * slots + 2 * UNROLL
    scratch = [
        pltpu.VMEM(((lines + 1) * FEATS, depth), BF16),
        pltpu.VMEM((half * TILE, FEATS), BF16),
        pltpu.VMEM((half * MIX, TILE), BF16),
    ]
    squares = [pltpu.VMEM((TILE, depth), F32)] * UNROLL
    partial, part_loads, *lent_lists = pl.pallas_call(
        functools.partial(
            early_kernel, own, rows, slots, lent, bits, placed, units, tuple(bases)
        ),
        out_shape=(
            jax.ShapeDtypeStruct(((lines + 1) * ROWS, depth), F32),
            jax.ShapeDtypeStruct((1, TILE), F32),
            jax.ShapeDtypeStruct((2 * length + 3,), jnp.int32),
            jax.ShapeDtypeStruct((lent * FEATS, depth), BF16),
        ),
        in_specs=[smem()] + [vmem()] * (3 + len(units)),
        out_specs=(vmem(), vmem(), smem(), vmem()),
        scratch_shapes=scratch
        + [
            pltpu.VMEM((lent, TILE), jnp.int32),
            pltpu.SMEM((lent, TILE), jnp.int32),
            pltpu.VMEM((3 * lent, TILE), F32),
            pltpu.SemaphoreType.DMA,
        ]
        + squares,
        compiler_params=limited(16),
        cost_estimate=pl.CostEstimate(flops=0, bytes_accessed=30_000_000, transcendentals=0),
    )(*own_lists, *gots, corner, early)
    groups = [own_lists, lent_lists]
    parts = len(groups)
    lists = [group[0] for group in groups]
    feats = [group[1] for group in groups]
    list_specs = [smem()] * parts + [vmem()] * parts
    outs = pl.pallas_call(
        functools.partial(late_kernel, own, lent, parts, bits),
        out_shape=(
            jax.ShapeDtypeStruct((3 * own, depth), F32),
            jax.ShapeDtypeStruct((3 * max(lent, 8), depth), F32),
            jax.ShapeDtypeStruct((1, TILE), F32),
            jax.ShapeDtypeStruct((2, 3 * planes, depth), F32),
            jax.ShapeDtypeStruct((2, 3 * rows + 8, depth), F32),
        ),
        in_specs=list_specs + [vmem()] * 7,
        out_specs=(vmem(),) * 5,
        scratch_shapes=scratch + [pltpu.VMEM(((lines + 1) * ROWS, depth), F32)] + squares,
        compiler_params=limited(16),
    )(
        *lists, *feats, late, partial, part_loads, flat_points, corner,
        wide(motion), wide(inverse_mass),
    )
    shift, lent_shift, state, row_sent, plane_sent = outs

    backs = [
        lax.ppermute(lent_shift, "slab", [(h ^ bit, h) for h in heavy]).reshape(
            3, share, rows, depth
        )
        for bit in units
    ]
    plane_halo = shifted_back(plane_sent, "slab")
    row_halo = shifted_back(row_sent, "ctrl").reshape(2, 3, planes, depth)
    node_shift, volume, change = pl.pallas_call(
        functools.partial(volume_kernel, keep, share),
        out_shape=(
            jax.ShapeDtypeStruct(node_points.shape, F32),
            jax.ShapeDtypeStruct(node_points.shape[1:], F32),
            jax.ShapeDtypeStruct(node_points.shape[1:], F32),
        ),
        in_specs=[vmem()] * (4 + len(backs)),
        out_specs=(vmem(),) * 3,
        compiler_params=limited(8),
    )(node_points, shift.reshape(3, planes, rows, depth), *backs, plane_halo, row_halo)
    return node_shift, volume, change, state[0, : motion.shape[0]]


def solution(mesh):
    placed = (
        P(("slab", "ctrl")),
        P(None, ("slab", "ctrl")),
        P(None, ("slab", "ctrl")),
        P(),
        P(),
        P(None, ("slab", "ctrl")),
        P(None, ("slab", "ctrl")),
        P(None, "slab", "ctrl", None),
        P("slab", "ctrl", None),
        P("slab", "ctrl"),
    )
    return jax.shard_map(
        local,
        mesh=mesh,
        in_specs=placed,
        out_specs=(
            P(None, "slab", "ctrl", None),
            P("slab", "ctrl", None),
            P("slab", "ctrl", None),
            P(),
        ),
        check_vma=False,
    )
```
